32 devices in a mesh: pipe: 4 (over y, core), expert: 4 (over z), tensor: 2 (over x).
Axes of the slice: x: 2, y: 2, z: 4, core: 2. Of those that a mesh axis runs over, the one named last changes fastest.
Arguments:
- sent_grad: bfloat16 [4, 512, 3584], P('pipe', 'expert', 'tensor'), may hold values from -4 to 4
- head_grad: bfloat16 [512, 3584], P('expert', 'tensor'), may hold values from -4 to 4
- probs: bfloat16 [4, 512, 8], P('pipe', 'expert'), may hold values from 0.049804688 to 1
- expert_ids: int32 [4, 512, 8], P('pipe', 'expert'), may hold values from 0 to 63, as said below
- hidden_act: bfloat16 [4, 64, 68, 1024], P('pipe', 'expert', None, 'tensor'), may hold values from -0.75 to 0.75
Outputs:
- w_down_grad: bfloat16 [4, 64, 1024, 3584], P('pipe', 'expert', 'tensor')
The draws below stay inside these ranges and needn't reach their ends.
Inputs may be any that keep to these rules, and one draw needn't show every extreme that they name: `expert_ids`: each token names 8 different experts. In each section and each block of 128 tokens one expert is named by exactly 17 pairs, one by 17 - 2 pairs, and every other expert by 17 - 1 pairs.
All inputs are finite; a program needn't handle non-finite values.
Results may differ from the reference program's by a relative error of at most 0.0049.
Values may be sent and summed in bfloat16 or wider, within the bound.
No kernel may reach another device: no remote copies, remote signals or barrier semaphores. Data moves between devices by JAX's collectives and lax.ppermute only.
A program may use at most 192 MiB of HBM per device.

```python
import jax
import jax.numpy as jnp
from jax import lax

D = 3584
HID = 1024
EXPERTS = 64
TOPK = 8
TOK = 128
MOST = 17
SLOTS = 68
TOKENS = 512
SECTIONS = 4
N_EXPERT = 4


def draw_expert_ids(key, part):
    spread = EXPERTS // TOPK
    blocks = SECTIONS * N_EXPERT
    hot_key, order_key, token_key, choice_key = jax.random.split(key, 4)
    hot = jax.random.randint(hot_key, (SECTIONS,), 0, EXPERTS, dtype=jnp.int32)
    hot_block = jnp.repeat(hot, N_EXPERT)
    order_keys = jax.random.split(order_key, blocks)
    token_keys = jax.random.split(token_key, blocks)
    choice_keys = jax.random.split(choice_key, blocks)

    def one_block(okey, tkey, ckey, hot_one):
        order = jax.random.permutation(okey, EXPERTS).astype(jnp.int32)
        position = jnp.argmax(order == hot_one).astype(jnp.int32)
        token_index = jnp.arange(TOK, dtype=jnp.int32)[:, None]
        column = jnp.arange(TOPK, dtype=jnp.int32)[None, :]
        chosen = order[(token_index + spread * column) % EXPERTS]
        extra = (token_index == (position + 1) % spread) & (column == 0)
        chosen = jnp.where(extra, hot_one, chosen)
        noise = jax.random.randint(ckey, (TOK, TOPK), 0, 1024, dtype=jnp.int32) * TOPK + column
        shuffle = jnp.argsort(noise, axis=1)
        chosen = jnp.take_along_axis(chosen, shuffle, axis=1)
        token_order = jax.random.permutation(tkey, TOK)
        return chosen[token_order]
    drawn = jax.vmap(one_block)(order_keys, token_keys, choice_keys, hot_block)
    return drawn.reshape(SECTIONS, N_EXPERT * TOK, TOPK).astype(jnp.int32)


def shard_levels(rng, dims, cuts, smallest, largest):
    gain, own = 1.0, jax.random.fold_in(rng, 6)
    for dim, blocks in cuts:
        steps = jnp.exp(jax.random.uniform(jax.random.fold_in(own, dim), (blocks,), jnp.float32, smallest / len(cuts), largest / len(cuts)))
        gain = gain * jnp.repeat(steps, dims[dim] // blocks).reshape([-1 if axis == dim else 1 for axis in range(len(dims))])
    return gain


def centred(key, shape, deviation, reach, cuts=(), kind=jnp.bfloat16):
    array = deviation * jax.random.normal(key, shape, jnp.float32)
    if cuts:
        array = array * shard_levels(key, shape, cuts, -0.22, 0.18)
    return jnp.clip(array, -reach, reach).astype(kind)


def setup_inputs(seed: int = 0) -> dict:
    key_list = jax.random.split(jax.random.key(seed), 6)
    sent_grad = centred(key_list[0], (SECTIONS, TOKENS, D), 0.5, 4.0, ((0, 4), (1, 4), (2, 2)))
    head_grad = centred(key_list[1], (TOKENS, D), 0.5, 4.0, ((0, 4), (1, 2)))
    probs = jnp.clip(0.049804688 + 0.9501953 * jax.random.uniform(key_list[2], (SECTIONS, TOKENS, TOPK), jnp.float32) ** shard_levels(key_list[2], (SECTIONS, TOKENS, TOPK), ((0, 4), (1, 4)), -0.2, 0.2), 0.049804688, 1.0).astype(jnp.bfloat16)
    expert_ids = draw_expert_ids(jax.random.fold_in(key_list[5], 71), 0)
    hidden_act = centred(key_list[4], (SECTIONS, EXPERTS, SLOTS, HID), SLOTS ** -0.5, 0.75, ((0, 4), (1, 4), (3, 2)))
    return dict(sent_grad=sent_grad, head_grad=head_grad, probs=probs, expert_ids=expert_ids, hidden_act=hidden_act)


def reference(sent_grad, head_grad, probs, expert_ids, hidden_act):
    sections = sent_grad.shape[0]
    tokens = sent_grad.shape[1]
    feature_count = sent_grad.shape[2]
    groups = tokens // TOK
    slot_count = groups * MOST
    grad_list = []
    for section in range(sections):
        if section == sections - 1:
            incoming = head_grad
        else:
            incoming = sent_grad[section + 1]
        pair_ids = expert_ids[section].reshape(groups, TOK * TOPK)
        onehot = (pair_ids[:, :, None] == jnp.arange(EXPERTS, dtype=jnp.int32)[None, None, :]).astype(jnp.int32)
        before = jnp.cumsum(onehot, axis=1) - onehot
        slot_rank = jnp.sum(before * onehot, axis=2).astype(jnp.int32)
        block_index = jnp.arange(groups, dtype=jnp.int32)[:, None]
        target = (pair_ids * slot_count + block_index * MOST + slot_rank).reshape(-1).astype(jnp.int32)
        copies = jnp.repeat(incoming, TOPK, axis=0)
        routed = jnp.zeros((EXPERTS * slot_count, feature_count), incoming.dtype).at[target].set(copies)
        routed = routed.reshape(EXPERTS, slot_count, feature_count)
        gate_slots = jnp.zeros((EXPERTS * slot_count,), probs.dtype).at[target].set(probs[section].reshape(-1))
        gate_slots = gate_slots.reshape(EXPERTS, slot_count)

        def expert_step(pieces):
            rows_e, gate_e, act_e = pieces
            weighted = (rows_e.astype(jnp.float32) * gate_e.astype(jnp.float32)[:, None]).astype(jnp.bfloat16)
            return jnp.dot(act_e.T, weighted, preferred_element_type=jnp.float32).astype(jnp.bfloat16)

        weight_grad = lax.map(expert_step, (routed, gate_slots, hidden_act[section]))
        grad_list.append(weight_grad)
    return jnp.stack(grad_list)
```

```python
import functools

import jax
import jax.numpy as jnp
from jax import lax
from jax.experimental import pallas as pl
from jax.experimental.pallas import tpu as pltpu
from jax.sharding import PartitionSpec as P

EXPERTS = 64
TOPK = 8
TOK = 128
MOST = 17
GROUP = 4
CHUNKS = 2


def passed_along(array, axis, by):
    peers = lax.axis_size(axis)
    pairs = [(i, i + by) for i in range(peers) if 0 <= i + by < peers]
    return lax.ppermute(array, axis, pairs)


def slot_ranks(pair_ids):
    onehot = (pair_ids[:, :, None] == jnp.arange(EXPERTS, dtype=jnp.int32)[None, None, :]).astype(
        jnp.int32
    )
    before = jnp.cumsum(onehot, axis=1) - onehot
    return jnp.sum(before * onehot, axis=2)


def place_rows(targets, capacity, source_rows, gate_values):
    pair_count = targets.shape[0]
    owner_pair = (
        jnp.full((capacity,), pair_count, jnp.int32)
        .at[targets]
        .set(jnp.arange(pair_count, dtype=jnp.int32), mode="drop")
    )
    filled = owner_pair < pair_count
    safe_pair = jnp.minimum(owner_pair, pair_count - 1)
    placed = jnp.where(
        filled[:, None], source_rows[safe_pair // TOPK], jnp.zeros((), source_rows.dtype)
    )
    placed_gate = jnp.where(
        filled, gate_values.reshape(-1)[safe_pair], jnp.zeros((), gate_values.dtype)
    )
    return (placed, placed_gate)


def arriving(sent_grad, head_grad):
    shifted = passed_along(sent_grad, "pipe", -1)
    is_last = lax.axis_index("pipe") == lax.axis_size("pipe") - 1
    return jnp.where(is_last, head_grad, shifted[0])


def local_by_slots(sent_grad, head_grad, probs, expert_ids, hidden_act):
    incoming = arriving(sent_grad, head_grad)
    feat_dev = incoming.shape[1]
    local_ids = expert_ids[0].reshape(1, TOK * TOPK)
    local_targets = (local_ids * MOST + slot_ranks(local_ids)).reshape(-1)
    send_rows, send_gate = place_rows(local_targets, EXPERTS * MOST, incoming, probs[0])
    recv_rows, recv_gate = (
        lax.all_to_all(
            send_rows.reshape(EXPERTS, MOST, feat_dev),
            "expert",
            split_axis=0,
            concat_axis=1,
            tiled=True,
        ),
        lax.all_to_all(
            send_gate.reshape(EXPERTS, MOST), "expert", split_axis=0, concat_axis=1, tiled=True
        ),
    )
    gate_wide = recv_gate.astype(jnp.float32)[:, :, None]
    full_rows = lax.all_gather(recv_rows, "tensor", axis=2, tiled=True)
    weighted = (full_rows.astype(jnp.float32) * gate_wide).astype(jnp.bfloat16)
    weight_grad = jnp.einsum(
        "esh,esd->ehd", hidden_act[0], weighted, preferred_element_type=jnp.float32
    ).astype(jnp.bfloat16)
    return weight_grad[None]


def place_kernel(blocks, owned, padded, where_ref, meta_ref, place_ref):
    first = where_ref[0] * owned
    experts = (first + lax.broadcasted_iota(jnp.int32, (owned, TOK), 0)).astype(jnp.float32)
    earlier = (
        lax.broadcasted_iota(jnp.int32, (TOK, TOK), 0)
        < lax.broadcasted_iota(jnp.int32, (TOK, TOK), 1)
    ).astype(jnp.float32)
    slots = lax.broadcasted_iota(jnp.int32, (padded, TOK), 0).astype(jnp.float32)
    for b in range(blocks):
        meta = meta_ref[b].astype(jnp.float32)
        named = jnp.zeros((owned, TOK), jnp.float32)
        gate = jnp.zeros((owned, TOK), jnp.float32)
        for k in range(TOPK):
            hit = experts == meta[k : k + 1, :]
            named = jnp.where(hit, 1.0, named)
            gate = jnp.where(hit, meta[TOPK + k : TOPK + k + 1, :], gate)
        rank = jnp.dot(named, earlier, preferred_element_type=jnp.float32)
        slot = jnp.where(named > 0.0, rank + float(b * MOST), -1.0)
        for e in range(owned):
            place_ref[e * padded : (e + 1) * padded, b * TOK : (b + 1) * TOK] = jnp.where(
                slots == slot[e : e + 1, :], gate[e : e + 1, :], 0.0
            ).astype(jnp.bfloat16)


def grad_kernel(padded, features, where_ref, place_ref, act_ref, rows_ref, *rest):
    out_ref, weighted_ref = rest[-2:]
    turn = lax.rem(pl.program_id(1), GROUP)

    @pl.when(turn == 0)
    def _():
        for n in range(0, features, 256):
            wide = slice(n, min(n + 256, features))
            weighted_ref[:, wide] = jnp.dot(
                place_ref[...], rows_ref[0, :, wide], preferred_element_type=jnp.float32
            ).astype(jnp.bfloat16)

    start = pl.multiple_of(turn * padded, padded)
    act = act_ref[0, :, :padded]
    for n in range(0, features, 256):
        wide = slice(n, min(n + 256, features))
        out_ref[0, :, wide] = jnp.dot(
            act, weighted_ref[pl.ds(start, padded), wide], preferred_element_type=jnp.float32
        ).astype(jnp.bfloat16)


def local_by_tokens(sent_grad, head_grad, probs, expert_ids, hidden_act):
    n_expert = lax.axis_size("expert")
    n_tensor = lax.axis_size("tensor")
    owned, slot_count, hid = hidden_act.shape[1:]
    feat_dev = sent_grad.shape[2]
    tokens = n_expert * TOK
    padded = -(-slot_count // 16) * 16
    span = feat_dev // CHUNKS

    meta = jnp.concatenate([expert_ids[0].astype(jnp.bfloat16), probs[0]], axis=1).T
    meta = lax.all_gather(meta, "expert")
    here = jnp.stack([lax.axis_index("expert"), lax.axis_index("tensor")]).astype(jnp.int32)
    smem = pl.BlockSpec(memory_space=pltpu.SMEM)
    place = pl.pallas_call(
        functools.partial(place_kernel, n_expert, owned, padded),
        out_shape=jax.ShapeDtypeStruct((owned * padded, tokens), jnp.bfloat16),
        in_specs=[smem, pl.BlockSpec(memory_space=pltpu.VMEM)],
        out_specs=pl.BlockSpec(memory_space=pltpu.VMEM),
        name="place",
    )(here, meta)
    act = jnp.pad(
        jnp.swapaxes(hidden_act[0], 1, 2), ((0, 0), (0, 0), (0, -slot_count % 128))
    )

    def grad_into(out, rows, parts, chunk, part_of):
        def column(p, where):
            return lax.rem(where[1] + part_of(p), n_tensor) * CHUNKS + chunk

        out_type = jax.ShapeDtypeStruct((owned, hid, n_tensor * feat_dev), jnp.bfloat16)
        wide = rows.shape[0] > 1
        in_specs = [
            pl.BlockSpec((GROUP * padded, tokens), lambda p, e, where: (e // GROUP, 0)),
            pl.BlockSpec((1, hid, act.shape[2]), lambda p, e, where: (e, 0, 0)),
            pl.BlockSpec(
                (1, tokens, span),
                lambda p, e, where: (
                    lax.rem(where[1] + part_of(p), n_tensor) if wide else 0,
                    0,
                    0,
                ),
            ),
        ]
        operands = [here, place, act, rows]
        aliases = {}
        if out is not None:
            in_specs.append(pl.BlockSpec(memory_space=pl.ANY))
            operands.append(out)
            aliases = {4: 0}
        return pl.pallas_call(
            functools.partial(grad_kernel, padded, span),
            out_shape=out_type,
            grid_spec=pltpu.PrefetchScalarGridSpec(
                num_scalar_prefetch=1,
                grid=(parts, owned),
                in_specs=in_specs,
                out_specs=pl.BlockSpec(
                    (1, hid, span), lambda p, e, where: (e, 0, column(p, where))
                ),
                scratch_shapes=[pltpu.VMEM((GROUP * padded, span), jnp.bfloat16)],
            ),
            input_output_aliases=aliases,
            compiler_params=pltpu.CompilerParams(vmem_limit_bytes=48 * 2**20),
            cost_estimate=pl.CostEstimate(
                flops=2 * parts * owned * hid * 256 * span,
                bytes_accessed=2 * parts * owned * hid * span,
                transcendentals=0,
            ),
            name="weight_grad",
        )(*operands)

    incoming = arriving(sent_grad, head_grad)
    own = [
        lax.all_gather(incoming[:, c * span : (c + 1) * span], "expert").reshape(1, tokens, span)
        for c in range(CHUNKS)
    ]
    others = [lax.all_gather(rows[0], "tensor") for rows in own]
    out = None
    for c in range(CHUNKS):
        out = grad_into(out, own[c], 1, c, lambda p: 0)
    for c in range(CHUNKS):
        out = grad_into(out, others[c], n_tensor - 1, c, lambda p: 1 + p)
    return out[None]


def local(*arrays):
    owned, slot_count = arrays[4].shape[1:3]
    tokens = lax.axis_size("expert") * TOK
    by_tokens = tokens <= owned * slot_count
    return (local_by_tokens if by_tokens else local_by_slots)(*arrays)


def solution(mesh):
    in_specs = (
        P("pipe", "expert", "tensor"),
        P("expert", "tensor"),
        P("pipe", "expert", None),
        P("pipe", "expert", None),
        P("pipe", "expert", None, "tensor"),
    )
    out_specs = P("pipe", "expert", "tensor", None)
    return jax.shard_map(local, mesh=mesh, in_specs=in_specs, out_specs=out_specs, check_vma=False)
```

```python
import functools

import jax
import jax.numpy as jnp
from jax import lax
from jax.experimental import pallas as pl
from jax.experimental.pallas import tpu as pltpu
from jax.sharding import PartitionSpec as P

EXPERTS = 64
TOPK = 8
TOK = 128
MOST = 17
GROUP = 4
DEEP = 128
BUFFERS = 4


def passed_along(array, axis, by):
    peers = lax.axis_size(axis)
    pairs = [(i, i + by) for i in range(peers) if 0 <= i + by < peers]
    return lax.ppermute(array, axis, pairs)


def slot_ranks(pair_ids):
    onehot = (pair_ids[:, :, None] == jnp.arange(EXPERTS, dtype=jnp.int32)[None, None, :]).astype(
        jnp.int32
    )
    before = jnp.cumsum(onehot, axis=1) - onehot
    return jnp.sum(before * onehot, axis=2)


def place_rows(targets, capacity, source_rows, gate_values):
    pair_count = targets.shape[0]
    owner_pair = (
        jnp.full((capacity,), pair_count, jnp.int32)
        .at[targets]
        .set(jnp.arange(pair_count, dtype=jnp.int32), mode="drop")
    )
    filled = owner_pair < pair_count
    safe_pair = jnp.minimum(owner_pair, pair_count - 1)
    placed = jnp.where(
        filled[:, None], source_rows[safe_pair // TOPK], jnp.zeros((), source_rows.dtype)
    )
    placed_gate = jnp.where(
        filled, gate_values.reshape(-1)[safe_pair], jnp.zeros((), gate_values.dtype)
    )
    return (placed, placed_gate)


def arriving(sent_grad, head_grad):
    shifted = passed_along(sent_grad, "pipe", -1)
    is_last = lax.axis_index("pipe") == lax.axis_size("pipe") - 1
    return jnp.where(is_last, head_grad, shifted[0])


def local_by_slots(sent_grad, head_grad, probs, expert_ids, hidden_act):
    incoming = arriving(sent_grad, head_grad)
    feat_dev = incoming.shape[1]
    local_ids = expert_ids[0].reshape(1, TOK * TOPK)
    local_targets = (local_ids * MOST + slot_ranks(local_ids)).reshape(-1)
    send_rows, send_gate = place_rows(local_targets, EXPERTS * MOST, incoming, probs[0])
    recv_rows, recv_gate = (
        lax.all_to_all(
            send_rows.reshape(EXPERTS, MOST, feat_dev),
            "expert",
            split_axis=0,
            concat_axis=1,
            tiled=True,
        ),
        lax.all_to_all(
            send_gate.reshape(EXPERTS, MOST), "expert", split_axis=0, concat_axis=1, tiled=True
        ),
    )
    gate_wide = recv_gate.astype(jnp.float32)[:, :, None]
    full_rows = lax.all_gather(recv_rows, "tensor", axis=2, tiled=True)
    weighted = (full_rows.astype(jnp.float32) * gate_wide).astype(jnp.bfloat16)
    weight_grad = jnp.einsum(
        "esh,esd->ehd", hidden_act[0], weighted, preferred_element_type=jnp.float32
    ).astype(jnp.bfloat16)
    return weight_grad[None]


def place_kernel(n_expert, owned, padded, here_ref, *refs):
    *metas, place_ref = refs
    me = here_ref[0]
    experts = (me * owned + lax.broadcasted_iota(jnp.int32, (owned, TOK), 0)).astype(jnp.float32)
    earlier = (
        lax.broadcasted_iota(jnp.int32, (TOK, TOK), 0)
        < lax.broadcasted_iota(jnp.int32, (TOK, TOK), 1)
    ).astype(jnp.float32)
    slots = lax.broadcasted_iota(jnp.int32, (padded, TOK), 0).astype(jnp.float32)
    for k in range(n_expert):
        first = (lax.rem(me + n_expert - k, n_expert) * MOST).astype(jnp.float32)
        meta = metas[k][...].astype(jnp.float32)
        named = jnp.zeros((owned, TOK), jnp.float32)
        gate = jnp.zeros((owned, TOK), jnp.float32)
        for c in range(TOPK):
            hit = experts == meta[c : c + 1, :]
            named = jnp.where(hit, 1.0, named)
            gate = jnp.where(hit, meta[TOPK + c : TOPK + c + 1, :], gate)
        rank = jnp.dot(named, earlier, preferred_element_type=jnp.float32)
        slot = jnp.where(named > 0.0, rank + first, -1.0)
        for e in range(owned):
            place_ref[e * padded : (e + 1) * padded, k * TOK : (k + 1) * TOK] = jnp.where(
                slots == slot[e : e + 1, :], gate[e : e + 1, :], 0.0
            ).astype(jnp.bfloat16)


def grad_kernel(n_expert, padded, other, here_ref, place_ref, act_ref, *refs):
    blocks = refs[: 2 * n_expert - 1]
    out_ref, rows_ref, weighted_ref, done_ref, rows_sem, out_sem = refs[-6:]
    owned, hid = act_ref.shape[:2]
    features = rows_ref.shape[1]
    me, side, sides = here_ref[0], here_ref[1], here_ref[2]
    column = pl.multiple_of(lax.rem(side + other, sides) * features, 128)

    def fetch(block, k):
        return pltpu.make_async_copy(
            block, rows_ref.at[k * TOK : (k + 1) * TOK], rows_sem.at[k]
        )

    fetch(blocks[0], 0).start()
    for k in range(1, n_expert):

        @pl.when(me >= k)
        def _():
            fetch(blocks[k], k).start()

        @pl.when(me < k)
        def _():
            fetch(blocks[2 * n_expert - 1 - k], k).start()

    for j in range(GROUP):
        weighted_ref[j, padded:, :] = jnp.zeros((DEEP - padded, features), jnp.bfloat16)
    for k in range(n_expert):
        fetch(blocks[0], k).wait()

    def leave(e):
        slot = lax.rem(e, BUFFERS)
        return pltpu.make_async_copy(
            done_ref.at[slot], out_ref.at[e, :, pl.ds(column, features)], out_sem.at[slot]
        )

    @pl.loop(0, owned // GROUP)
    def _(g):
        start = pl.multiple_of(g * GROUP * padded, GROUP * padded)
        for n in range(0, features, 256):
            wide = slice(n, min(n + 256, features))
            weighted = jnp.dot(
                place_ref[pl.ds(start, GROUP * padded), :],
                rows_ref[:, wide],
                preferred_element_type=jnp.float32,
            ).astype(jnp.bfloat16)
            for j in range(GROUP):
                weighted_ref[j, :padded, wide] = weighted[j * padded : (j + 1) * padded]

        @pl.loop(0, GROUP)
        def _(j):
            e = g * GROUP + j

            @pl.when(e >= BUFFERS)
            def _():
                leave(e - BUFFERS).wait()

            slot = lax.rem(e, BUFFERS)
            for n in range(0, features, 256):
                wide = slice(n, min(n + 256, features))
                done_ref[slot, :, wide] = jnp.dot(
                    act_ref[e], weighted_ref[j, :, wide], preferred_element_type=jnp.float32
                ).astype(jnp.bfloat16)
            leave(e).start()

    @pl.loop(owned - BUFFERS, owned)
    def _(e):
        leave(e).wait()


def local_by_tokens(sent_grad, head_grad, probs, expert_ids, hidden_act):
    n_expert = lax.axis_size("expert")
    n_tensor = lax.axis_size("tensor")
    owned, slot_count, hid = hidden_act.shape[1:]
    feat_dev = sent_grad.shape[2]
    tokens = n_expert * TOK
    padded = -(-slot_count // 16) * 16
    smem = pl.BlockSpec(memory_space=pltpu.SMEM)
    vmem = pl.BlockSpec(memory_space=pltpu.VMEM)
    anywhere = pl.BlockSpec(memory_space=pl.ANY)

    def turned(array, axis, by):
        peers = lax.axis_size(axis)
        return lax.ppermute(array, axis, [(i, (i + by) % peers) for i in range(peers)])

    def hop(array, by, age):
        pairs = [
            (i, i + by)
            for i in range(n_expert)
            if 0 <= i + by < n_expert and 0 <= i - by * age < n_expert
        ]
        return lax.ppermute(array, "expert", pairs)

    def across(array, by, away):
        pairs = []
        for i in range(n_expert):
            if 0 <= i - by < n_expert:
                for t in range(n_tensor):
                    pairs.append((i * n_tensor + t, i * n_tensor + (t + away) % n_tensor))
        return lax.ppermute(array, ("expert", "tensor"), pairs)

    meta = jnp.concatenate([expert_ids[0].astype(jnp.bfloat16), probs[0]], axis=1).T
    metas = [meta] + [turned(meta, "expert", k) for k in range(1, n_expert)]
    here = jnp.stack(
        [lax.axis_index("expert"), lax.axis_index("tensor"), jnp.int32(n_tensor)]
    ).astype(jnp.int32)
    place = pl.pallas_call(
        functools.partial(place_kernel, n_expert, owned, padded),
        out_shape=jax.ShapeDtypeStruct((owned * padded, tokens), jnp.bfloat16),
        in_specs=[smem] + [vmem] * n_expert,
        out_specs=vmem,
        name="place",
    )(here, *metas)
    act = jnp.pad(
        jnp.swapaxes(hidden_act[0], 1, 2), ((0, 0), (0, 0), (0, DEEP - slot_count))
    )

    def grad_into(out, blocks, other):
        operands = [here, place, act, *blocks]
        in_specs = [smem, vmem, vmem] + [anywhere] * len(blocks)
        aliases = {}
        if out is not None:
            aliases = {len(operands): 0}
            in_specs.append(anywhere)
            operands.append(out)
        return pl.pallas_call(
            functools.partial(grad_kernel, n_expert, padded, other),
            out_shape=jax.ShapeDtypeStruct((owned, hid, n_tensor * feat_dev), jnp.bfloat16),
            in_specs=in_specs,
            out_specs=anywhere,
            scratch_shapes=[
                pltpu.VMEM((tokens, feat_dev), jnp.bfloat16),
                pltpu.VMEM((GROUP, DEEP, feat_dev), jnp.bfloat16),
                pltpu.VMEM((BUFFERS, hid, feat_dev), jnp.bfloat16),
                pltpu.SemaphoreType.DMA((n_expert,)),
                pltpu.SemaphoreType.DMA((BUFFERS,)),
            ],
            input_output_aliases=aliases,
            compiler_params=pltpu.CompilerParams(vmem_limit_bytes=40 * 2**20),
            cost_estimate=pl.CostEstimate(
                flops=2 * owned * hid * 256 * feat_dev,
                bytes_accessed=2 * owned * hid * feat_dev,
                transcendentals=0,
            ),
            name="weight_grad",
        )(*operands)

    incoming = arriving(sent_grad, head_grad)
    ups, downs = [incoming], [incoming]
    beside = {t: [across(incoming, 0, t)] for t in range(1, n_tensor)}
    beside_up = {t: [] for t in beside}
    beside_down = {t: [] for t in beside}
    for age in range(n_expert - 1):
        ups.append(hop(ups[-1], 1, age))
        downs.append(hop(downs[-1], -1, age))
        for t in beside:
            beside_up[t].append(across(ups[-1], age + 1, t))
            beside_down[t].append(across(downs[-1], -age - 1, t))
    out = grad_into(None, [incoming] + ups[1:] + downs[1:], 0)
    for t in beside:
        out = grad_into(out, beside[t] + beside_up[t] + beside_down[t], n_tensor - t)
    return out[None]


def local(*arrays):
    owned, slot_count = arrays[4].shape[1:3]
    tokens = lax.axis_size("expert") * TOK
    by_tokens = tokens <= owned * slot_count
    return (local_by_tokens if by_tokens else local_by_slots)(*arrays)


def solution(mesh):
    in_specs = (
        P("pipe", "expert", "tensor"),
        P("expert", "tensor"),
        P("pipe", "expert", None),
        P("pipe", "expert", None),
        P("pipe", "expert", None, "tensor"),
    )
    out_specs = P("pipe", "expert", "tensor", None)
    return jax.shard_map(local, mesh=mesh, in_specs=in_specs, out_specs=out_specs, check_vma=False)
```

```python
import functools

import jax
import jax.numpy as jnp
from jax import lax
from jax.experimental import pallas as pl
from jax.experimental.pallas import tpu as pltpu
from jax.sharding import PartitionSpec as P

EXPERTS = 64
TOPK = 8
TOK = 128
MOST = 17
ROOM = 32
GROUPS = 2
BUFFERS = 4


def passed_along(array, axis, by):
    peers = lax.axis_size(axis)
    pairs = [(i, i + by) for i in range(peers) if 0 <= i + by < peers]
    return lax.ppermute(array, axis, pairs)


def slot_ranks(pair_ids):
    onehot = (pair_ids[:, :, None] == jnp.arange(EXPERTS, dtype=jnp.int32)[None, None, :]).astype(
        jnp.int32
    )
    before = jnp.cumsum(onehot, axis=1) - onehot
    return jnp.sum(before * onehot, axis=2)


def place_rows(targets, capacity, source_rows, gate_values):
    pair_count = targets.shape[0]
    owner_pair = (
        jnp.full((capacity,), pair_count, jnp.int32)
        .at[targets]
        .set(jnp.arange(pair_count, dtype=jnp.int32), mode="drop")
    )
    filled = owner_pair < pair_count
    safe_pair = jnp.minimum(owner_pair, pair_count - 1)
    placed = jnp.where(
        filled[:, None], source_rows[safe_pair // TOPK], jnp.zeros((), source_rows.dtype)
    )
    placed_gate = jnp.where(
        filled, gate_values.reshape(-1)[safe_pair], jnp.zeros((), gate_values.dtype)
    )
    return (placed, placed_gate)


def arriving(sent_grad, head_grad):
    shifted = passed_along(sent_grad, "pipe", -1)
    is_last = lax.axis_index("pipe") == lax.axis_size("pipe") - 1
    return jnp.where(is_last, head_grad, shifted[0])


def local_by_slots(sent_grad, head_grad, probs, expert_ids, hidden_act):
    incoming = arriving(sent_grad, head_grad)
    feat_dev = incoming.shape[1]
    local_ids = expert_ids[0].reshape(1, TOK * TOPK)
    local_targets = (local_ids * MOST + slot_ranks(local_ids)).reshape(-1)
    send_rows, send_gate = place_rows(local_targets, EXPERTS * MOST, incoming, probs[0])
    recv_rows, recv_gate = (
        lax.all_to_all(
            send_rows.reshape(EXPERTS, MOST, feat_dev),
            "expert",
            split_axis=0,
            concat_axis=1,
            tiled=True,
        ),
        lax.all_to_all(
            send_gate.reshape(EXPERTS, MOST), "expert", split_axis=0, concat_axis=1, tiled=True
        ),
    )
    gate_wide = recv_gate.astype(jnp.float32)[:, :, None]
    full_rows = lax.all_gather(recv_rows, "tensor", axis=2, tiled=True)
    weighted = (full_rows.astype(jnp.float32) * gate_wide).astype(jnp.bfloat16)
    weight_grad = jnp.einsum(
        "esh,esd->ehd", hidden_act[0], weighted, preferred_element_type=jnp.float32
    ).astype(jnp.bfloat16)
    return weight_grad[None]


def place_kernel(n_expert, owned, here_ref, *refs):
    *metas, place_ref = refs
    first = here_ref[0] * owned
    experts = (first + lax.broadcasted_iota(jnp.int32, (owned, TOK), 0)).astype(jnp.float32)
    earlier = (
        lax.broadcasted_iota(jnp.int32, (TOK, TOK), 0)
        < lax.broadcasted_iota(jnp.int32, (TOK, TOK), 1)
    ).astype(jnp.float32)
    ranks = lax.broadcasted_iota(jnp.int32, (ROOM, TOK), 0).astype(jnp.float32)
    for k in range(n_expert):
        meta = metas[k][...].astype(jnp.float32)
        named = jnp.zeros((owned, TOK), jnp.float32)
        gate = jnp.zeros((owned, TOK), jnp.float32)
        for c in range(TOPK):
            hit = experts == meta[c : c + 1, :]
            named = jnp.where(hit, 1.0, named)
            gate = jnp.where(hit, meta[TOPK + c : TOPK + c + 1, :], gate)
        rank = jnp.dot(named, earlier, preferred_element_type=jnp.float32)
        rank = jnp.where(named > 0.0, rank, -1.0)
        for e in range(owned):
            place_ref[k, e * ROOM : (e + 1) * ROOM, :] = jnp.where(
                ranks == rank[e : e + 1, :], gate[e : e + 1, :], 0.0
            ).astype(jnp.bfloat16)


def grad_kernel(n_expert, other, pair, here_ref, place_ref, act_ref, *refs):
    blocks = refs[:n_expert]
    out_ref, rows_ref, weighted_ref, done_ref, rows_sem, out_sem = refs[-6:]
    owned, hid, deep = act_ref.shape
    features = rows_ref.shape[2]
    me, side, sides = here_ref[0], here_ref[1], here_ref[2]
    column = pl.multiple_of(lax.rem(side + other, sides) * features, 128)
    share = owned // GROUPS

    def fetch(k):
        return pltpu.make_async_copy(blocks[k], rows_ref.at[k], rows_sem.at[k])

    def leave(e):
        slot = lax.rem(e, BUFFERS)
        return pltpu.make_async_copy(
            done_ref.at[slot], out_ref.at[e, :, pl.ds(column, features)], out_sem.at[slot]
        )

    def tiles():
        for n in range(0, features, 256):
            yield slice(n, min(n + 256, features))

    for k in range(n_expert):
        fetch(k).start()
    for k in range(n_expert):
        fetch(k).wait()

    @pl.loop(0, GROUPS)
    def _(g):
        start = pl.multiple_of(g * share * ROOM, share * ROOM)
        for k in range(n_expert):
            block = lax.rem(me + n_expert - k, n_expert)
            spot = pl.ds(pl.multiple_of(block * ROOM, ROOM), ROOM)
            for wide in tiles():
                weighted = jnp.dot(
                    place_ref[k, pl.ds(start, share * ROOM), :],
                    rows_ref[k, :, wide],
                    preferred_element_type=jnp.float32,
                ).astype(jnp.bfloat16)
                for j in range(share):
                    weighted_ref[j, spot, wide] = weighted[j * ROOM : (j + 1) * ROOM]

        @pl.loop(0, share // pair)
        def _(p):
            e = g * share + p * pair
            for i in range(pair):

                @pl.when(e + i >= BUFFERS)
                def _():
                    leave(e + i - BUFFERS).wait()

            acts = [act_ref[e + i] for i in range(pair)]
            zero = jnp.zeros((hid, deep), jnp.bfloat16)
            left = jnp.concatenate(
                [
                    jnp.concatenate([acts[i] if i == j else zero for j in range(pair)], axis=1)
                    for i in range(pair)
                ],
                axis=0,
            )
            for wide in tiles():
                right = jnp.concatenate(
                    [weighted_ref[p * pair + i, :, wide] for i in range(pair)], axis=0
                )
                grad = jnp.dot(left, right, preferred_element_type=jnp.float32)
                grad = grad.astype(jnp.bfloat16)
                for i in range(pair):
                    done_ref[lax.rem(e + i, BUFFERS), :, wide] = grad[i * hid : (i + 1) * hid]
            for i in range(pair):
                leave(e + i).start()

    @pl.loop(owned - BUFFERS, owned)
    def _(e):
        leave(e).wait()


def local_by_tokens(sent_grad, head_grad, probs, expert_ids, hidden_act):
    n_expert = lax.axis_size("expert")
    n_tensor = lax.axis_size("tensor")
    owned, _, hid = hidden_act.shape[1:]
    feat_dev = sent_grad.shape[2]
    smem = pl.BlockSpec(memory_space=pltpu.SMEM)
    vmem = pl.BlockSpec(memory_space=pltpu.VMEM)
    anywhere = pl.BlockSpec(memory_space=pl.ANY)

    def turned(array, axis, by):
        peers = lax.axis_size(axis)
        return lax.ppermute(array, axis, [(i, (i + by) % peers) for i in range(peers)])

    meta = jnp.concatenate([expert_ids[0].astype(jnp.bfloat16), probs[0]], axis=1).T
    metas = [meta] + [turned(meta, "expert", k) for k in range(1, n_expert)]
    here = jnp.stack(
        [lax.axis_index("expert"), lax.axis_index("tensor"), jnp.int32(n_tensor)]
    ).astype(jnp.int32)
    act = hidden_act[0].reshape(owned, n_expert, MOST, hid)
    act = jnp.pad(act, ((0, 0), (0, 0), (0, ROOM - MOST), (0, 0)))
    act = jnp.swapaxes(act.reshape(owned, n_expert * ROOM, hid), 1, 2)

    def grad_into(out, blocks, other, pair):
        operands = [here, place, act, *blocks]
        in_specs = [smem, vmem, vmem] + [anywhere] * len(blocks)
        aliases = {}
        if out is not None:
            aliases = {len(operands): 0}
            in_specs.append(anywhere)
            operands.append(out)
        return pl.pallas_call(
            functools.partial(grad_kernel, n_expert, other, pair),
            out_shape=jax.ShapeDtypeStruct((owned, hid, n_tensor * feat_dev), jnp.bfloat16),
            in_specs=in_specs,
            out_specs=anywhere,
            scratch_shapes=[
                pltpu.VMEM((n_expert, TOK, feat_dev), jnp.bfloat16),
                pltpu.VMEM((owned // GROUPS, n_expert * ROOM, feat_dev), jnp.bfloat16),
                pltpu.VMEM((BUFFERS, hid, feat_dev), jnp.bfloat16),
                pltpu.SemaphoreType.DMA((n_expert,)),
                pltpu.SemaphoreType.DMA((BUFFERS,)),
            ],
            input_output_aliases=aliases,
            compiler_params=pltpu.CompilerParams(vmem_limit_bytes=40 * 2**20),
            cost_estimate=pl.CostEstimate(
                flops=2 * owned * hid * 256 * feat_dev,
                bytes_accessed=2 * owned * hid * feat_dev,
                transcendentals=0,
            ),
            name="weight_grad",
        )(*operands)

    shifted = passed_along(sent_grad, "pipe", -1)
    shifted, *metas = lax.optimization_barrier((shifted, *metas))
    is_last = lax.axis_index("pipe") == lax.axis_size("pipe") - 1
    rows = [jnp.where(is_last, head_grad, shifted[0])]
    place = pl.pallas_call(
        functools.partial(place_kernel, n_expert, owned),
        out_shape=jax.ShapeDtypeStruct((n_expert, owned * ROOM, TOK), jnp.bfloat16),
        in_specs=[smem] + [vmem] * n_expert,
        out_specs=vmem,
        name="place",
    )(here, *metas)
    beside = {t: [turned(rows[0], "tensor", t)] for t in range(1, n_tensor)}
    for k in range(1, n_expert):
        rows.append(turned(rows[-1], "expert", 1))
        if k == 1:
            rows[1], place, act = lax.optimization_barrier((rows[1], place, act))
        else:
            earlier = {t: beside[t][k - 2] for t in beside}
            rows[k], earlier = lax.optimization_barrier((rows[k], earlier))
            for t in beside:
                beside[t][k - 2] = earlier[t]
        for t in beside:
            beside[t].append(turned(rows[k], "tensor", t))
    out = grad_into(None, rows, 0, 1)
    for t in beside:
        out = grad_into(out, beside[t], n_tensor - t, 2)
    return out[None]


def local(*arrays):
    owned, slot_count = arrays[4].shape[1:3]
    tokens = lax.axis_size("expert") * TOK
    by_tokens = tokens <= owned * slot_count
    return (local_by_tokens if by_tokens else local_by_slots)(*arrays)


def solution(mesh):
    in_specs = (
        P("pipe", "expert", "tensor"),
        P("expert", "tensor"),
        P("pipe", "expert", None),
        P("pipe", "expert", None),
        P("pipe", "expert", None, "tensor"),
    )
    out_specs = P("pipe", "expert", "tensor", None)
    return jax.shard_map(local, mesh=mesh, in_specs=in_specs, out_specs=out_specs, check_vma=False)
```

```python
import functools

import jax
import jax.numpy as jnp
from jax import lax
from jax.experimental import pallas as pl
from jax.experimental.pallas import tpu as pltpu
from jax.sharding import PartitionSpec as P

EXPERTS = 64
TOPK = 8
TOK = 128
MOST = 17
ROOM = 32
GROUPS = 2
TURN = 4
CHUNKS = (1024, 768)


def passed_along(array, axis, by):
    peers = lax.axis_size(axis)
    pairs = [(i, i + by) for i in range(peers) if 0 <= i + by < peers]
    return lax.ppermute(array, axis, pairs)


def slot_ranks(pair_ids):
    onehot = (pair_ids[:, :, None] == jnp.arange(EXPERTS, dtype=jnp.int32)[None, None, :]).astype(
        jnp.int32
    )
    before = jnp.cumsum(onehot, axis=1) - onehot
    return jnp.sum(before * onehot, axis=2)


def place_rows(targets, capacity, source_rows, gate_values):
    pair_count = targets.shape[0]
    owner_pair = (
        jnp.full((capacity,), pair_count, jnp.int32)
        .at[targets]
        .set(jnp.arange(pair_count, dtype=jnp.int32), mode="drop")
    )
    filled = owner_pair < pair_count
    safe_pair = jnp.minimum(owner_pair, pair_count - 1)
    placed = jnp.where(
        filled[:, None], source_rows[safe_pair // TOPK], jnp.zeros((), source_rows.dtype)
    )
    placed_gate = jnp.where(
        filled, gate_values.reshape(-1)[safe_pair], jnp.zeros((), gate_values.dtype)
    )
    return (placed, placed_gate)


def arriving(sent_grad, head_grad):
    shifted = passed_along(sent_grad, "pipe", -1)
    is_last = lax.axis_index("pipe") == lax.axis_size("pipe") - 1
    return jnp.where(is_last, head_grad, shifted[0])


def local_by_slots(sent_grad, head_grad, probs, expert_ids, hidden_act):
    incoming = arriving(sent_grad, head_grad)
    feat_dev = incoming.shape[1]
    local_ids = expert_ids[0].reshape(1, TOK * TOPK)
    local_targets = (local_ids * MOST + slot_ranks(local_ids)).reshape(-1)
    send_rows, send_gate = place_rows(local_targets, EXPERTS * MOST, incoming, probs[0])
    recv_rows, recv_gate = (
        lax.all_to_all(
            send_rows.reshape(EXPERTS, MOST, feat_dev),
            "expert",
            split_axis=0,
            concat_axis=1,
            tiled=True,
        ),
        lax.all_to_all(
            send_gate.reshape(EXPERTS, MOST), "expert", split_axis=0, concat_axis=1, tiled=True
        ),
    )
    gate_wide = recv_gate.astype(jnp.float32)[:, :, None]
    full_rows = lax.all_gather(recv_rows, "tensor", axis=2, tiled=True)
    weighted = (full_rows.astype(jnp.float32) * gate_wide).astype(jnp.bfloat16)
    weight_grad = jnp.einsum(
        "esh,esd->ehd", hidden_act[0], weighted, preferred_element_type=jnp.float32
    ).astype(jnp.bfloat16)
    return weight_grad[None]


def place_kernel(n_expert, owned, *refs):
    *metas, place_ref = refs
    first = lax.axis_index("expert") * owned
    experts = (first + lax.broadcasted_iota(jnp.int32, (owned, TOK), 0)).astype(jnp.float32)
    earlier = (
        lax.broadcasted_iota(jnp.int32, (TOK, TOK), 0)
        < lax.broadcasted_iota(jnp.int32, (TOK, TOK), 1)
    ).astype(jnp.float32)
    ranks = lax.broadcasted_iota(jnp.int32, (ROOM, TOK), 0).astype(jnp.float32)
    for k in range(n_expert):
        meta = metas[k][...].astype(jnp.float32)
        named = jnp.zeros((owned, TOK), jnp.float32)
        gate = jnp.zeros((owned, TOK), jnp.float32)
        for c in range(TOPK):
            hit = experts == meta[c : c + 1, :]
            named = jnp.where(hit, 1.0, named)
            gate = jnp.where(hit, meta[TOPK + c : TOPK + c + 1, :], gate)
        rank = jnp.dot(named, earlier, preferred_element_type=jnp.float32)
        rank = jnp.where(named > 0.0, rank, -1.0)
        for e in range(owned):
            place_ref[k, e * ROOM : (e + 1) * ROOM, :] = jnp.where(
                ranks == rank[e : e + 1, :], gate[e : e + 1, :], 0.0
            ).astype(jnp.bfloat16)


def grad_kernel(n_expert, other, offset, feat_dev, turn, split, place_ref, act_ref, *refs):
    blocks = refs[:n_expert]
    out_ref, weighted_ref, done_ref, out_sem = refs[-4:]
    owned, hid, _ = act_ref.shape
    features = done_ref.shape[2]
    me = lax.axis_index("expert")
    side = lax.rem(lax.axis_index("tensor") + other, lax.axis_size("tensor"))
    column = pl.multiple_of(side * feat_dev + offset, 128)
    share = owned // GROUPS
    part = hid // split

    def leave(e, slot, s):
        some = slice(s * part, (s + 1) * part)
        return pltpu.make_async_copy(
            done_ref.at[slot, some],
            out_ref.at[e, some, pl.ds(column, features)],
            out_sem.at[slot, s],
        )

    def tiles():
        for n in range(0, features, 256):
            yield slice(n, min(n + 256, features))

    @pl.loop(0, GROUPS)
    def _(g):
        start = pl.multiple_of(g * share * ROOM, share * ROOM)
        for k in range(n_expert):
            block = lax.rem(me + n_expert - k, n_expert)
            spot = pl.ds(pl.multiple_of(block * ROOM, ROOM), ROOM)
            for wide in tiles():
                weighted = jnp.dot(
                    place_ref[k, pl.ds(start, share * ROOM), :],
                    blocks[k][:, wide],
                    preferred_element_type=jnp.float32,
                ).astype(jnp.bfloat16)
                for j in range(share):
                    weighted_ref[j, spot, wide] = weighted[j * ROOM : (j + 1) * ROOM]

        @pl.loop(0, share // turn)
        def _(p):
            for i in range(turn):
                e = g * share + p * turn + i
                slot = i if turn == TURN else lax.rem(e, TURN)

                @pl.when(e >= TURN)
                def _():
                    for s in range(split):
                        leave(e - TURN, slot, s).wait()

                for wide in tiles():
                    done_ref[slot, :, wide] = jnp.dot(
                        act_ref[e],
                        weighted_ref[p * turn + i, :, wide],
                        preferred_element_type=jnp.float32,
                    ).astype(jnp.bfloat16)
                for s in range(split):
                    leave(e, slot, s).start()

    for slot in range(TURN):
        for s in range(split):
            leave(owned - TURN + slot, slot, s).wait()


def local_by_tokens(sent_grad, head_grad, probs, expert_ids, hidden_act):
    n_expert = lax.axis_size("expert")
    n_tensor = lax.axis_size("tensor")
    owned, _, hid = hidden_act.shape[1:]
    feat_dev = sent_grad.shape[2]
    vmem = pl.BlockSpec(memory_space=pltpu.VMEM)
    anywhere = pl.BlockSpec(memory_space=pl.ANY)

    def turned(array, axis, by):
        peers = lax.axis_size(axis)
        return lax.ppermute(array, axis, [(i, (i + by) % peers) for i in range(peers)])

    meta = jnp.concatenate([expert_ids[0].astype(jnp.bfloat16), probs[0]], axis=1).T
    metas = [meta] + [turned(meta, "expert", k) for k in range(1, n_expert)]
    act = hidden_act[0].reshape(owned, n_expert, MOST, hid)
    act = jnp.pad(act, ((0, 0), (0, 0), (0, ROOM - MOST), (0, 0)))
    act = jnp.swapaxes(act.reshape(owned, n_expert * ROOM, hid), 1, 2)

    def grad_into(out, blocks, other, offset, turn, split):
        span = blocks[0].shape[1]
        operands = [place, act, *blocks]
        in_specs = [vmem] * len(operands)
        aliases = {}
        if out is not None:
            aliases = {len(operands): 0}
            in_specs.append(anywhere)
            operands.append(out)
        return pl.pallas_call(
            functools.partial(grad_kernel, n_expert, other, offset, feat_dev, turn, split),
            out_shape=jax.ShapeDtypeStruct((owned, hid, n_tensor * feat_dev), jnp.bfloat16),
            in_specs=in_specs,
            out_specs=anywhere,
            scratch_shapes=[
                pltpu.VMEM((owned // GROUPS, n_expert * ROOM, span), jnp.bfloat16),
                pltpu.VMEM((TURN, hid, span), jnp.bfloat16),
                pltpu.SemaphoreType.DMA((TURN, split)),
            ],
            input_output_aliases=aliases,
            compiler_params=pltpu.CompilerParams(vmem_limit_bytes=24 * 2**20),
            cost_estimate=pl.CostEstimate(
                flops=2 * owned * hid * 256 * span,
                bytes_accessed=2 * owned * hid * span,
                transcendentals=0,
            ),
            name="weight_grad",
        )(*operands)

    shifted = passed_along(sent_grad, "pipe", -1)
    is_last = lax.axis_index("pipe") == lax.axis_size("pipe") - 1
    place = pl.pallas_call(
        functools.partial(place_kernel, n_expert, owned),
        out_shape=jax.ShapeDtypeStruct((n_expert, owned * ROOM, TOK), jnp.bfloat16),
        in_specs=[vmem] * n_expert,
        out_specs=vmem,
        compiler_params=pltpu.CompilerParams(vmem_limit_bytes=8 * 2**20),
        name="place",
    )(*metas)

    offsets = [sum(CHUNKS[:c]) for c in range(len(CHUNKS))]
    rows, beside = [], []
    for offset, span in zip(offsets, CHUNKS):
        some = slice(offset, offset + span)
        rows.append([jnp.where(is_last, head_grad[:, some], shifted[0][:, some])])
        beside.append({t: [turned(rows[-1][0], "tensor", t)] for t in range(1, n_tensor)})
    for k in range(1, n_expert):
        for c in range(len(CHUNKS)):
            rows[c].append(turned(rows[c][-1], "expert", 1))
            for t in beside[c]:
                beside[c][t].append(turned(rows[c][k], "tensor", t))
        if k >= 2:
            late = [rows[c][k - 1] for c in range(1, len(CHUNKS))]
            passed = [beside[c][t][k - 2] for c in range(len(CHUNKS)) for t in beside[c]]
            if k == 2:
                late += [place, act]
            rows[0][k], late, passed = lax.optimization_barrier((rows[0][k], late, passed))
            if k == 2:
                place, act = late[-2:]
    out = None
    forms = iter([(4, 1), (1, 4), (4, 4), (2, 4)])
    for c, offset in enumerate(offsets):
        out = grad_into(out, rows[c], 0, offset, *next(forms))
        for t in beside[c]:
            out = grad_into(out, beside[c][t], n_tensor - t, offset, *next(forms))
    return out[None]


def local(*arrays):
    owned, slot_count = arrays[4].shape[1:3]
    tokens = lax.axis_size("expert") * TOK
    by_tokens = tokens <= owned * slot_count
    return (local_by_tokens if by_tokens else local_by_slots)(*arrays)


def solution(mesh):
    in_specs = (
        P("pipe", "expert", "tensor"),
        P("expert", "tensor"),
        P("pipe", "expert", None),
        P("pipe", "expert", None),
        P("pipe", "expert", None, "tensor"),
    )
    out_specs = P("pipe", "expert", "tensor", None)
    return jax.shard_map(local, mesh=mesh, in_specs=in_specs, out_specs=out_specs, check_vma=False)
```

```python
import functools

import jax
import jax.numpy as jnp
from jax import lax
from jax.experimental import pallas as pl
from jax.experimental.pallas import tpu as pltpu
from jax.sharding import PartitionSpec as P

EXPERTS = 64
TOPK = 8
TOK = 128
MOST = 17
ROOM = 32
GROUPS = 2
BUFFERS = 4
CHUNKS = (768, 1024)
NOTES = 128


def passed_along(array, axis, by):
    peers = lax.axis_size(axis)
    pairs = [(i, i + by) for i in range(peers) if 0 <= i + by < peers]
    return lax.ppermute(array, axis, pairs)


def slot_ranks(pair_ids):
    onehot = (pair_ids[:, :, None] == jnp.arange(EXPERTS, dtype=jnp.int32)[None, None, :]).astype(
        jnp.int32
    )
    before = jnp.cumsum(onehot, axis=1) - onehot
    return jnp.sum(before * onehot, axis=2)


def place_rows(targets, capacity, source_rows, gate_values):
    pair_count = targets.shape[0]
    owner_pair = (
        jnp.full((capacity,), pair_count, jnp.int32)
        .at[targets]
        .set(jnp.arange(pair_count, dtype=jnp.int32), mode="drop")
    )
    filled = owner_pair < pair_count
    safe_pair = jnp.minimum(owner_pair, pair_count - 1)
    placed = jnp.where(
        filled[:, None], source_rows[safe_pair // TOPK], jnp.zeros((), source_rows.dtype)
    )
    placed_gate = jnp.where(
        filled, gate_values.reshape(-1)[safe_pair], jnp.zeros((), gate_values.dtype)
    )
    return (placed, placed_gate)


def arriving(sent_grad, head_grad):
    shifted = passed_along(sent_grad, "pipe", -1)
    is_last = lax.axis_index("pipe") == lax.axis_size("pipe") - 1
    return jnp.where(is_last, head_grad, shifted[0])


def local_by_slots(sent_grad, head_grad, probs, expert_ids, hidden_act):
    incoming = arriving(sent_grad, head_grad)
    feat_dev = incoming.shape[1]
    local_ids = expert_ids[0].reshape(1, TOK * TOPK)
    local_targets = (local_ids * MOST + slot_ranks(local_ids)).reshape(-1)
    send_rows, send_gate = place_rows(local_targets, EXPERTS * MOST, incoming, probs[0])
    recv_rows, recv_gate = (
        lax.all_to_all(
            send_rows.reshape(EXPERTS, MOST, feat_dev),
            "expert",
            split_axis=0,
            concat_axis=1,
            tiled=True,
        ),
        lax.all_to_all(
            send_gate.reshape(EXPERTS, MOST), "expert", split_axis=0, concat_axis=1, tiled=True
        ),
    )
    gate_wide = recv_gate.astype(jnp.float32)[:, :, None]
    full_rows = lax.all_gather(recv_rows, "tensor", axis=2, tiled=True)
    weighted = (full_rows.astype(jnp.float32) * gate_wide).astype(jnp.bfloat16)
    weight_grad = jnp.einsum(
        "esh,esd->ehd", hidden_act[0], weighted, preferred_element_type=jnp.float32
    ).astype(jnp.bfloat16)
    return weight_grad[None]


def join_kernel(shifted_ref, head_ref, ids_ref, probs_ref, *out_refs):
    is_last = lax.axis_index("pipe") == lax.axis_size("pipe") - 1
    rows = jnp.where(is_last, head_ref[...], shifted_ref[...])
    whole_ref, *chunk_refs = out_refs
    whole_ref[...] = rows
    offset = 0
    for span, chunk_ref in zip(CHUNKS, chunk_refs):
        chunk_ref[:, :span] = rows[:, offset : offset + span]
        offset += span
    first_ref, span = chunk_refs[0], CHUNKS[0]
    first_ref[: 2 * TOPK, span:] = jnp.concatenate(
        [ids_ref[...].astype(jnp.float32), probs_ref[...].astype(jnp.float32)], axis=0
    ).astype(jnp.bfloat16)
    first_ref[2 * TOPK :, span:] = jnp.zeros((TOK - 2 * TOPK, NOTES), jnp.bfloat16)


def place_kernel(owned, *refs):
    *blocks, place_ref = refs
    first = lax.axis_index("expert") * owned
    experts = (first + lax.broadcasted_iota(jnp.int32, (owned, TOK), 0)).astype(jnp.float32)
    earlier = (
        lax.broadcasted_iota(jnp.int32, (TOK, TOK), 0)
        < lax.broadcasted_iota(jnp.int32, (TOK, TOK), 1)
    ).astype(jnp.float32)
    ranks = lax.broadcasted_iota(jnp.int32, (ROOM, TOK), 0).astype(jnp.float32)
    for k, block in enumerate(blocks):
        meta = block[: 2 * TOPK, CHUNKS[0] :].astype(jnp.float32)
        named = jnp.zeros((owned, TOK), jnp.float32)
        gate = jnp.zeros((owned, TOK), jnp.float32)
        for c in range(TOPK):
            hit = experts == meta[c : c + 1, :]
            named = jnp.where(hit, 1.0, named)
            gate = jnp.where(hit, meta[TOPK + c : TOPK + c + 1, :], gate)
        rank = jnp.dot(named, earlier, preferred_element_type=jnp.float32)
        rank = jnp.where(named > 0.0, rank, -1.0)
        for e in range(owned):
            place_ref[k, e * ROOM : (e + 1) * ROOM, :] = jnp.where(
                ranks == rank[e : e + 1, :], gate[e : e + 1, :], 0.0
            ).astype(jnp.bfloat16)


def grad_kernel(n_expert, other, offset, feat_dev, starts, place_ref, act_ref, *refs):
    blocks = refs[:n_expert]
    out_ref, weighted_ref, done_ref, out_sem = refs[-4:]
    owned, hid, _ = act_ref.shape
    features = done_ref.shape[2]
    me = lax.axis_index("expert")
    side = lax.rem(lax.axis_index("tensor") + other, lax.axis_size("tensor"))
    column = pl.multiple_of(side * feat_dev + offset, 128)
    share = owned // GROUPS

    def leave(e):
        slot = lax.rem(e, BUFFERS)
        return pltpu.make_async_copy(
            done_ref.at[slot], out_ref.at[e, :, pl.ds(column, features)], out_sem.at[slot]
        )

    def tiles():
        for n in range(0, features, 256):
            yield n, min(n + 256, features)

    @pl.loop(0, GROUPS)
    def _(g):
        first = pl.multiple_of(g * share * ROOM, share * ROOM)
        for k in range(n_expert):
            block = lax.rem(me + n_expert - k, n_expert)
            spot = pl.ds(pl.multiple_of(block * ROOM, ROOM), ROOM)
            for low, high in tiles():
                weighted = jnp.dot(
                    place_ref[k, pl.ds(first, share * ROOM), :],
                    blocks[k][:, starts[k] + low : starts[k] + high],
                    preferred_element_type=jnp.float32,
                ).astype(jnp.bfloat16)
                for j in range(share):
                    weighted_ref[j, spot, low:high] = weighted[j * ROOM : (j + 1) * ROOM]

        @pl.loop(0, share)
        def _(j):
            e = g * share + j

            @pl.when(e >= BUFFERS)
            def _():
                leave(e - BUFFERS).wait()

            for low, high in tiles():
                done_ref[lax.rem(e, BUFFERS), :, low:high] = jnp.dot(
                    act_ref[e], weighted_ref[j, :, low:high], preferred_element_type=jnp.float32
                ).astype(jnp.bfloat16)
            leave(e).start()

    @pl.loop(owned - BUFFERS, owned)
    def _(e):
        leave(e).wait()


def local_by_tokens(sent_grad, head_grad, probs, expert_ids, hidden_act):
    n_expert = lax.axis_size("expert")
    n_tensor = lax.axis_size("tensor")
    owned, _, hid = hidden_act.shape[1:]
    feat_dev = sent_grad.shape[2]
    vmem = pl.BlockSpec(memory_space=pltpu.VMEM)
    anywhere = pl.BlockSpec(memory_space=pl.ANY)

    def small_call(kernel, shapes, operands, name):
        return pl.pallas_call(
            kernel,
            out_shape=[jax.ShapeDtypeStruct(shape, jnp.bfloat16) for shape in shapes],
            in_specs=[vmem] * len(operands),
            out_specs=[vmem] * len(shapes),
            compiler_params=pltpu.CompilerParams(vmem_limit_bytes=8 * 2**20),
            name=name,
        )(*operands)

    def turned(array, axis, by):
        peers = lax.axis_size(axis)
        return lax.ppermute(array, axis, [(i, (i + by) % peers) for i in range(peers)])

    def across(array):
        return {t: turned(array, "tensor", t) for t in range(1, n_tensor)}

    act = hidden_act[0].reshape(owned, n_expert, MOST, hid)
    act = jnp.pad(act, ((0, 0), (0, 0), (0, ROOM - MOST), (0, 0)))
    act = jnp.swapaxes(act.reshape(owned, n_expert * ROOM, hid), 1, 2)

    def grad_into(out, blocks, starts, other, chunk):
        span, offset = CHUNKS[chunk], sum(CHUNKS[:chunk])
        operands = [place, act, *blocks]
        in_specs = [vmem] * len(operands)
        aliases = {}
        if out is not None:
            aliases = {len(operands): 0}
            in_specs.append(anywhere)
            operands.append(out)
        return pl.pallas_call(
            functools.partial(grad_kernel, n_expert, other, offset, feat_dev, starts),
            out_shape=jax.ShapeDtypeStruct((owned, hid, n_tensor * feat_dev), jnp.bfloat16),
            in_specs=in_specs,
            out_specs=anywhere,
            scratch_shapes=[
                pltpu.VMEM((owned // GROUPS, n_expert * ROOM, span), jnp.bfloat16),
                pltpu.VMEM((BUFFERS, hid, span), jnp.bfloat16),
                pltpu.SemaphoreType.DMA((BUFFERS,)),
            ],
            input_output_aliases=aliases,
            compiler_params=pltpu.CompilerParams(vmem_limit_bytes=24 * 2**20),
            cost_estimate=pl.CostEstimate(
                flops=2 * owned * hid * 256 * span,
                bytes_accessed=2 * owned * hid * span,
                transcendentals=0,
            ),
            name="weight_grad",
        )(*operands)

    shifted = passed_along(sent_grad, "pipe", -1)[0]
    widths = (feat_dev, CHUNKS[0] + NOTES) + CHUNKS[1:]
    whole, *firsts = small_call(
        join_kernel,
        [(TOK, width) for width in widths],
        [shifted, head_grad, expert_ids[0].T, probs[0].T],
        "join",
    )
    beside_whole = across(whole)
    rows, beside = [], []
    for first in firsts:
        if rows:
            rows[-1][1], first = lax.optimization_barrier((rows[-1][1], first))
        blocks = {0: first}
        blocks[1] = turned(first, "expert", 1)
        blocks[n_expert - 1] = turned(first, "expert", -1)
        for k in range(2, n_expert - 1):
            blocks[k] = turned(blocks[k - 1], "expert", 1)
        rows.append(blocks)
        beside.append({k: across(blocks[k]) for k in range(1, n_expert)})
    (place,) = small_call(
        functools.partial(place_kernel, owned),
        [(n_expert, owned * ROOM, TOK)],
        [rows[0][k] for k in range(n_expert)],
        "place",
    )
    out = None
    for c in range(len(CHUNKS)):
        out = grad_into(out, [rows[c][k] for k in range(n_expert)], (0,) * n_expert, 0, c)
        for t in range(1, n_tensor):
            blocks = [beside_whole[t]] + [beside[c][k][t] for k in range(1, n_expert)]
            starts = (sum(CHUNKS[:c]),) + (0,) * (n_expert - 1)
            out = grad_into(out, blocks, starts, n_tensor - t, c)
    return out[None]


def local(*arrays):
    owned, slot_count = arrays[4].shape[1:3]
    tokens = lax.axis_size("expert") * TOK
    by_tokens = tokens <= owned * slot_count
    return (local_by_tokens if by_tokens else local_by_slots)(*arrays)


def solution(mesh):
    in_specs = (
        P("pipe", "expert", "tensor"),
        P("expert", "tensor"),
        P("pipe", "expert", None),
        P("pipe", "expert", None),
        P("pipe", "expert", None, "tensor"),
    )
    out_specs = P("pipe", "expert", "tensor", None)
    return jax.shard_map(local, mesh=mesh, in_specs=in_specs, out_specs=out_specs, check_vma=False)
```

```python
import functools

import jax
import jax.numpy as jnp
from jax import lax
from jax.experimental import pallas as pl
from jax.experimental.pallas import tpu as pltpu
from jax.sharding import PartitionSpec as P

EXPERTS = 64
TOPK = 8
TOK = 128
MOST = 17
ROOM = 32
CHUNKS = (768, 1024)
NOTES = 128


def passed_along(array, axis, by):
    peers = lax.axis_size(axis)
    pairs = [(i, i + by) for i in range(peers) if 0 <= i + by < peers]
    return lax.ppermute(array, axis, pairs)


def slot_ranks(pair_ids):
    onehot = (pair_ids[:, :, None] == jnp.arange(EXPERTS, dtype=jnp.int32)[None, None, :]).astype(
        jnp.int32
    )
    before = jnp.cumsum(onehot, axis=1) - onehot
    return jnp.sum(before * onehot, axis=2)


def place_rows(targets, capacity, source_rows, gate_values):
    pair_count = targets.shape[0]
    owner_pair = (
        jnp.full((capacity,), pair_count, jnp.int32)
        .at[targets]
        .set(jnp.arange(pair_count, dtype=jnp.int32), mode="drop")
    )
    filled = owner_pair < pair_count
    safe_pair = jnp.minimum(owner_pair, pair_count - 1)
    placed = jnp.where(
        filled[:, None], source_rows[safe_pair // TOPK], jnp.zeros((), source_rows.dtype)
    )
    placed_gate = jnp.where(
        filled, gate_values.reshape(-1)[safe_pair], jnp.zeros((), gate_values.dtype)
    )
    return (placed, placed_gate)


def arriving(sent_grad, head_grad):
    shifted = passed_along(sent_grad, "pipe", -1)
    is_last = lax.axis_index("pipe") == lax.axis_size("pipe") - 1
    return jnp.where(is_last, head_grad, shifted[0])


def local_by_slots(sent_grad, head_grad, probs, expert_ids, hidden_act):
    incoming = arriving(sent_grad, head_grad)
    feat_dev = incoming.shape[1]
    local_ids = expert_ids[0].reshape(1, TOK * TOPK)
    local_targets = (local_ids * MOST + slot_ranks(local_ids)).reshape(-1)
    send_rows, send_gate = place_rows(local_targets, EXPERTS * MOST, incoming, probs[0])
    recv_rows, recv_gate = (
        lax.all_to_all(
            send_rows.reshape(EXPERTS, MOST, feat_dev),
            "expert",
            split_axis=0,
            concat_axis=1,
            tiled=True,
        ),
        lax.all_to_all(
            send_gate.reshape(EXPERTS, MOST), "expert", split_axis=0, concat_axis=1, tiled=True
        ),
    )
    gate_wide = recv_gate.astype(jnp.float32)[:, :, None]
    full_rows = lax.all_gather(recv_rows, "tensor", axis=2, tiled=True)
    weighted = (full_rows.astype(jnp.float32) * gate_wide).astype(jnp.bfloat16)
    weight_grad = jnp.einsum(
        "esh,esd->ehd", hidden_act[0], weighted, preferred_element_type=jnp.float32
    ).astype(jnp.bfloat16)
    return weight_grad[None]


def notes_kernel(head_ref, ids_ref, probs_ref, kept_ref, notes_ref):
    kept_ref[...] = head_ref[...]
    notes_ref[: 2 * TOPK] = jnp.concatenate(
        [ids_ref[...].astype(jnp.float32), probs_ref[...].astype(jnp.float32)], axis=0
    ).astype(jnp.bfloat16)
    notes_ref[2 * TOPK :] = jnp.zeros((TOK - 2 * TOPK, NOTES), jnp.bfloat16)


def join_kernel(shifted_ref, head_ref, notes_ref, *out_refs):
    is_last = lax.axis_index("pipe") == lax.axis_size("pipe") - 1
    rows = jnp.where(is_last, head_ref[...], shifted_ref[...])
    whole_ref, *chunk_refs = out_refs
    whole_ref[...] = rows
    offset = 0
    for span, chunk_ref in zip(CHUNKS, chunk_refs):
        chunk_ref[:, :span] = rows[:, offset : offset + span]
        offset += span
    chunk_refs[0][:, CHUNKS[0] :] = notes_ref[...]


def place_kernel(owned, *refs):
    *blocks, place_ref = refs
    first = lax.axis_index("expert") * owned
    experts = (first + lax.broadcasted_iota(jnp.int32, (owned, TOK), 0)).astype(jnp.float32)
    earlier = (
        lax.broadcasted_iota(jnp.int32, (TOK, TOK), 0)
        < lax.broadcasted_iota(jnp.int32, (TOK, TOK), 1)
    ).astype(jnp.float32)
    ranks = lax.broadcasted_iota(jnp.int32, (ROOM, TOK), 0).astype(jnp.float32)
    for k, block in enumerate(blocks):
        meta = block[: 2 * TOPK, CHUNKS[0] :].astype(jnp.float32)
        named = jnp.zeros((owned, TOK), jnp.float32)
        gate = jnp.zeros((owned, TOK), jnp.float32)
        for c in range(TOPK):
            hit = experts == meta[c : c + 1, :]
            named = jnp.where(hit, 1.0, named)
            gate = jnp.where(hit, meta[TOPK + c : TOPK + c + 1, :], gate)
        rank = jnp.dot(named, earlier, preferred_element_type=jnp.float32)
        rank = jnp.where(named > 0.0, rank, -1.0)
        for e in range(owned):
            place_ref[k, e * ROOM : (e + 1) * ROOM, :] = jnp.where(
                ranks == rank[e : e + 1, :], gate[e : e + 1, :], 0.0
            ).astype(jnp.bfloat16)


def grad_kernel(n_expert, other, offset, feat_dev, starts, form, place_ref, act_ref, *refs):
    groups, buffers, looped = form
    blocks = refs[:n_expert]
    out_ref, weighted_ref, done_ref, out_sem = refs[-4:]
    owned, hid, _ = act_ref.shape
    features = done_ref.shape[2]
    me = lax.axis_index("expert")
    side = lax.rem(lax.axis_index("tensor") + other, lax.axis_size("tensor"))
    column = pl.multiple_of(side * feat_dev + offset, 128)
    share = owned // groups

    def leave(e):
        slot = lax.rem(e, buffers)
        return pltpu.make_async_copy(
            done_ref.at[slot], out_ref.at[e, :, pl.ds(column, features)], out_sem.at[slot]
        )

    def over_tiles(step, loop):
        if loop:

            @pl.loop(0, features // 256)
            def _(n):
                step(pl.multiple_of(n * 256, 256))

        else:
            for n in range(0, features, 256):
                step(n)

    @pl.loop(0, groups)
    def _(g):
        first = pl.multiple_of(g * share * ROOM, share * ROOM)

        def weigh(n):
            for k in range(n_expert):
                block = lax.rem(me + n_expert - k, n_expert)
                spot = pl.ds(pl.multiple_of(block * ROOM, ROOM), ROOM)
                weighted = jnp.dot(
                    place_ref[k, pl.ds(first, share * ROOM), :],
                    blocks[k][:, pl.ds(starts[k] + n, 256)],
                    preferred_element_type=jnp.float32,
                ).astype(jnp.bfloat16)
                for j in range(share):
                    weighted_ref[j, spot, pl.ds(n, 256)] = weighted[j * ROOM : (j + 1) * ROOM]

        over_tiles(weigh, "weigh" in looped)

        @pl.loop(0, share)
        def _(j):
            e = g * share + j

            @pl.when(e >= buffers)
            def _():
                leave(e - buffers).wait()

            def multiply(n):
                done_ref[lax.rem(e, buffers), :, pl.ds(n, 256)] = jnp.dot(
                    act_ref[e],
                    weighted_ref[j, :, pl.ds(n, 256)],
                    preferred_element_type=jnp.float32,
                ).astype(jnp.bfloat16)

            over_tiles(multiply, "multiply" in looped)
            leave(e).start()

    @pl.loop(owned - buffers, owned)
    def _(e):
        leave(e).wait()


def local_by_tokens(sent_grad, head_grad, probs, expert_ids, hidden_act):
    n_expert = lax.axis_size("expert")
    n_tensor = lax.axis_size("tensor")
    owned, _, hid = hidden_act.shape[1:]
    feat_dev = sent_grad.shape[2]
    vmem = pl.BlockSpec(memory_space=pltpu.VMEM)
    anywhere = pl.BlockSpec(memory_space=pl.ANY)

    def small_call(kernel, shapes, operands, name):
        return pl.pallas_call(
            kernel,
            out_shape=[jax.ShapeDtypeStruct(shape, jnp.bfloat16) for shape in shapes],
            in_specs=[vmem] * len(operands),
            out_specs=[vmem] * len(shapes),
            compiler_params=pltpu.CompilerParams(vmem_limit_bytes=8 * 2**20),
            name=name,
        )(*operands)

    def turned(array, axis, by):
        peers = lax.axis_size(axis)
        return lax.ppermute(array, axis, [(i, (i + by) % peers) for i in range(peers)])

    def across(array):
        return {t: turned(array, "tensor", t) for t in range(1, n_tensor)}

    act = hidden_act[0].reshape(owned, n_expert, MOST, hid)
    act = jnp.pad(act, ((0, 0), (0, 0), (0, ROOM - MOST), (0, 0)))
    act = act.reshape(owned, n_expert * ROOM, hid)

    def grad_into(out, blocks, starts, other, chunk, form):
        span, offset = CHUNKS[chunk], sum(CHUNKS[:chunk])
        operands = [place, act, *blocks]
        in_specs = [vmem] * len(operands)
        aliases = {}
        if out is not None:
            aliases = {len(operands): 0}
            in_specs.append(anywhere)
            operands.append(out)
        return pl.pallas_call(
            functools.partial(grad_kernel, n_expert, other, offset, feat_dev, starts, form),
            out_shape=jax.ShapeDtypeStruct((owned, hid, n_tensor * feat_dev), jnp.bfloat16),
            in_specs=in_specs,
            out_specs=anywhere,
            scratch_shapes=[
                pltpu.VMEM((owned // form[0], n_expert * ROOM, span), jnp.bfloat16),
                pltpu.VMEM((form[1], hid, span), jnp.bfloat16),
                pltpu.SemaphoreType.DMA((form[1],)),
            ],
            input_output_aliases=aliases,
            compiler_params=pltpu.CompilerParams(vmem_limit_bytes=24 * 2**20),
            cost_estimate=pl.CostEstimate(
                flops=2 * owned * hid * 256 * span,
                bytes_accessed=2 * owned * hid * span,
                transcendentals=0,
            ),
            name="weight_grad",
        )(*operands)

    shifted = passed_along(sent_grad, "pipe", -1)[0]
    widths = (feat_dev, CHUNKS[0] + NOTES) + CHUNKS[1:]
    kept, notes = small_call(
        notes_kernel,
        [head_grad.shape, (TOK, NOTES)],
        [head_grad, expert_ids[0].T, probs[0].T],
        "notes",
    )
    shifted, kept, notes, act = lax.optimization_barrier((shifted, kept, notes, act))
    act = jnp.swapaxes(act, 1, 2)
    whole, *firsts = small_call(
        join_kernel, [(TOK, width) for width in widths], [shifted, kept, notes], "join"
    )
    beside_whole = across(whole)
    rows = []
    for first in firsts:
        blocks = {0: first}
        if rows:
            rows[-1][1], first, act = lax.optimization_barrier((rows[-1][1], first, act))
        blocks[1] = turned(first, "expert", 1)
        blocks[n_expert - 1] = turned(first, "expert", -1)
        rows.append(blocks)
    beside = []
    for blocks in rows:
        for k in range(2, n_expert - 1):
            blocks[k] = turned(blocks[k - 1], "expert", 1)
        beside.append({k: across(blocks[k]) for k in range(1, n_expert)})
    (place,) = small_call(
        functools.partial(place_kernel, owned),
        [(n_expert, owned * ROOM, TOK)],
        [rows[0][k] for k in range(n_expert)],
        "place",
    )
    forms = iter([(4, 4, ""), (2, 4, "weigh"), (2, 4, "multiply"), (2, 8, "")])
    out = None
    for c in range(len(CHUNKS)):
        blocks = [rows[c][k] for k in range(n_expert)]
        out = grad_into(out, blocks, (0,) * n_expert, 0, c, next(forms))
        for t in range(1, n_tensor):
            blocks = [beside_whole[t]] + [beside[c][k][t] for k in range(1, n_expert)]
            starts = (sum(CHUNKS[:c]),) + (0,) * (n_expert - 1)
            out = grad_into(out, blocks, starts, n_tensor - t, c, next(forms))
    return out[None]


def local(*arrays):
    owned, slot_count = arrays[4].shape[1:3]
    tokens = lax.axis_size("expert") * TOK
    by_tokens = tokens <= owned * slot_count
    return (local_by_tokens if by_tokens else local_by_slots)(*arrays)


def solution(mesh):
    in_specs = (
        P("pipe", "expert", "tensor"),
        P("expert", "tensor"),
        P("pipe", "expert", None),
        P("pipe", "expert", None),
        P("pipe", "expert", None, "tensor"),
    )
    out_specs = P("pipe", "expert", "tensor", None)
    return jax.shard_map(local, mesh=mesh, in_specs=in_specs, out_specs=out_specs, check_vma=False)
```

```python
import functools

import jax
import jax.numpy as jnp
from jax import lax
from jax.experimental import pallas as pl
from jax.experimental.pallas import tpu as pltpu
from jax.sharding import PartitionSpec as P

EXPERTS = 64
TOPK = 8
TOK = 128
MOST = 17
ROOM = 32
CHUNKS = (768, 1024)
NOTES = 128
BUFFERS = 4


def passed_along(array, axis, by):
    peers = lax.axis_size(axis)
    pairs = [(i, i + by) for i in range(peers) if 0 <= i + by < peers]
    return lax.ppermute(array, axis, pairs)


def slot_ranks(pair_ids):
    onehot = (pair_ids[:, :, None] == jnp.arange(EXPERTS, dtype=jnp.int32)[None, None, :]).astype(
        jnp.int32
    )
    before = jnp.cumsum(onehot, axis=1) - onehot
    return jnp.sum(before * onehot, axis=2)


def place_rows(targets, capacity, source_rows, gate_values):
    pair_count = targets.shape[0]
    owner_pair = (
        jnp.full((capacity,), pair_count, jnp.int32)
        .at[targets]
        .set(jnp.arange(pair_count, dtype=jnp.int32), mode="drop")
    )
    filled = owner_pair < pair_count
    safe_pair = jnp.minimum(owner_pair, pair_count - 1)
    placed = jnp.where(
        filled[:, None], source_rows[safe_pair // TOPK], jnp.zeros((), source_rows.dtype)
    )
    placed_gate = jnp.where(
        filled, gate_values.reshape(-1)[safe_pair], jnp.zeros((), gate_values.dtype)
    )
    return (placed, placed_gate)


def arriving(sent_grad, head_grad):
    shifted = passed_along(sent_grad, "pipe", -1)
    is_last = lax.axis_index("pipe") == lax.axis_size("pipe") - 1
    return jnp.where(is_last, head_grad, shifted[0])


def local_by_slots(sent_grad, head_grad, probs, expert_ids, hidden_act):
    incoming = arriving(sent_grad, head_grad)
    feat_dev = incoming.shape[1]
    local_ids = expert_ids[0].reshape(1, TOK * TOPK)
    local_targets = (local_ids * MOST + slot_ranks(local_ids)).reshape(-1)
    send_rows, send_gate = place_rows(local_targets, EXPERTS * MOST, incoming, probs[0])
    recv_rows, recv_gate = (
        lax.all_to_all(
            send_rows.reshape(EXPERTS, MOST, feat_dev),
            "expert",
            split_axis=0,
            concat_axis=1,
            tiled=True,
        ),
        lax.all_to_all(
            send_gate.reshape(EXPERTS, MOST), "expert", split_axis=0, concat_axis=1, tiled=True
        ),
    )
    gate_wide = recv_gate.astype(jnp.float32)[:, :, None]
    full_rows = lax.all_gather(recv_rows, "tensor", axis=2, tiled=True)
    weighted = (full_rows.astype(jnp.float32) * gate_wide).astype(jnp.bfloat16)
    weight_grad = jnp.einsum(
        "esh,esd->ehd", hidden_act[0], weighted, preferred_element_type=jnp.float32
    ).astype(jnp.bfloat16)
    return weight_grad[None]


def notes_kernel(head_ref, ids_ref, probs_ref, kept_ref, notes_ref):
    kept_ref[...] = head_ref[...]
    notes_ref[: 2 * TOPK] = jnp.concatenate(
        [ids_ref[...].astype(jnp.float32), probs_ref[...].astype(jnp.float32)], axis=0
    ).astype(jnp.bfloat16)
    notes_ref[2 * TOPK :] = jnp.zeros((TOK - 2 * TOPK, NOTES), jnp.bfloat16)


def join_kernel(shifted_ref, head_ref, notes_ref, *out_refs):
    is_last = lax.axis_index("pipe") == lax.axis_size("pipe") - 1
    rows = jnp.where(is_last, head_ref[...], shifted_ref[...])
    whole_ref, *chunk_refs = out_refs
    whole_ref[...] = rows
    offset = 0
    for span, chunk_ref in zip(CHUNKS, chunk_refs):
        chunk_ref[:, :span] = rows[:, offset : offset + span]
        offset += span
    chunk_refs[0][:, CHUNKS[0] :] = notes_ref[...]


def turn_kernel(n_expert, act_ref, turned_ref):
    owned, slot_count, _ = act_ref.shape
    me = lax.axis_index("expert")
    slot = lax.broadcasted_iota(jnp.int32, (slot_count, n_expert * ROOM), 0)
    spot = lax.broadcasted_iota(jnp.int32, (slot_count, n_expert * ROOM), 1)
    block = jnp.zeros_like(slot)
    for b in range(1, n_expert):
        block += (slot >= b * MOST).astype(jnp.int32)
    back = me - block
    back = jnp.where(back < 0, back + n_expert, back)
    target = back * ROOM + slot - block * MOST
    for e in range(owned):
        turned_ref[e] = lax.dot_general(
            act_ref[e],
            (spot == target + e).astype(jnp.bfloat16),
            (((0,), (0,)), ((), ())),
            preferred_element_type=jnp.float32,
        ).astype(jnp.bfloat16)


def place_kernel(owned, *refs):
    *blocks, place_ref = refs
    first = lax.axis_index("expert") * owned
    rows = place_ref.shape[1]
    experts = (first + lax.broadcasted_iota(jnp.int32, (owned, TOK), 0)).astype(jnp.float32)
    earlier = (
        lax.broadcasted_iota(jnp.int32, (TOK, TOK), 0)
        < lax.broadcasted_iota(jnp.int32, (TOK, TOK), 1)
    ).astype(jnp.float32)
    row = lax.broadcasted_iota(jnp.int32, (rows, owned), 0)
    start = lax.broadcasted_iota(jnp.int32, (rows, owned), 1) * MOST
    spread = ((row >= start) & (row < start + MOST)).astype(jnp.float32)
    wanted = lax.broadcasted_iota(jnp.int32, (rows, TOK), 0)
    for e in range(1, owned):
        wanted -= MOST * (
            lax.broadcasted_iota(jnp.int32, (rows, TOK), 0) >= e * MOST
        ).astype(jnp.int32)
    wanted = wanted.astype(jnp.float32)
    for k, block in enumerate(blocks):
        meta = block[: 2 * TOPK, CHUNKS[0] :].astype(jnp.float32)
        named = jnp.zeros((owned, TOK), jnp.float32)
        gate = jnp.zeros((owned, TOK), jnp.float32)
        for c in range(TOPK):
            hit = experts == meta[c : c + 1, :]
            named = jnp.where(hit, 1.0, named)
            gate = jnp.where(hit, meta[TOPK + c : TOPK + c + 1, :], gate)
        rank = jnp.dot(named, earlier, preferred_element_type=jnp.float32)
        rank = jnp.where(named > 0.0, rank, -1.0)
        rank = jnp.dot(spread, rank, preferred_element_type=jnp.float32)
        gate = jnp.dot(spread, gate, preferred_element_type=jnp.float32)
        place_ref[k] = jnp.where(rank == wanted, gate, 0.0).astype(jnp.bfloat16)


def grad_kernel(n_expert, other, offset, feat_dev, starts, turn, place_ref, act_ref, *refs):
    blocks = refs[:n_expert]
    out_ref, weighted_ref, done_ref, out_sem = refs[-4:]
    owned, hid, _ = act_ref.shape
    features = done_ref.shape[2]
    side = lax.rem(lax.axis_index("tensor") + other, lax.axis_size("tensor"))
    column = pl.multiple_of(side * feat_dev + offset, 128)

    def leave(e):
        slot = lax.rem(e, BUFFERS)
        return pltpu.make_async_copy(
            done_ref.at[slot], out_ref.at[e, :, pl.ds(column, features)], out_sem.at[slot]
        )

    @pl.loop(0, features // 256)
    def _(t):
        wide = pl.ds(pl.multiple_of(t * 256, 256), 256)
        for k in range(n_expert):
            rows = pl.ds(pl.multiple_of(starts[k] + t * 256, 256), 256)
            weighted_ref[k, :, wide] = jnp.dot(
                place_ref[k], blocks[k][:, rows], preferred_element_type=jnp.float32
            ).astype(jnp.bfloat16)

    @pl.loop(0, owned // turn)
    def _(p):
        for i in range(turn):
            e = p * turn + i

            @pl.when(e >= BUFFERS)
            def _():
                leave(e - BUFFERS).wait()

        for i in range(turn):
            e = p * turn + i
            window = pl.ds(pl.multiple_of(e * 16, 16), ROOM)
            for n in range(0, features, 256):
                right = jnp.concatenate(
                    [weighted_ref[k, window, n : n + 256] for k in range(n_expert)], axis=0
                )
                done_ref[lax.rem(e, BUFFERS), :, n : n + 256] = jnp.dot(
                    act_ref[e], right, preferred_element_type=jnp.float32
                ).astype(jnp.bfloat16)
        for i in range(turn):
            leave(p * turn + i).start()

    @pl.loop(owned - BUFFERS, owned)
    def _(e):
        leave(e).wait()


def local_by_tokens(sent_grad, head_grad, probs, expert_ids, hidden_act):
    n_expert = lax.axis_size("expert")
    n_tensor = lax.axis_size("tensor")
    owned, _, hid = hidden_act.shape[1:]
    feat_dev = sent_grad.shape[2]
    vmem = pl.BlockSpec(memory_space=pltpu.VMEM)
    anywhere = pl.BlockSpec(memory_space=pl.ANY)

    def small_call(kernel, shapes, operands, name):
        return pl.pallas_call(
            kernel,
            out_shape=[jax.ShapeDtypeStruct(shape, jnp.bfloat16) for shape in shapes],
            in_specs=[vmem] * len(operands),
            out_specs=[vmem] * len(shapes),
            compiler_params=pltpu.CompilerParams(vmem_limit_bytes=8 * 2**20),
            name=name,
        )(*operands)

    def turned(array, axis, by):
        peers = lax.axis_size(axis)
        return lax.ppermute(array, axis, [(i, (i + by) % peers) for i in range(peers)])

    def across(array):
        return {t: turned(array, "tensor", t) for t in range(1, n_tensor)}

    def grad_into(out, blocks, starts, other, chunk, turn):
        span, offset = CHUNKS[chunk], sum(CHUNKS[:chunk])
        operands = [place, act, *blocks]
        in_specs = [vmem] * len(operands)
        aliases = {}
        if out is not None:
            aliases = {len(operands): 0}
            in_specs.append(anywhere)
            operands.append(out)
        return pl.pallas_call(
            functools.partial(grad_kernel, n_expert, other, offset, feat_dev, starts, turn),
            out_shape=jax.ShapeDtypeStruct((owned, hid, n_tensor * feat_dev), jnp.bfloat16),
            in_specs=in_specs,
            out_specs=anywhere,
            scratch_shapes=[
                pltpu.VMEM((n_expert, place.shape[1], span), jnp.bfloat16),
                pltpu.VMEM((BUFFERS, hid, span), jnp.bfloat16),
                pltpu.SemaphoreType.DMA((BUFFERS,)),
            ],
            input_output_aliases=aliases,
            compiler_params=pltpu.CompilerParams(vmem_limit_bytes=24 * 2**20),
            cost_estimate=pl.CostEstimate(
                flops=2 * owned * hid * 256 * span,
                bytes_accessed=2 * owned * hid * span,
                transcendentals=0,
            ),
            name="weight_grad",
        )(*operands)

    shifted = passed_along(sent_grad, "pipe", -1)[0]
    widths = (feat_dev, CHUNKS[0] + NOTES) + CHUNKS[1:]
    kept, notes = small_call(
        notes_kernel,
        [head_grad.shape, (TOK, NOTES)],
        [head_grad, expert_ids[0].T, probs[0].T],
        "notes",
    )
    shifted, kept, notes, act = lax.optimization_barrier((shifted, kept, notes, hidden_act[0]))
    (act,) = small_call(
        functools.partial(turn_kernel, n_expert), [(owned, hid, n_expert * ROOM)], [act], "turn"
    )
    whole, *firsts = small_call(
        join_kernel, [(TOK, width) for width in widths], [shifted, kept, notes], "join"
    )
    beside_whole = across(whole)
    rows = []
    for first in firsts:
        blocks = {0: first}
        blocks[1] = turned(first, "expert", 1)
        if not rows:
            blocks[1], first, act, firsts[1:] = lax.optimization_barrier(
                (blocks[1], first, act, firsts[1:])
            )
        for k in range(2, n_expert - 1):
            blocks[k] = turned(blocks[k - 1], "expert", 1)
        blocks[n_expert - 1] = turned(first, "expert", -1)
        rows.append(blocks)
    beside = [{k: across(blocks[k]) for k in range(1, n_expert)} for blocks in rows]
    (place,) = small_call(
        functools.partial(place_kernel, owned),
        [(n_expert, 16 * (owned + 1), TOK)],
        [rows[0][k] for k in range(n_expert)],
        "place",
    )
    turns = iter([1, 2, 1, 2])
    out = None
    for c in range(len(CHUNKS)):
        blocks = [rows[c][k] for k in range(n_expert)]
        out = grad_into(out, blocks, (0,) * n_expert, 0, c, next(turns))
        for t in range(1, n_tensor):
            blocks = [beside_whole[t]] + [beside[c][k][t] for k in range(1, n_expert)]
            starts = (sum(CHUNKS[:c]),) + (0,) * (n_expert - 1)
            out = grad_into(out, blocks, starts, n_tensor - t, c, next(turns))
    return out[None]


def local(*arrays):
    owned, slot_count = arrays[4].shape[1:3]
    tokens = lax.axis_size("expert") * TOK
    by_tokens = owned <= 16 and tokens <= owned * slot_count
    return (local_by_tokens if by_tokens else local_by_slots)(*arrays)


def solution(mesh):
    in_specs = (
        P("pipe", "expert", "tensor"),
        P("expert", "tensor"),
        P("pipe", "expert", None),
        P("pipe", "expert", None),
        P("pipe", "expert", None, "tensor"),
    )
    out_specs = P("pipe", "expert", "tensor", None)
    return jax.shard_map(local, mesh=mesh, in_specs=in_specs, out_specs=out_specs, check_vma=False)
```

```python
import functools

import jax
import jax.numpy as jnp
from jax import lax
from jax.experimental import pallas as pl
from jax.experimental.pallas import tpu as pltpu
from jax.sharding import PartitionSpec as P

EXPERTS = 64
TOPK = 8
TOK = 128
MOST = 17
ROOM = 32
BUFFERS = 4


def passed_along(array, axis, by):
    peers = lax.axis_size(axis)
    pairs = [(i, i + by) for i in range(peers) if 0 <= i + by < peers]
    return lax.ppermute(array, axis, pairs)


def slot_ranks(pair_ids):
    onehot = (pair_ids[:, :, None] == jnp.arange(EXPERTS, dtype=jnp.int32)[None, None, :]).astype(
        jnp.int32
    )
    before = jnp.cumsum(onehot, axis=1) - onehot
    return jnp.sum(before * onehot, axis=2)


def place_rows(targets, capacity, source_rows, gate_values):
    pair_count = targets.shape[0]
    owner_pair = (
        jnp.full((capacity,), pair_count, jnp.int32)
        .at[targets]
        .set(jnp.arange(pair_count, dtype=jnp.int32), mode="drop")
    )
    filled = owner_pair < pair_count
    safe_pair = jnp.minimum(owner_pair, pair_count - 1)
    placed = jnp.where(
        filled[:, None], source_rows[safe_pair // TOPK], jnp.zeros((), source_rows.dtype)
    )
    placed_gate = jnp.where(
        filled, gate_values.reshape(-1)[safe_pair], jnp.zeros((), gate_values.dtype)
    )
    return (placed, placed_gate)


def arriving(sent_grad, head_grad):
    shifted = passed_along(sent_grad, "pipe", -1)
    is_last = lax.axis_index("pipe") == lax.axis_size("pipe") - 1
    return jnp.where(is_last, head_grad, shifted[0])


def local_by_slots(sent_grad, head_grad, probs, expert_ids, hidden_act):
    incoming = arriving(sent_grad, head_grad)
    feat_dev = incoming.shape[1]
    local_ids = expert_ids[0].reshape(1, TOK * TOPK)
    local_targets = (local_ids * MOST + slot_ranks(local_ids)).reshape(-1)
    send_rows, send_gate = place_rows(local_targets, EXPERTS * MOST, incoming, probs[0])
    recv_rows, recv_gate = (
        lax.all_to_all(
            send_rows.reshape(EXPERTS, MOST, feat_dev),
            "expert",
            split_axis=0,
            concat_axis=1,
            tiled=True,
        ),
        lax.all_to_all(
            send_gate.reshape(EXPERTS, MOST), "expert", split_axis=0, concat_axis=1, tiled=True
        ),
    )
    gate_wide = recv_gate.astype(jnp.float32)[:, :, None]
    full_rows = lax.all_gather(recv_rows, "tensor", axis=2, tiled=True)
    weighted = (full_rows.astype(jnp.float32) * gate_wide).astype(jnp.bfloat16)
    weight_grad = jnp.einsum(
        "esh,esd->ehd", hidden_act[0], weighted, preferred_element_type=jnp.float32
    ).astype(jnp.bfloat16)
    return weight_grad[None]


def notes_kernel(head_ref, ids_ref, probs_ref, kept_ref, notes_ref):
    kept_ref[...] = head_ref[...]
    notes_ref[...] = jnp.concatenate(
        [ids_ref[...].astype(jnp.float32), probs_ref[...].astype(jnp.float32)], axis=0
    ).astype(jnp.bfloat16)


def join_kernel(shifted_ref, head_ref, rows_ref):
    is_last = lax.axis_index("pipe") == lax.axis_size("pipe") - 1
    rows_ref[...] = jnp.where(is_last, head_ref[...], shifted_ref[...])


def turn_kernel(n_expert, act_ref, turned_ref):
    owned, slot_count, _ = act_ref.shape
    me = lax.axis_index("expert")
    slot = lax.broadcasted_iota(jnp.int32, (slot_count, n_expert * ROOM), 0)
    spot = lax.broadcasted_iota(jnp.int32, (slot_count, n_expert * ROOM), 1)
    block = jnp.zeros_like(slot)
    for b in range(1, n_expert):
        block += (slot >= b * MOST).astype(jnp.int32)
    back = me - block
    back = jnp.where(back < 0, back + n_expert, back)
    target = back * ROOM + slot - block * MOST
    for e in range(owned):
        turned_ref[e] = lax.dot_general(
            act_ref[e],
            (spot == target + e).astype(jnp.bfloat16),
            (((0,), (0,)), ((), ())),
            preferred_element_type=jnp.float32,
        ).astype(jnp.bfloat16)


def place_kernel(owned, *refs):
    *notes, place_ref = refs
    first = lax.axis_index("expert") * owned
    rows = place_ref.shape[1]
    experts = (first + lax.broadcasted_iota(jnp.int32, (owned, TOK), 0)).astype(jnp.float32)
    earlier = (
        lax.broadcasted_iota(jnp.int32, (TOK, TOK), 0)
        < lax.broadcasted_iota(jnp.int32, (TOK, TOK), 1)
    ).astype(jnp.float32)
    row = lax.broadcasted_iota(jnp.int32, (rows, owned), 0)
    start = lax.broadcasted_iota(jnp.int32, (rows, owned), 1) * MOST
    spread = ((row >= start) & (row < start + MOST)).astype(jnp.float32)
    wanted = lax.broadcasted_iota(jnp.int32, (rows, TOK), 0)
    for e in range(1, owned):
        wanted -= MOST * (
            lax.broadcasted_iota(jnp.int32, (rows, TOK), 0) >= e * MOST
        ).astype(jnp.int32)
    wanted = wanted.astype(jnp.float32)
    for k, note in enumerate(notes):
        meta = note[...].astype(jnp.float32)
        named = jnp.zeros((owned, TOK), jnp.float32)
        gate = jnp.zeros((owned, TOK), jnp.float32)
        for c in range(TOPK):
            hit = experts == meta[c : c + 1, :]
            named = jnp.where(hit, 1.0, named)
            gate = jnp.where(hit, meta[TOPK + c : TOPK + c + 1, :], gate)
        rank = jnp.dot(named, earlier, preferred_element_type=jnp.float32)
        rank = jnp.where(named > 0.0, rank, -1.0)
        rank = jnp.dot(spread, rank, preferred_element_type=jnp.float32)
        gate = jnp.dot(spread, gate, preferred_element_type=jnp.float32)
        place_ref[k] = jnp.where(rank == wanted, gate, 0.0).astype(jnp.bfloat16)


def grad_kernel(n_expert, other, lanes, place_ref, act_ref, *refs):
    blocks = refs[:n_expert]
    out_ref, weighted_ref, done_ref, out_sem = refs[-4:]
    owned, hid, _ = act_ref.shape
    features = done_ref.shape[2]
    side = lax.rem(lax.axis_index("tensor") + other, lax.axis_size("tensor"))
    column = pl.multiple_of(side * features, 128)
    part = hid // lanes

    def leave(e, lane):
        slot = lax.rem(e, BUFFERS)
        some = slice(lane * part, (lane + 1) * part)
        return pltpu.make_async_copy(
            done_ref.at[slot, some],
            out_ref.at[e, some, pl.ds(column, features)],
            out_sem.at[slot, lane],
        )

    @pl.loop(0, features // 256)
    def _(t):
        wide = pl.ds(pl.multiple_of(t * 256, 256), 256)
        for k in range(n_expert):
            weighted_ref[k, :, wide] = jnp.dot(
                place_ref[k], blocks[k][:, wide], preferred_element_type=jnp.float32
            ).astype(jnp.bfloat16)

    @pl.loop(0, owned)
    def _(e):
        @pl.when(e >= BUFFERS)
        def _():
            for lane in range(lanes):
                leave(e - BUFFERS, lane).wait()

        window = pl.ds(pl.multiple_of(e * 16, 16), ROOM)
        for n in range(0, features, 256):
            right = jnp.concatenate(
                [weighted_ref[k, window, n : n + 256] for k in range(n_expert)], axis=0
            )
            done_ref[lax.rem(e, BUFFERS), :, n : n + 256] = jnp.dot(
                act_ref[e], right, preferred_element_type=jnp.float32
            ).astype(jnp.bfloat16)
        for lane in range(lanes):
            leave(e, lane).start(priority=lane)

    @pl.loop(owned - BUFFERS, owned)
    def _(e):
        for lane in range(lanes):
            leave(e, lane).wait()


def local_by_tokens(sent_grad, head_grad, probs, expert_ids, hidden_act):
    n_expert = lax.axis_size("expert")
    n_tensor = lax.axis_size("tensor")
    owned, _, hid = hidden_act.shape[1:]
    feat_dev = sent_grad.shape[2]
    vmem = pl.BlockSpec(memory_space=pltpu.VMEM)
    anywhere = pl.BlockSpec(memory_space=pl.ANY)

    def small_call(kernel, shapes, operands, name):
        return pl.pallas_call(
            kernel,
            out_shape=[jax.ShapeDtypeStruct(shape, jnp.bfloat16) for shape in shapes],
            in_specs=[vmem] * len(operands),
            out_specs=[vmem] * len(shapes),
            compiler_params=pltpu.CompilerParams(vmem_limit_bytes=8 * 2**20),
            name=name,
        )(*operands)

    def turned(array, axis, by):
        peers = lax.axis_size(axis)
        return lax.ppermute(array, axis, [(i, (i + by) % peers) for i in range(peers)])

    def across(array):
        return {t: turned(array, "tensor", t) for t in range(1, n_tensor)}

    def grad_into(out, blocks, other, lanes):
        operands = [place, act, *blocks]
        in_specs = [vmem] * len(operands)
        aliases = {}
        if out is not None:
            aliases = {len(operands): 0}
            in_specs.append(anywhere)
            operands.append(out)
        return pl.pallas_call(
            functools.partial(grad_kernel, n_expert, other, lanes),
            out_shape=jax.ShapeDtypeStruct((owned, hid, n_tensor * feat_dev), jnp.bfloat16),
            in_specs=in_specs,
            out_specs=anywhere,
            scratch_shapes=[
                pltpu.VMEM((n_expert, place.shape[1], feat_dev), jnp.bfloat16),
                pltpu.VMEM((BUFFERS, hid, feat_dev), jnp.bfloat16),
                pltpu.SemaphoreType.DMA((BUFFERS, lanes)),
            ],
            input_output_aliases=aliases,
            compiler_params=pltpu.CompilerParams(vmem_limit_bytes=24 * 2**20),
            cost_estimate=pl.CostEstimate(
                flops=2 * owned * hid * 256 * feat_dev,
                bytes_accessed=2 * owned * hid * feat_dev,
                transcendentals=0,
            ),
            name="weight_grad",
        )(*operands)

    shifted = passed_along(sent_grad, "pipe", -1)[0]
    kept, notes = small_call(
        notes_kernel,
        [head_grad.shape, (2 * TOPK, TOK)],
        [head_grad, expert_ids[0].T, probs[0].T],
        "notes",
    )
    shifted, kept, notes, act = lax.optimization_barrier((shifted, kept, notes, hidden_act[0]))
    (act,) = small_call(
        functools.partial(turn_kernel, n_expert), [(owned, hid, n_expert * ROOM)], [act], "turn"
    )
    (first,) = small_call(join_kernel, [(TOK, feat_dev)], [shifted, kept], "join")

    notes = [notes] + [turned(notes, "expert", k) for k in range(1, n_expert)]
    blocks = {0: first, 1: turned(first, "expert", 1)}
    beside = {0: across(first)}
    blocks[1], below, act, notes[1:] = lax.optimization_barrier((blocks[1], first, act, notes[1:]))
    for k in range(2, n_expert - 1):
        blocks[k] = turned(blocks[k - 1], "expert", 1)
    blocks[n_expert - 1] = turned(below, "expert", -1)
    for k in range(1, n_expert):
        beside[k] = across(blocks[k])
    (place,) = small_call(
        functools.partial(place_kernel, owned), [(n_expert, 16 * (owned + 1), TOK)], notes, "place"
    )
    out = grad_into(None, [blocks[k] for k in range(n_expert)], 0, 2)
    for t in range(1, n_tensor):
        out = grad_into(out, [beside[k][t] for k in range(n_expert)], n_tensor - t, 1)
    return out[None]


def local(*arrays):
    owned, slot_count = arrays[4].shape[1:3]
    tokens = lax.axis_size("expert") * TOK
    by_tokens = owned <= 16 and tokens <= owned * slot_count
    return (local_by_tokens if by_tokens else local_by_slots)(*arrays)


def solution(mesh):
    in_specs = (
        P("pipe", "expert", "tensor"),
        P("expert", "tensor"),
        P("pipe", "expert", None),
        P("pipe", "expert", None),
        P("pipe", "expert", None, "tensor"),
    )
    out_specs = P("pipe", "expert", "tensor", None)
    return jax.shard_map(local, mesh=mesh, in_specs=in_specs, out_specs=out_specs, check_vma=False)
```

```python
import functools

import jax
import jax.numpy as jnp
from jax import lax
from jax.experimental import pallas as pl
from jax.experimental.pallas import tpu as pltpu
from jax.sharding import PartitionSpec as P

EXPERTS = 64
TOPK = 8
TOK = 128
MOST = 17
ROOM = 32
BUFFERS = 4


def passed_along(array, axis, by):
    peers = lax.axis_size(axis)
    pairs = [(i, i + by) for i in range(peers) if 0 <= i + by < peers]
    return lax.ppermute(array, axis, pairs)


def slot_ranks(pair_ids):
    onehot = (pair_ids[:, :, None] == jnp.arange(EXPERTS, dtype=jnp.int32)[None, None, :]).astype(
        jnp.int32
    )
    before = jnp.cumsum(onehot, axis=1) - onehot
    return jnp.sum(before * onehot, axis=2)


def place_rows(targets, capacity, source_rows, gate_values):
    pair_count = targets.shape[0]
    owner_pair = (
        jnp.full((capacity,), pair_count, jnp.int32)
        .at[targets]
        .set(jnp.arange(pair_count, dtype=jnp.int32), mode="drop")
    )
    filled = owner_pair < pair_count
    safe_pair = jnp.minimum(owner_pair, pair_count - 1)
    placed = jnp.where(
        filled[:, None], source_rows[safe_pair // TOPK], jnp.zeros((), source_rows.dtype)
    )
    placed_gate = jnp.where(
        filled, gate_values.reshape(-1)[safe_pair], jnp.zeros((), gate_values.dtype)
    )
    return (placed, placed_gate)


def arriving(sent_grad, head_grad):
    shifted = passed_along(sent_grad, "pipe", -1)
    is_last = lax.axis_index("pipe") == lax.axis_size("pipe") - 1
    return jnp.where(is_last, head_grad, shifted[0])


def local_by_slots(sent_grad, head_grad, probs, expert_ids, hidden_act):
    incoming = arriving(sent_grad, head_grad)
    feat_dev = incoming.shape[1]
    local_ids = expert_ids[0].reshape(1, TOK * TOPK)
    local_targets = (local_ids * MOST + slot_ranks(local_ids)).reshape(-1)
    send_rows, send_gate = place_rows(local_targets, EXPERTS * MOST, incoming, probs[0])
    recv_rows, recv_gate = (
        lax.all_to_all(
            send_rows.reshape(EXPERTS, MOST, feat_dev),
            "expert",
            split_axis=0,
            concat_axis=1,
            tiled=True,
        ),
        lax.all_to_all(
            send_gate.reshape(EXPERTS, MOST), "expert", split_axis=0, concat_axis=1, tiled=True
        ),
    )
    gate_wide = recv_gate.astype(jnp.float32)[:, :, None]
    full_rows = lax.all_gather(recv_rows, "tensor", axis=2, tiled=True)
    weighted = (full_rows.astype(jnp.float32) * gate_wide).astype(jnp.bfloat16)
    weight_grad = jnp.einsum(
        "esh,esd->ehd", hidden_act[0], weighted, preferred_element_type=jnp.float32
    ).astype(jnp.bfloat16)
    return weight_grad[None]


def notes_kernel(head_ref, ids_ref, probs_ref, kept_ref, notes_ref):
    kept_ref[...] = head_ref[...]
    notes_ref[...] = jnp.concatenate(
        [ids_ref[...].astype(jnp.float32), probs_ref[...].astype(jnp.float32)], axis=0
    ).astype(jnp.bfloat16)


def join_kernel(shifted_ref, head_ref, rows_ref):
    is_last = lax.axis_index("pipe") == lax.axis_size("pipe") - 1
    rows_ref[...] = jnp.where(is_last, head_ref[...], shifted_ref[...])


def turn_kernel(n_expert, act_ref, turned_ref):
    owned, slot_count, _ = act_ref.shape
    me = lax.axis_index("expert")
    slot = lax.broadcasted_iota(jnp.int32, (slot_count, n_expert * ROOM), 0)
    spot = lax.broadcasted_iota(jnp.int32, (slot_count, n_expert * ROOM), 1)
    block = jnp.zeros_like(slot)
    for b in range(1, n_expert):
        block += (slot >= b * MOST).astype(jnp.int32)
    back = me - block
    back = jnp.where(back < 0, back + n_expert, back)
    target = back * ROOM + slot - block * MOST
    for e in range(owned):
        turned_ref[e] = lax.dot_general(
            act_ref[e],
            (spot == target + e).astype(jnp.bfloat16),
            (((0,), (0,)), ((), ())),
            preferred_element_type=jnp.float32,
        ).astype(jnp.bfloat16)


def place_kernel(owned, *refs):
    *notes, place_ref = refs
    first = lax.axis_index("expert") * owned
    rows = place_ref.shape[1]
    experts = (first + lax.broadcasted_iota(jnp.int32, (owned, TOK), 0)).astype(jnp.float32)
    earlier = (
        lax.broadcasted_iota(jnp.int32, (TOK, TOK), 0)
        < lax.broadcasted_iota(jnp.int32, (TOK, TOK), 1)
    ).astype(jnp.float32)
    row = lax.broadcasted_iota(jnp.int32, (rows, owned), 0)
    start = lax.broadcasted_iota(jnp.int32, (rows, owned), 1) * MOST
    spread = ((row >= start) & (row < start + MOST)).astype(jnp.float32)
    wanted = lax.broadcasted_iota(jnp.int32, (rows, TOK), 0)
    for e in range(1, owned):
        wanted -= MOST * (
            lax.broadcasted_iota(jnp.int32, (rows, TOK), 0) >= e * MOST
        ).astype(jnp.int32)
    wanted = wanted.astype(jnp.float32)
    for k, note in enumerate(notes):
        meta = note[...].astype(jnp.float32)
        named = jnp.zeros((owned, TOK), jnp.float32)
        gate = jnp.zeros((owned, TOK), jnp.float32)
        for c in range(TOPK):
            hit = experts == meta[c : c + 1, :]
            named = jnp.where(hit, 1.0, named)
            gate = jnp.where(hit, meta[TOPK + c : TOPK + c + 1, :], gate)
        rank = jnp.dot(named, earlier, preferred_element_type=jnp.float32)
        rank = jnp.where(named > 0.0, rank, -1.0)
        rank = jnp.dot(spread, rank, preferred_element_type=jnp.float32)
        gate = jnp.dot(spread, gate, preferred_element_type=jnp.float32)
        place_ref[k] = jnp.where(rank == wanted, gate, 0.0).astype(jnp.bfloat16)


def grad_kernel(n_expert, other, breadth, place_ref, act_ref, *refs):
    blocks = refs[:n_expert]
    out_ref, weighted_ref, done_ref, out_sem = refs[-4:]
    owned, hid, _ = act_ref.shape
    features = done_ref.shape[2]
    side = lax.rem(lax.axis_index("tensor") + other, lax.axis_size("tensor"))
    column = pl.multiple_of(side * features, 128)

    def leave(e):
        slot = lax.rem(e, BUFFERS)
        return pltpu.make_async_copy(
            done_ref.at[slot], out_ref.at[e, :, pl.ds(column, features)], out_sem.at[slot]
        )

    @pl.loop(0, features // 256)
    def _(t):
        wide = pl.ds(pl.multiple_of(t * 256, 256), 256)
        for k in range(n_expert):
            weighted_ref[k, :, wide] = jnp.dot(
                place_ref[k], blocks[k][:, wide], preferred_element_type=jnp.float32
            ).astype(jnp.bfloat16)

    @pl.loop(0, owned)
    def _(e):
        @pl.when(e >= BUFFERS)
        def _():
            leave(e - BUFFERS).wait()

        window = pl.ds(pl.multiple_of(e * 16, 16), ROOM)
        for n in range(0, features, breadth):
            wide = slice(n, min(n + breadth, features))
            right = jnp.concatenate(
                [weighted_ref[k, window, wide] for k in range(n_expert)], axis=0
            )
            done_ref[lax.rem(e, BUFFERS), :, wide] = jnp.dot(
                act_ref[e], right, preferred_element_type=jnp.float32
            ).astype(jnp.bfloat16)
        leave(e).start()

    @pl.loop(owned - BUFFERS, owned)
    def _(e):
        leave(e).wait()


def local_by_tokens(sent_grad, head_grad, probs, expert_ids, hidden_act):
    n_expert = lax.axis_size("expert")
    n_tensor = lax.axis_size("tensor")
    owned, _, hid = hidden_act.shape[1:]
    feat_dev = sent_grad.shape[2]
    vmem = pl.BlockSpec(memory_space=pltpu.VMEM)
    anywhere = pl.BlockSpec(memory_space=pl.ANY)

    def small_call(kernel, shapes, operands, name):
        return pl.pallas_call(
            kernel,
            out_shape=[jax.ShapeDtypeStruct(shape, jnp.bfloat16) for shape in shapes],
            in_specs=[vmem] * len(operands),
            out_specs=[vmem] * len(shapes),
            compiler_params=pltpu.CompilerParams(vmem_limit_bytes=8 * 2**20),
            name=name,
        )(*operands)

    def turned(array, axis, by):
        peers = lax.axis_size(axis)
        return lax.ppermute(array, axis, [(i, (i + by) % peers) for i in range(peers)])

    def across(array):
        return {t: turned(array, "tensor", t) for t in range(1, n_tensor)}

    def grad_into(out, blocks, other, breadth):
        operands = [place, act, *blocks]
        in_specs = [vmem] * len(operands)
        aliases = {}
        if out is not None:
            aliases = {len(operands): 0}
            in_specs.append(anywhere)
            operands.append(out)
        return pl.pallas_call(
            functools.partial(grad_kernel, n_expert, other, breadth),
            out_shape=jax.ShapeDtypeStruct((owned, hid, n_tensor * feat_dev), jnp.bfloat16),
            in_specs=in_specs,
            out_specs=anywhere,
            scratch_shapes=[
                pltpu.VMEM((n_expert, place.shape[1], feat_dev), jnp.bfloat16),
                pltpu.VMEM((BUFFERS, hid, feat_dev), jnp.bfloat16),
                pltpu.SemaphoreType.DMA((BUFFERS,)),
            ],
            input_output_aliases=aliases,
            compiler_params=pltpu.CompilerParams(vmem_limit_bytes=24 * 2**20),
            cost_estimate=pl.CostEstimate(
                flops=2 * owned * hid * 256 * feat_dev,
                bytes_accessed=2 * owned * hid * feat_dev,
                transcendentals=0,
            ),
            name="weight_grad",
        )(*operands)

    shifted = passed_along(sent_grad, "pipe", -1)[0]
    kept, notes = small_call(
        notes_kernel,
        [head_grad.shape, (2 * TOPK, TOK)],
        [head_grad, expert_ids[0].T, probs[0].T],
        "notes",
    )
    notes = [notes] + [turned(notes, "expert", k) for k in range(1, n_expert)]
    shifted, kept, notes, act = lax.optimization_barrier((shifted, kept, notes, hidden_act[0]))
    (act,) = small_call(
        functools.partial(turn_kernel, n_expert), [(owned, hid, n_expert * ROOM)], [act], "turn"
    )
    (first,) = small_call(join_kernel, [(TOK, feat_dev)], [shifted, kept], "join")

    blocks = {0: first, 1: turned(first, "expert", 1)}
    beside = {0: across(first)}
    blocks[1], below, act, beside[0] = lax.optimization_barrier((blocks[1], first, act, beside[0]))
    for k in range(2, n_expert - 1):
        blocks[k] = turned(blocks[k - 1], "expert", 1)
    blocks[n_expert - 1] = turned(below, "expert", -1)
    for k in range(1, n_expert):
        beside[k] = across(blocks[k])
    (place,) = small_call(
        functools.partial(place_kernel, owned), [(n_expert, 16 * (owned + 1), TOK)], notes, "place"
    )
    out = grad_into(None, [blocks[k] for k in range(n_expert)], 0, 512)
    for t in range(1, n_tensor):
        out = grad_into(out, [beside[k][t] for k in range(n_expert)], n_tensor - t, feat_dev)
    return out[None]


def local(*arrays):
    owned, slot_count = arrays[4].shape[1:3]
    tokens = lax.axis_size("expert") * TOK
    by_tokens = owned <= 16 and tokens <= owned * slot_count
    return (local_by_tokens if by_tokens else local_by_slots)(*arrays)


def solution(mesh):
    in_specs = (
        P("pipe", "expert", "tensor"),
        P("expert", "tensor"),
        P("pipe", "expert", None),
        P("pipe", "expert", None),
        P("pipe", "expert", None, "tensor"),
    )
    out_specs = P("pipe", "expert", "tensor", None)
    return jax.shard_map(local, mesh=mesh, in_specs=in_specs, out_specs=out_specs, check_vma=False)
```

```python
import functools
import itertools

import jax
import jax.numpy as jnp
from jax import lax
from jax.experimental import pallas as pl
from jax.experimental.pallas import tpu as pltpu
from jax.sharding import PartitionSpec as P

EXPERTS = 64
TOPK = 8
TOK = 128
MOST = 17
ROOM = 32
BUFFERS = 4


def passed_along(array, axis, by):
    peers = lax.axis_size(axis)
    pairs = [(i, i + by) for i in range(peers) if 0 <= i + by < peers]
    return lax.ppermute(array, axis, pairs)


def slot_ranks(pair_ids):
    onehot = (pair_ids[:, :, None] == jnp.arange(EXPERTS, dtype=jnp.int32)[None, None, :]).astype(
        jnp.int32
    )
    before = jnp.cumsum(onehot, axis=1) - onehot
    return jnp.sum(before * onehot, axis=2)


def place_rows(targets, capacity, source_rows, gate_values):
    pair_count = targets.shape[0]
    owner_pair = (
        jnp.full((capacity,), pair_count, jnp.int32)
        .at[targets]
        .set(jnp.arange(pair_count, dtype=jnp.int32), mode="drop")
    )
    filled = owner_pair < pair_count
    safe_pair = jnp.minimum(owner_pair, pair_count - 1)
    placed = jnp.where(
        filled[:, None], source_rows[safe_pair // TOPK], jnp.zeros((), source_rows.dtype)
    )
    placed_gate = jnp.where(
        filled, gate_values.reshape(-1)[safe_pair], jnp.zeros((), gate_values.dtype)
    )
    return (placed, placed_gate)


def arriving(sent_grad, head_grad):
    shifted = passed_along(sent_grad, "pipe", -1)
    is_last = lax.axis_index("pipe") == lax.axis_size("pipe") - 1
    return jnp.where(is_last, head_grad, shifted[0])


def local_by_slots(sent_grad, head_grad, probs, expert_ids, hidden_act):
    incoming = arriving(sent_grad, head_grad)
    feat_dev = incoming.shape[1]
    local_ids = expert_ids[0].reshape(1, TOK * TOPK)
    local_targets = (local_ids * MOST + slot_ranks(local_ids)).reshape(-1)
    send_rows, send_gate = place_rows(local_targets, EXPERTS * MOST, incoming, probs[0])
    recv_rows, recv_gate = (
        lax.all_to_all(
            send_rows.reshape(EXPERTS, MOST, feat_dev),
            "expert",
            split_axis=0,
            concat_axis=1,
            tiled=True,
        ),
        lax.all_to_all(
            send_gate.reshape(EXPERTS, MOST), "expert", split_axis=0, concat_axis=1, tiled=True
        ),
    )
    gate_wide = recv_gate.astype(jnp.float32)[:, :, None]
    full_rows = lax.all_gather(recv_rows, "tensor", axis=2, tiled=True)
    weighted = (full_rows.astype(jnp.float32) * gate_wide).astype(jnp.bfloat16)
    weight_grad = jnp.einsum(
        "esh,esd->ehd", hidden_act[0], weighted, preferred_element_type=jnp.float32
    ).astype(jnp.bfloat16)
    return weight_grad[None]


def notes_kernel(ids_ref, probs_ref, notes_ref):
    notes_ref[...] = jnp.concatenate(
        [ids_ref[...].astype(jnp.float32), probs_ref[...].astype(jnp.float32)], axis=0
    ).astype(jnp.bfloat16)


def turn_kernel(n_expert, act_ref, turned_ref):
    owned, slot_count, _ = act_ref.shape
    me = lax.axis_index("expert")
    slot = lax.broadcasted_iota(jnp.int32, (slot_count, n_expert * ROOM), 0)
    spot = lax.broadcasted_iota(jnp.int32, (slot_count, n_expert * ROOM), 1)
    block = jnp.zeros_like(slot)
    for b in range(1, n_expert):
        block += (slot >= b * MOST).astype(jnp.int32)
    back = me - block
    back = jnp.where(back < 0, back + n_expert, back)
    target = back * ROOM + slot - block * MOST
    for e in range(owned):
        turned_ref[e] = lax.dot_general(
            act_ref[e],
            (spot == target + e).astype(jnp.bfloat16),
            (((0,), (0,)), ((), ())),
            preferred_element_type=jnp.float32,
        ).astype(jnp.bfloat16)


def place_kernel(owned, *refs):
    *notes, place_ref = refs
    first = lax.axis_index("expert") * owned
    rows = place_ref.shape[1]
    experts = (first + lax.broadcasted_iota(jnp.int32, (owned, TOK), 0)).astype(jnp.float32)
    earlier = (
        lax.broadcasted_iota(jnp.int32, (TOK, TOK), 0)
        < lax.broadcasted_iota(jnp.int32, (TOK, TOK), 1)
    ).astype(jnp.float32)
    row = lax.broadcasted_iota(jnp.int32, (rows, owned), 0)
    start = lax.broadcasted_iota(jnp.int32, (rows, owned), 1) * MOST
    spread = ((row >= start) & (row < start + MOST)).astype(jnp.float32)
    wanted = lax.broadcasted_iota(jnp.int32, (rows, TOK), 0)
    for e in range(1, owned):
        wanted -= MOST * (
            lax.broadcasted_iota(jnp.int32, (rows, TOK), 0) >= e * MOST
        ).astype(jnp.int32)
    wanted = wanted.astype(jnp.float32)
    for k, note in enumerate(notes):
        meta = note[...].astype(jnp.float32)
        named = jnp.zeros((owned, TOK), jnp.float32)
        gate = jnp.zeros((owned, TOK), jnp.float32)
        for c in range(TOPK):
            hit = experts == meta[c : c + 1, :]
            named = jnp.where(hit, 1.0, named)
            gate = jnp.where(hit, meta[TOPK + c : TOPK + c + 1, :], gate)
        rank = jnp.dot(named, earlier, preferred_element_type=jnp.float32)
        rank = jnp.where(named > 0.0, rank, -1.0)
        rank = jnp.dot(spread, rank, preferred_element_type=jnp.float32)
        gate = jnp.dot(spread, gate, preferred_element_type=jnp.float32)
        place_ref[k] = jnp.where(rank == wanted, gate, 0.0).astype(jnp.bfloat16)


def grad_kernel(n_expert, other, place_ref, act_ref, *refs):
    blocks = refs[:n_expert]
    out_ref, weighted_ref, done_ref, out_sem = refs[-4:]
    owned, hid, _ = act_ref.shape
    features = done_ref.shape[2]
    side = lax.rem(lax.axis_index("tensor") + other, lax.axis_size("tensor"))
    column = pl.multiple_of(side * features, 128)

    def leave(e):
        slot = lax.rem(e, BUFFERS)
        return pltpu.make_async_copy(
            done_ref.at[slot], out_ref.at[e, :, pl.ds(column, features)], out_sem.at[slot]
        )

    @pl.loop(0, features // 256)
    def _(t):
        wide = pl.ds(pl.multiple_of(t * 256, 256), 256)
        for k in range(n_expert):
            weighted_ref[k, :, wide] = jnp.dot(
                place_ref[k], blocks[k][:, wide], preferred_element_type=jnp.float32
            ).astype(jnp.bfloat16)

    @pl.loop(0, owned)
    def _(e):
        @pl.when(e >= BUFFERS)
        def _():
            leave(e - BUFFERS).wait()

        window = pl.ds(pl.multiple_of(e * 16, 16), ROOM)
        for n in range(0, features, 256):
            wide = slice(n, min(n + 256, features))
            right = jnp.concatenate(
                [weighted_ref[k, window, wide] for k in range(n_expert)], axis=0
            )
            done_ref[lax.rem(e, BUFFERS), :, wide] = jnp.dot(
                act_ref[e], right, preferred_element_type=jnp.float32
            ).astype(jnp.bfloat16)
        leave(e).start()

    @pl.loop(owned - BUFFERS, owned)
    def _(e):
        leave(e).wait()


def local_by_tokens(sent_grad, head_grad, probs, expert_ids, hidden_act):
    n_expert = lax.axis_size("expert")
    n_tensor = lax.axis_size("tensor")
    owned, _, hid = hidden_act.shape[1:]
    feat_dev = sent_grad.shape[2]
    vmem = pl.BlockSpec(memory_space=pltpu.VMEM)
    anywhere = pl.BlockSpec(memory_space=pl.ANY)

    def small_call(kernel, shapes, operands, name):
        return pl.pallas_call(
            kernel,
            out_shape=[jax.ShapeDtypeStruct(shape, jnp.bfloat16) for shape in shapes],
            in_specs=[vmem] * len(operands),
            out_specs=[vmem] * len(shapes),
            compiler_params=pltpu.CompilerParams(vmem_limit_bytes=8 * 2**20),
            name=name,
        )(*operands)

    def turned(array, pipe=0, expert=0, tensor=0):
        axes = ("pipe", "expert", "tensor")
        sizes = [lax.axis_size(axis) for axis in axes]
        steps = (pipe, expert, tensor)

        def rank(place):
            return (place[0] * sizes[1] + place[1]) * sizes[2] + place[2]

        pairs = []
        for place in itertools.product(*map(range, sizes)):
            target = [(i + by) % size for i, by, size in zip(place, steps, sizes)]
            pairs.append((rank(place), rank(target)))
        return lax.ppermute(array, axes, pairs)

    def grad_into(out, blocks, other):
        operands = [place, act, *blocks]
        in_specs = [vmem] * len(operands)
        aliases = {}
        if out is not None:
            aliases = {len(operands): 0}
            in_specs.append(anywhere)
            operands.append(out)
        return pl.pallas_call(
            functools.partial(grad_kernel, n_expert, other),
            out_shape=jax.ShapeDtypeStruct((owned, hid, n_tensor * feat_dev), jnp.bfloat16),
            in_specs=in_specs,
            out_specs=anywhere,
            scratch_shapes=[
                pltpu.VMEM((n_expert, place.shape[1], feat_dev), jnp.bfloat16),
                pltpu.VMEM((BUFFERS, hid, feat_dev), jnp.bfloat16),
                pltpu.SemaphoreType.DMA((BUFFERS,)),
            ],
            input_output_aliases=aliases,
            compiler_params=pltpu.CompilerParams(vmem_limit_bytes=24 * 2**20),
            cost_estimate=pl.CostEstimate(
                flops=2 * owned * hid * 256 * feat_dev,
                bytes_accessed=2 * owned * hid * feat_dev,
                transcendentals=0,
            ),
            name="weight_grad",
        )(*operands)

    payload = jnp.where(lax.axis_index("pipe") == 0, head_grad, sent_grad[0])
    blocks = {1: turned(payload, -1, 1)}
    beside = {0: {t: turned(payload, -1, 0, t) for t in range(1, n_tensor)}}
    (notes,) = small_call(
        notes_kernel, [(2 * TOPK, TOK)], [expert_ids[0].T, probs[0].T], "notes"
    )
    notes = [notes] + [turned(notes, 0, k) for k in range(1, n_expert)]
    (act,) = small_call(
        functools.partial(turn_kernel, n_expert),
        [(owned, hid, n_expert * ROOM)],
        [hidden_act[0]],
        "turn",
    )
    beside[0], payload, act, notes[1:] = lax.optimization_barrier(
        (beside[0], payload, act, notes[1:])
    )
    blocks[n_expert - 1] = turned(payload, -1, -1)
    blocks[0] = turned(payload, -1)
    for k in range(2, n_expert - 1):
        blocks[k] = turned(blocks[k - 1], 0, 1)
    for k in range(1, n_expert):
        beside[k] = {t: turned(blocks[k], 0, 0, t) for t in range(1, n_tensor)}
    (place,) = small_call(
        functools.partial(place_kernel, owned), [(n_expert, 16 * (owned + 1), TOK)], notes, "place"
    )
    out = grad_into(None, [blocks[k] for k in range(n_expert)], 0)
    for t in range(1, n_tensor):
        out = grad_into(out, [beside[k][t] for k in range(n_expert)], n_tensor - t)
    return out[None]


def local(*arrays):
    owned, slot_count = arrays[4].shape[1:3]
    tokens = lax.axis_size("expert") * TOK
    by_tokens = owned <= 16 and tokens <= owned * slot_count
    return (local_by_tokens if by_tokens else local_by_slots)(*arrays)


def solution(mesh):
    in_specs = (
        P("pipe", "expert", "tensor"),
        P("expert", "tensor"),
        P("pipe", "expert", None),
        P("pipe", "expert", None),
        P("pipe", "expert", None, "tensor"),
    )
    out_specs = P("pipe", "expert", "tensor", None)
    return jax.shard_map(local, mesh=mesh, in_specs=in_specs, out_specs=out_specs, check_vma=False)
```

```python
import functools
import itertools

import jax
import jax.numpy as jnp
from jax import lax
from jax.experimental import pallas as pl
from jax.experimental.pallas import tpu as pltpu
from jax.sharding import PartitionSpec as P

EXPERTS = 64
TOPK = 8
TOK = 128
MOST = 17
ROOM = 32
BUFFERS = 4


def passed_along(array, axis, by):
    peers = lax.axis_size(axis)
    pairs = [(i, i + by) for i in range(peers) if 0 <= i + by < peers]
    return lax.ppermute(array, axis, pairs)


def slot_ranks(pair_ids):
    onehot = (pair_ids[:, :, None] == jnp.arange(EXPERTS, dtype=jnp.int32)[None, None, :]).astype(
        jnp.int32
    )
    before = jnp.cumsum(onehot, axis=1) - onehot
    return jnp.sum(before * onehot, axis=2)


def place_rows(targets, capacity, source_rows, gate_values):
    pair_count = targets.shape[0]
    owner_pair = (
        jnp.full((capacity,), pair_count, jnp.int32)
        .at[targets]
        .set(jnp.arange(pair_count, dtype=jnp.int32), mode="drop")
    )
    filled = owner_pair < pair_count
    safe_pair = jnp.minimum(owner_pair, pair_count - 1)
    placed = jnp.where(
        filled[:, None], source_rows[safe_pair // TOPK], jnp.zeros((), source_rows.dtype)
    )
    placed_gate = jnp.where(
        filled, gate_values.reshape(-1)[safe_pair], jnp.zeros((), gate_values.dtype)
    )
    return (placed, placed_gate)


def arriving(sent_grad, head_grad):
    shifted = passed_along(sent_grad, "pipe", -1)
    is_last = lax.axis_index("pipe") == lax.axis_size("pipe") - 1
    return jnp.where(is_last, head_grad, shifted[0])


def local_by_slots(sent_grad, head_grad, probs, expert_ids, hidden_act):
    incoming = arriving(sent_grad, head_grad)
    feat_dev = incoming.shape[1]
    local_ids = expert_ids[0].reshape(1, TOK * TOPK)
    local_targets = (local_ids * MOST + slot_ranks(local_ids)).reshape(-1)
    send_rows, send_gate = place_rows(local_targets, EXPERTS * MOST, incoming, probs[0])
    recv_rows, recv_gate = (
        lax.all_to_all(
            send_rows.reshape(EXPERTS, MOST, feat_dev),
            "expert",
            split_axis=0,
            concat_axis=1,
            tiled=True,
        ),
        lax.all_to_all(
            send_gate.reshape(EXPERTS, MOST), "expert", split_axis=0, concat_axis=1, tiled=True
        ),
    )
    gate_wide = recv_gate.astype(jnp.float32)[:, :, None]
    full_rows = lax.all_gather(recv_rows, "tensor", axis=2, tiled=True)
    weighted = (full_rows.astype(jnp.float32) * gate_wide).astype(jnp.bfloat16)
    weight_grad = jnp.einsum(
        "esh,esd->ehd", hidden_act[0], weighted, preferred_element_type=jnp.float32
    ).astype(jnp.bfloat16)
    return weight_grad[None]


def notes_kernel(ids_ref, probs_ref, notes_ref):
    notes_ref[...] = jnp.concatenate(
        [ids_ref[...].astype(jnp.float32), probs_ref[...].astype(jnp.float32)], axis=0
    ).astype(jnp.bfloat16)


def turn_kernel(n_expert, act_ref, turned_ref):
    owned, slot_count, _ = act_ref.shape
    me = lax.axis_index("expert")
    slot = lax.broadcasted_iota(jnp.int32, (slot_count, n_expert * ROOM), 0)
    spot = lax.broadcasted_iota(jnp.int32, (slot_count, n_expert * ROOM), 1)
    block = jnp.zeros_like(slot)
    for b in range(1, n_expert):
        block += (slot >= b * MOST).astype(jnp.int32)
    back = me - block
    back = jnp.where(back < 0, back + n_expert, back)
    target = back * ROOM + slot - block * MOST
    for e in range(owned):
        turned_ref[e] = lax.dot_general(
            act_ref[e],
            (spot == target + e).astype(jnp.bfloat16),
            (((0,), (0,)), ((), ())),
            preferred_element_type=jnp.float32,
        ).astype(jnp.bfloat16)


def place_kernel(owned, *refs):
    *notes, place_ref = refs
    first = lax.axis_index("expert") * owned
    rows = place_ref.shape[1]
    experts = (first + lax.broadcasted_iota(jnp.int32, (owned, TOK), 0)).astype(jnp.float32)
    earlier = (
        lax.broadcasted_iota(jnp.int32, (TOK, TOK), 0)
        < lax.broadcasted_iota(jnp.int32, (TOK, TOK), 1)
    ).astype(jnp.float32)
    row = lax.broadcasted_iota(jnp.int32, (rows, owned), 0)
    start = lax.broadcasted_iota(jnp.int32, (rows, owned), 1) * MOST
    spread = ((row >= start) & (row < start + MOST)).astype(jnp.float32)
    wanted = lax.broadcasted_iota(jnp.int32, (rows, TOK), 0)
    for e in range(1, owned):
        wanted -= MOST * (
            lax.broadcasted_iota(jnp.int32, (rows, TOK), 0) >= e * MOST
        ).astype(jnp.int32)
    wanted = wanted.astype(jnp.float32)
    for k, note in enumerate(notes):
        meta = note[...].astype(jnp.float32)
        named = jnp.zeros((owned, TOK), jnp.float32)
        gate = jnp.zeros((owned, TOK), jnp.float32)
        for c in range(TOPK):
            hit = experts == meta[c : c + 1, :]
            named = jnp.where(hit, 1.0, named)
            gate = jnp.where(hit, meta[TOPK + c : TOPK + c + 1, :], gate)
        rank = jnp.dot(named, earlier, preferred_element_type=jnp.float32)
        rank = jnp.where(named > 0.0, rank, -1.0)
        rank = jnp.dot(spread, rank, preferred_element_type=jnp.float32)
        gate = jnp.dot(spread, gate, preferred_element_type=jnp.float32)
        place_ref[k] = jnp.where(rank == wanted, gate, 0.0).astype(jnp.bfloat16)


def grad_kernel(n_expert, other, place_ref, act_ref, *refs):
    blocks = refs[:n_expert]
    out_ref, weighted_ref, done_ref, out_sem = refs[-4:]
    owned, hid, _ = act_ref.shape
    features = done_ref.shape[2]
    side = lax.rem(lax.axis_index("tensor") + other, lax.axis_size("tensor"))
    column = pl.multiple_of(side * features, 128)

    def leave(e):
        slot = lax.rem(e, BUFFERS)
        return pltpu.make_async_copy(
            done_ref.at[slot], out_ref.at[e, :, pl.ds(column, features)], out_sem.at[slot]
        )

    @pl.loop(0, features // 256)
    def _(t):
        wide = pl.ds(pl.multiple_of(t * 256, 256), 256)
        for k in range(n_expert):
            weighted_ref[k, :, wide] = jnp.dot(
                place_ref[k], blocks[k][:, wide], preferred_element_type=jnp.float32
            ).astype(jnp.bfloat16)

    @pl.loop(0, owned)
    def _(e):
        @pl.when(e >= BUFFERS)
        def _():
            leave(e - BUFFERS).wait()

        window = pl.ds(pl.multiple_of(e * 16, 16), ROOM)
        for n in range(0, features, 256):
            wide = slice(n, min(n + 256, features))
            right = jnp.concatenate(
                [weighted_ref[k, window, wide] for k in range(n_expert)], axis=0
            )
            done_ref[lax.rem(e, BUFFERS), :, wide] = jnp.dot(
                act_ref[e], right, preferred_element_type=jnp.float32
            ).astype(jnp.bfloat16)
        leave(e).start()

    @pl.loop(owned - BUFFERS, owned)
    def _(e):
        leave(e).wait()


def local_by_tokens(sent_grad, head_grad, probs, expert_ids, hidden_act):
    n_expert = lax.axis_size("expert")
    n_tensor = lax.axis_size("tensor")
    owned, _, hid = hidden_act.shape[1:]
    feat_dev = sent_grad.shape[2]
    vmem = pl.BlockSpec(memory_space=pltpu.VMEM)
    anywhere = pl.BlockSpec(memory_space=pl.ANY)

    def small_call(kernel, shapes, operands, name):
        return pl.pallas_call(
            kernel,
            out_shape=[jax.ShapeDtypeStruct(shape, jnp.bfloat16) for shape in shapes],
            in_specs=[vmem] * len(operands),
            out_specs=[vmem] * len(shapes),
            compiler_params=pltpu.CompilerParams(vmem_limit_bytes=8 * 2**20),
            name=name,
        )(*operands)

    def turned(array, pipe=0, expert=0, tensor=0):
        axes = ("pipe", "expert", "tensor")
        sizes = [lax.axis_size(axis) for axis in axes]
        steps = (pipe, expert, tensor)

        def rank(place):
            return (place[0] * sizes[1] + place[1]) * sizes[2] + place[2]

        pairs = []
        for place in itertools.product(*map(range, sizes)):
            target = [(i + by) % size for i, by, size in zip(place, steps, sizes)]
            pairs.append((rank(place), rank(target)))
        return lax.ppermute(array, axes, pairs)

    def grad_into(out, blocks, other):
        operands = [place, act, *blocks]
        in_specs = [vmem] * len(operands)
        aliases = {}
        if out is not None:
            aliases = {len(operands): 0}
            in_specs.append(anywhere)
            operands.append(out)
        return pl.pallas_call(
            functools.partial(grad_kernel, n_expert, other),
            out_shape=jax.ShapeDtypeStruct((owned, hid, n_tensor * feat_dev), jnp.bfloat16),
            in_specs=in_specs,
            out_specs=anywhere,
            scratch_shapes=[
                pltpu.VMEM((n_expert, place.shape[1], feat_dev), jnp.bfloat16),
                pltpu.VMEM((BUFFERS, hid, feat_dev), jnp.bfloat16),
                pltpu.SemaphoreType.DMA((BUFFERS,)),
            ],
            input_output_aliases=aliases,
            compiler_params=pltpu.CompilerParams(vmem_limit_bytes=24 * 2**20),
            cost_estimate=pl.CostEstimate(
                flops=2 * owned * hid * 256 * feat_dev,
                bytes_accessed=2 * owned * hid * feat_dev,
                transcendentals=0,
            ),
            name="weight_grad",
        )(*operands)

    payload = jnp.where(lax.axis_index("pipe") == 0, head_grad, sent_grad[0])
    (notes,) = small_call(
        notes_kernel, [(2 * TOPK, TOK)], [expert_ids[0].T, probs[0].T], "notes"
    )
    (act,) = small_call(
        functools.partial(turn_kernel, n_expert),
        [(owned, hid, n_expert * ROOM)],
        [hidden_act[0]],
        "turn",
    )
    last = n_expert - 1
    blocks = {1: turned(payload, -1, 1), last: turned(payload, -1, -1)}
    notes = {0: notes, 1: turned(notes, 0, 1), last: turned(notes, 0, -1)}
    beside = {0: {t: turned(payload, -1, 0, t) for t in range(1, n_tensor)}}
    beside[1] = {t: turned(blocks[1], 0, 0, t) for t in range(1, n_tensor)}
    blocks, notes, beside[0], payload, act = lax.optimization_barrier(
        (blocks, notes, beside[0], payload, act)
    )
    for k in range(2, last):
        blocks[k] = turned(blocks[k - 1], 0, 1)
        notes[k] = turned(notes[k - 1], 0, 1)
    blocks[0] = turned(payload, -1)
    for k in range(2, n_expert):
        beside[k] = {t: turned(blocks[k], 0, 0, t) for t in range(1, n_tensor)}
    (place,) = small_call(
        functools.partial(place_kernel, owned),
        [(n_expert, 16 * (owned + 1), TOK)],
        [notes[k] for k in range(n_expert)],
        "place",
    )
    out = grad_into(None, [blocks[k] for k in range(n_expert)], 0)
    for t in range(1, n_tensor):
        out = grad_into(out, [beside[k][t] for k in range(n_expert)], n_tensor - t)
    return out[None]


def local(*arrays):
    owned, slot_count = arrays[4].shape[1:3]
    tokens = lax.axis_size("expert") * TOK
    by_tokens = owned <= 16 and tokens <= owned * slot_count
    return (local_by_tokens if by_tokens else local_by_slots)(*arrays)


def solution(mesh):
    in_specs = (
        P("pipe", "expert", "tensor"),
        P("expert", "tensor"),
        P("pipe", "expert", None),
        P("pipe", "expert", None),
        P("pipe", "expert", None, "tensor"),
    )
    out_specs = P("pipe", "expert", "tensor", None)
    return jax.shard_map(local, mesh=mesh, in_specs=in_specs, out_specs=out_specs, check_vma=False)
```

```python
import functools
import itertools

import jax
import jax.numpy as jnp
from jax import lax
from jax.experimental import pallas as pl
from jax.experimental.pallas import tpu as pltpu
from jax.sharding import PartitionSpec as P

EXPERTS = 64
TOPK = 8
TOK = 128
MOST = 17
ROOM = 32
BUFFERS = 4


def passed_along(array, axis, by):
    peers = lax.axis_size(axis)
    pairs = [(i, i + by) for i in range(peers) if 0 <= i + by < peers]
    return lax.ppermute(array, axis, pairs)


def slot_ranks(pair_ids):
    onehot = (pair_ids[:, :, None] == jnp.arange(EXPERTS, dtype=jnp.int32)[None, None, :]).astype(
        jnp.int32
    )
    before = jnp.cumsum(onehot, axis=1) - onehot
    return jnp.sum(before * onehot, axis=2)


def place_rows(targets, capacity, source_rows, gate_values):
    pair_count = targets.shape[0]
    owner_pair = (
        jnp.full((capacity,), pair_count, jnp.int32)
        .at[targets]
        .set(jnp.arange(pair_count, dtype=jnp.int32), mode="drop")
    )
    filled = owner_pair < pair_count
    safe_pair = jnp.minimum(owner_pair, pair_count - 1)
    placed = jnp.where(
        filled[:, None], source_rows[safe_pair // TOPK], jnp.zeros((), source_rows.dtype)
    )
    placed_gate = jnp.where(
        filled, gate_values.reshape(-1)[safe_pair], jnp.zeros((), gate_values.dtype)
    )
    return (placed, placed_gate)


def arriving(sent_grad, head_grad):
    shifted = passed_along(sent_grad, "pipe", -1)
    is_last = lax.axis_index("pipe") == lax.axis_size("pipe") - 1
    return jnp.where(is_last, head_grad, shifted[0])


def local_by_slots(sent_grad, head_grad, probs, expert_ids, hidden_act):
    incoming = arriving(sent_grad, head_grad)
    feat_dev = incoming.shape[1]
    local_ids = expert_ids[0].reshape(1, TOK * TOPK)
    local_targets = (local_ids * MOST + slot_ranks(local_ids)).reshape(-1)
    send_rows, send_gate = place_rows(local_targets, EXPERTS * MOST, incoming, probs[0])
    recv_rows, recv_gate = (
        lax.all_to_all(
            send_rows.reshape(EXPERTS, MOST, feat_dev),
            "expert",
            split_axis=0,
            concat_axis=1,
            tiled=True,
        ),
        lax.all_to_all(
            send_gate.reshape(EXPERTS, MOST), "expert", split_axis=0, concat_axis=1, tiled=True
        ),
    )
    gate_wide = recv_gate.astype(jnp.float32)[:, :, None]
    full_rows = lax.all_gather(recv_rows, "tensor", axis=2, tiled=True)
    weighted = (full_rows.astype(jnp.float32) * gate_wide).astype(jnp.bfloat16)
    weight_grad = jnp.einsum(
        "esh,esd->ehd", hidden_act[0], weighted, preferred_element_type=jnp.float32
    ).astype(jnp.bfloat16)
    return weight_grad[None]


def notes_kernel(ids_ref, probs_ref, notes_ref):
    notes_ref[...] = jnp.concatenate(
        [ids_ref[...].astype(jnp.float32), probs_ref[...].astype(jnp.float32)], axis=0
    ).astype(jnp.bfloat16)


def turn_kernel(n_expert, act_ref, turned_ref):
    owned, slot_count, _ = act_ref.shape
    me = lax.axis_index("expert")
    slot = lax.broadcasted_iota(jnp.int32, (slot_count, n_expert * ROOM), 0)
    spot = lax.broadcasted_iota(jnp.int32, (slot_count, n_expert * ROOM), 1)
    block = jnp.zeros_like(slot)
    for b in range(1, n_expert):
        block += (slot >= b * MOST).astype(jnp.int32)
    back = me - block
    back = jnp.where(back < 0, back + n_expert, back)
    target = back * ROOM + slot - block * MOST
    for e in range(owned):
        turned_ref[e] = lax.dot_general(
            act_ref[e],
            (spot == target + e).astype(jnp.bfloat16),
            (((0,), (0,)), ((), ())),
            preferred_element_type=jnp.float32,
        ).astype(jnp.bfloat16)


def place_kernel(owned, *refs):
    *notes, place_ref = refs
    first = lax.axis_index("expert") * owned
    rows = place_ref.shape[1]
    experts = (first + lax.broadcasted_iota(jnp.int32, (owned, TOK), 0)).astype(jnp.float32)
    earlier = (
        lax.broadcasted_iota(jnp.int32, (TOK, TOK), 0)
        < lax.broadcasted_iota(jnp.int32, (TOK, TOK), 1)
    ).astype(jnp.float32)
    row = lax.broadcasted_iota(jnp.int32, (rows, owned), 0)
    start = lax.broadcasted_iota(jnp.int32, (rows, owned), 1) * MOST
    spread = ((row >= start) & (row < start + MOST)).astype(jnp.float32)
    wanted = lax.broadcasted_iota(jnp.int32, (rows, TOK), 0)
    for e in range(1, owned):
        wanted -= MOST * (
            lax.broadcasted_iota(jnp.int32, (rows, TOK), 0) >= e * MOST
        ).astype(jnp.int32)
    wanted = wanted.astype(jnp.float32)
    for k, note in enumerate(notes):
        meta = note[...].astype(jnp.float32)
        named = jnp.zeros((owned, TOK), jnp.float32)
        gate = jnp.zeros((owned, TOK), jnp.float32)
        for c in range(TOPK):
            hit = experts == meta[c : c + 1, :]
            named = jnp.where(hit, 1.0, named)
            gate = jnp.where(hit, meta[TOPK + c : TOPK + c + 1, :], gate)
        rank = jnp.dot(named, earlier, preferred_element_type=jnp.float32)
        rank = jnp.where(named > 0.0, rank, -1.0)
        rank = jnp.dot(spread, rank, preferred_element_type=jnp.float32)
        gate = jnp.dot(spread, gate, preferred_element_type=jnp.float32)
        place_ref[k] = jnp.where(rank == wanted, gate, 0.0).astype(jnp.bfloat16)


def early_kernel(ks, place_ref, *refs):
    blocks, outs = refs[: len(ks)], refs[len(ks) :]
    weigh_tiles([place_ref.at[k] for k in ks], blocks, outs)


def weigh_tiles(places, blocks, outs):
    @pl.loop(0, blocks[0].shape[1] // 256)
    def _(t):
        wide = pl.ds(pl.multiple_of(t * 256, 256), 256)
        for place, block, out in zip(places, blocks, outs):
            out[:, wide] = jnp.dot(
                place[...], block[:, wide], preferred_element_type=jnp.float32
            ).astype(jnp.bfloat16)


def grad_kernel(n_expert, other, early, place_ref, act_ref, *refs):
    blocks = refs[:n_expert]
    out_ref, weighted_ref, done_ref, out_sem = refs[-4:]
    owned, hid, _ = act_ref.shape
    features = done_ref.shape[2]
    side = lax.rem(lax.axis_index("tensor") + other, lax.axis_size("tensor"))
    column = pl.multiple_of(side * features, 128)

    def leave(e):
        slot = lax.rem(e, BUFFERS)
        return pltpu.make_async_copy(
            done_ref.at[slot], out_ref.at[e, :, pl.ds(column, features)], out_sem.at[slot]
        )

    late = [weighted_ref.at[k] for k in range(n_expert - early)]
    weigh_tiles([place_ref.at[k] for k in range(early, n_expert)], blocks[early:], late)
    weighted = [*blocks[:early], *late]

    @pl.loop(0, owned)
    def _(e):
        @pl.when(e >= BUFFERS)
        def _():
            leave(e - BUFFERS).wait()

        window = pl.ds(pl.multiple_of(e * 16, 16), ROOM)
        for n in range(0, features, 256):
            wide = slice(n, min(n + 256, features))
            right = jnp.concatenate([rows[window, wide] for rows in weighted], axis=0)
            done_ref[lax.rem(e, BUFFERS), :, wide] = jnp.dot(
                act_ref[e], right, preferred_element_type=jnp.float32
            ).astype(jnp.bfloat16)
        leave(e).start()

    @pl.loop(owned - BUFFERS, owned)
    def _(e):
        leave(e).wait()


def local_by_tokens(sent_grad, head_grad, probs, expert_ids, hidden_act):
    n_expert = lax.axis_size("expert")
    n_tensor = lax.axis_size("tensor")
    owned, _, hid = hidden_act.shape[1:]
    feat_dev = sent_grad.shape[2]
    vmem = pl.BlockSpec(memory_space=pltpu.VMEM)
    anywhere = pl.BlockSpec(memory_space=pl.ANY)

    def small_call(kernel, shapes, operands, name):
        return pl.pallas_call(
            kernel,
            out_shape=[jax.ShapeDtypeStruct(shape, jnp.bfloat16) for shape in shapes],
            in_specs=[vmem] * len(operands),
            out_specs=[vmem] * len(shapes),
            compiler_params=pltpu.CompilerParams(vmem_limit_bytes=16 * 2**20),
            name=name,
        )(*operands)

    def turned(array, pipe=0, expert=0, tensor=0):
        axes = ("pipe", "expert", "tensor")
        sizes = [lax.axis_size(axis) for axis in axes]
        steps = (pipe, expert, tensor)

        def rank(place):
            return (place[0] * sizes[1] + place[1]) * sizes[2] + place[2]

        pairs = []
        for place in itertools.product(*map(range, sizes)):
            target = [(i + by) % size for i, by, size in zip(place, steps, sizes)]
            pairs.append((rank(place), rank(target)))
        return lax.ppermute(array, axes, pairs)

    def grad_into(out, blocks, other, early):
        operands = [place, act, *blocks]
        in_specs = [vmem] * len(operands)
        aliases = {}
        if out is not None:
            aliases = {len(operands): 0}
            in_specs.append(anywhere)
            operands.append(out)
        return pl.pallas_call(
            functools.partial(grad_kernel, n_expert, other, early),
            out_shape=jax.ShapeDtypeStruct((owned, hid, n_tensor * feat_dev), jnp.bfloat16),
            in_specs=in_specs,
            out_specs=anywhere,
            scratch_shapes=[
                pltpu.VMEM((n_expert - early, place.shape[1], feat_dev), jnp.bfloat16),
                pltpu.VMEM((BUFFERS, hid, feat_dev), jnp.bfloat16),
                pltpu.SemaphoreType.DMA((BUFFERS,)),
            ],
            input_output_aliases=aliases,
            compiler_params=pltpu.CompilerParams(vmem_limit_bytes=28 * 2**20),
            cost_estimate=pl.CostEstimate(
                flops=2 * owned * hid * 256 * feat_dev,
                bytes_accessed=2 * owned * hid * feat_dev,
                transcendentals=0,
            ),
            name="weight_grad",
        )(*operands)

    payload = jnp.where(lax.axis_index("pipe") == 0, head_grad, sent_grad[0])
    blocks = {1: turned(payload, -1, 1)}
    beside = {0: {t: turned(payload, -1, 0, t) for t in range(1, n_tensor)}}
    (notes,) = small_call(
        notes_kernel, [(2 * TOPK, TOK)], [expert_ids[0].T, probs[0].T], "notes"
    )
    notes = [notes] + [turned(notes, 0, k) for k in range(1, n_expert)]
    (act,) = small_call(
        functools.partial(turn_kernel, n_expert),
        [(owned, hid, n_expert * ROOM)],
        [hidden_act[0]],
        "turn",
    )
    beside[0], payload, act, notes[1:] = lax.optimization_barrier(
        (beside[0], payload, act, notes[1:])
    )
    blocks[n_expert - 1] = turned(payload, -1, -1)
    blocks[0] = turned(payload, -1)
    for k in range(2, n_expert - 1):
        blocks[k] = turned(blocks[k - 1], 0, 1)
    (place,) = small_call(
        functools.partial(place_kernel, owned), [(n_expert, 16 * (owned + 1), TOK)], notes, "place"
    )
    def weighed(sources):
        return small_call(
            functools.partial(early_kernel, range(len(sources))),
            [(place.shape[1], feat_dev)] * len(sources),
            [place, *sources],
            "early",
        )

    middle = n_expert - 2
    own = weighed([blocks[k] for k in range(n_expert - 1)])
    others = {t: weighed([beside[0][t]]) for t in beside[0]}
    for k in range(1, n_expert):
        if k == middle:
            blocks[k], own, others = lax.optimization_barrier((blocks[k], own, others))
        beside[k] = {t: turned(blocks[k], 0, 0, t) for t in range(1, n_tensor)}
    out = grad_into(None, [*own, blocks[n_expert - 1]], 0, n_expert - 1)
    for t in others:
        late = [beside[k][t] for k in range(1, n_expert)]
        out = grad_into(out, [*others[t], *late], n_tensor - t, 1)
    return out[None]


def local(*arrays):
    owned, slot_count = arrays[4].shape[1:3]
    tokens = lax.axis_size("expert") * TOK
    by_tokens = owned <= 16 and tokens <= owned * slot_count
    return (local_by_tokens if by_tokens else local_by_slots)(*arrays)


def solution(mesh):
    in_specs = (
        P("pipe", "expert", "tensor"),
        P("expert", "tensor"),
        P("pipe", "expert", None),
        P("pipe", "expert", None),
        P("pipe", "expert", None, "tensor"),
    )
    out_specs = P("pipe", "expert", "tensor", None)
    return jax.shard_map(local, mesh=mesh, in_specs=in_specs, out_specs=out_specs, check_vma=False)
```

```python
import functools
import itertools

import jax
import jax.numpy as jnp
from jax import lax
from jax.experimental import pallas as pl
from jax.experimental.pallas import tpu as pltpu
from jax.sharding import PartitionSpec as P

EXPERTS = 64
TOPK = 8
TOK = 128
MOST = 17
ROOM = 32
BUFFERS = 4


def passed_along(array, axis, by):
    peers = lax.axis_size(axis)
    pairs = [(i, i + by) for i in range(peers) if 0 <= i + by < peers]
    return lax.ppermute(array, axis, pairs)


def slot_ranks(pair_ids):
    onehot = (pair_ids[:, :, None] == jnp.arange(EXPERTS, dtype=jnp.int32)[None, None, :]).astype(
        jnp.int32
    )
    before = jnp.cumsum(onehot, axis=1) - onehot
    return jnp.sum(before * onehot, axis=2)


def place_rows(targets, capacity, source_rows, gate_values):
    pair_count = targets.shape[0]
    owner_pair = (
        jnp.full((capacity,), pair_count, jnp.int32)
        .at[targets]
        .set(jnp.arange(pair_count, dtype=jnp.int32), mode="drop")
    )
    filled = owner_pair < pair_count
    safe_pair = jnp.minimum(owner_pair, pair_count - 1)
    placed = jnp.where(
        filled[:, None], source_rows[safe_pair // TOPK], jnp.zeros((), source_rows.dtype)
    )
    placed_gate = jnp.where(
        filled, gate_values.reshape(-1)[safe_pair], jnp.zeros((), gate_values.dtype)
    )
    return (placed, placed_gate)


def arriving(sent_grad, head_grad):
    shifted = passed_along(sent_grad, "pipe", -1)
    is_last = lax.axis_index("pipe") == lax.axis_size("pipe") - 1
    return jnp.where(is_last, head_grad, shifted[0])


def local_by_slots(sent_grad, head_grad, probs, expert_ids, hidden_act):
    incoming = arriving(sent_grad, head_grad)
    feat_dev = incoming.shape[1]
    local_ids = expert_ids[0].reshape(1, TOK * TOPK)
    local_targets = (local_ids * MOST + slot_ranks(local_ids)).reshape(-1)
    send_rows, send_gate = place_rows(local_targets, EXPERTS * MOST, incoming, probs[0])
    recv_rows, recv_gate = (
        lax.all_to_all(
            send_rows.reshape(EXPERTS, MOST, feat_dev),
            "expert",
            split_axis=0,
            concat_axis=1,
            tiled=True,
        ),
        lax.all_to_all(
            send_gate.reshape(EXPERTS, MOST), "expert", split_axis=0, concat_axis=1, tiled=True
        ),
    )
    gate_wide = recv_gate.astype(jnp.float32)[:, :, None]
    full_rows = lax.all_gather(recv_rows, "tensor", axis=2, tiled=True)
    weighted = (full_rows.astype(jnp.float32) * gate_wide).astype(jnp.bfloat16)
    weight_grad = jnp.einsum(
        "esh,esd->ehd", hidden_act[0], weighted, preferred_element_type=jnp.float32
    ).astype(jnp.bfloat16)
    return weight_grad[None]


def notes_kernel(ids_ref, probs_ref, notes_ref):
    notes_ref[...] = jnp.concatenate(
        [ids_ref[...].astype(jnp.float32), probs_ref[...].astype(jnp.float32)], axis=0
    ).astype(jnp.bfloat16)


def turn_kernel(n_expert, act_ref, turned_ref):
    owned, slot_count, _ = act_ref.shape
    me = lax.axis_index("expert")
    slot = lax.broadcasted_iota(jnp.int32, (slot_count, n_expert * ROOM), 0)
    spot = lax.broadcasted_iota(jnp.int32, (slot_count, n_expert * ROOM), 1)
    block = jnp.zeros_like(slot)
    for b in range(1, n_expert):
        block += (slot >= b * MOST).astype(jnp.int32)
    back = me - block
    back = jnp.where(back < 0, back + n_expert, back)
    target = back * ROOM + slot - block * MOST
    for e in range(owned):
        turned_ref[e] = lax.dot_general(
            act_ref[e],
            (spot == target + e).astype(jnp.bfloat16),
            (((0,), (0,)), ((), ())),
            preferred_element_type=jnp.float32,
        ).astype(jnp.bfloat16)


def place_kernel(owned, *refs):
    *notes, place_ref = refs
    first = lax.axis_index("expert") * owned
    rows = place_ref.shape[1]
    experts = (first + lax.broadcasted_iota(jnp.int32, (owned, TOK), 0)).astype(jnp.float32)
    earlier = (
        lax.broadcasted_iota(jnp.int32, (TOK, TOK), 0)
        < lax.broadcasted_iota(jnp.int32, (TOK, TOK), 1)
    ).astype(jnp.float32)
    row = lax.broadcasted_iota(jnp.int32, (rows, owned), 0)
    start = lax.broadcasted_iota(jnp.int32, (rows, owned), 1) * MOST
    spread = ((row >= start) & (row < start + MOST)).astype(jnp.float32)
    wanted = lax.broadcasted_iota(jnp.int32, (rows, TOK), 0)
    for e in range(1, owned):
        wanted -= MOST * (
            lax.broadcasted_iota(jnp.int32, (rows, TOK), 0) >= e * MOST
        ).astype(jnp.int32)
    wanted = wanted.astype(jnp.float32)
    for k, note in enumerate(notes):
        meta = note[...].astype(jnp.float32)
        named = jnp.zeros((owned, TOK), jnp.float32)
        gate = jnp.zeros((owned, TOK), jnp.float32)
        for c in range(TOPK):
            hit = experts == meta[c : c + 1, :]
            named = jnp.where(hit, 1.0, named)
            gate = jnp.where(hit, meta[TOPK + c : TOPK + c + 1, :], gate)
        rank = jnp.dot(named, earlier, preferred_element_type=jnp.float32)
        rank = jnp.where(named > 0.0, rank, -1.0)
        rank = jnp.dot(spread, rank, preferred_element_type=jnp.float32)
        gate = jnp.dot(spread, gate, preferred_element_type=jnp.float32)
        place_ref[k] = jnp.where(rank == wanted, gate, 0.0).astype(jnp.bfloat16)


def early_kernel(ks, place_ref, *refs):
    blocks, outs = refs[: len(ks)], refs[len(ks) :]
    weigh_tiles([place_ref.at[k] for k in ks], blocks, outs)


def weigh_tiles(places, blocks, outs):
    @pl.loop(0, blocks[0].shape[1] // 256)
    def _(t):
        wide = pl.ds(pl.multiple_of(t * 256, 256), 256)
        for place, block, out in zip(places, blocks, outs):
            out[:, wide] = jnp.dot(
                place[...], block[:, wide], preferred_element_type=jnp.float32
            ).astype(jnp.bfloat16)


def grad_kernel(n_expert, other, early, place_ref, act_ref, *refs):
    blocks = refs[:n_expert]
    out_ref, weighted_ref, done_ref, out_sem = refs[-4:]
    owned, hid, _ = act_ref.shape
    features = done_ref.shape[2]
    side = lax.rem(lax.axis_index("tensor") + other, lax.axis_size("tensor"))
    column = pl.multiple_of(side * features, 128)

    def leave(e):
        slot = lax.rem(e, BUFFERS)
        return pltpu.make_async_copy(
            done_ref.at[slot], out_ref.at[e, :, pl.ds(column, features)], out_sem.at[slot]
        )

    late = [weighted_ref.at[k] for k in range(n_expert - early)]
    weigh_tiles([place_ref.at[k] for k in range(early, n_expert)], blocks[early:], late)
    weighted = [*blocks[:early], *late]

    @pl.loop(0, owned)
    def _(e):
        @pl.when(e >= BUFFERS)
        def _():
            leave(e - BUFFERS).wait()

        window = pl.ds(pl.multiple_of(e * 16, 16), ROOM)
        for n in range(0, features, 256):
            wide = slice(n, min(n + 256, features))
            right = jnp.concatenate([rows[window, wide] for rows in weighted], axis=0)
            done_ref[lax.rem(e, BUFFERS), :, wide] = jnp.dot(
                act_ref[e], right, preferred_element_type=jnp.float32
            ).astype(jnp.bfloat16)
        leave(e).start()

    @pl.loop(owned - BUFFERS, owned)
    def _(e):
        leave(e).wait()


def local_by_tokens(sent_grad, head_grad, probs, expert_ids, hidden_act):
    n_expert = lax.axis_size("expert")
    n_tensor = lax.axis_size("tensor")
    owned, _, hid = hidden_act.shape[1:]
    feat_dev = sent_grad.shape[2]
    vmem = pl.BlockSpec(memory_space=pltpu.VMEM)
    anywhere = pl.BlockSpec(memory_space=pl.ANY)

    def small_call(kernel, shapes, operands, name):
        return pl.pallas_call(
            kernel,
            out_shape=[jax.ShapeDtypeStruct(shape, jnp.bfloat16) for shape in shapes],
            in_specs=[vmem] * len(operands),
            out_specs=[vmem] * len(shapes),
            compiler_params=pltpu.CompilerParams(vmem_limit_bytes=16 * 2**20),
            name=name,
        )(*operands)

    def turned(array, pipe=0, expert=0, tensor=0):
        axes = ("pipe", "expert", "tensor")
        sizes = [lax.axis_size(axis) for axis in axes]
        steps = (pipe, expert, tensor)

        def rank(place):
            return (place[0] * sizes[1] + place[1]) * sizes[2] + place[2]

        pairs = []
        for place in itertools.product(*map(range, sizes)):
            target = [(i + by) % size for i, by, size in zip(place, steps, sizes)]
            pairs.append((rank(place), rank(target)))
        return lax.ppermute(array, axes, pairs)

    def grad_into(out, blocks, other, early):
        operands = [place, act, *blocks]
        in_specs = [vmem] * len(operands)
        aliases = {}
        if out is not None:
            aliases = {len(operands): 0}
            in_specs.append(anywhere)
            operands.append(out)
        return pl.pallas_call(
            functools.partial(grad_kernel, n_expert, other, early),
            out_shape=jax.ShapeDtypeStruct((owned, hid, n_tensor * feat_dev), jnp.bfloat16),
            in_specs=in_specs,
            out_specs=anywhere,
            scratch_shapes=[
                pltpu.VMEM((n_expert - early, place.shape[1], feat_dev), jnp.bfloat16),
                pltpu.VMEM((BUFFERS, hid, feat_dev), jnp.bfloat16),
                pltpu.SemaphoreType.DMA((BUFFERS,)),
            ],
            input_output_aliases=aliases,
            compiler_params=pltpu.CompilerParams(vmem_limit_bytes=28 * 2**20),
            cost_estimate=pl.CostEstimate(
                flops=2 * owned * hid * 256 * feat_dev,
                bytes_accessed=2 * owned * hid * feat_dev,
                transcendentals=0,
            ),
            name="weight_grad",
        )(*operands)

    payload = jnp.where(lax.axis_index("pipe") == 0, head_grad, sent_grad[0])
    blocks = {1: turned(payload, -1, 1)}
    beside = {0: {t: turned(payload, -1, 0, t) for t in range(1, n_tensor)}}
    (notes,) = small_call(
        notes_kernel, [(2 * TOPK, TOK)], [expert_ids[0].T, probs[0].T], "notes"
    )
    notes = [notes] + [turned(notes, 0, k) for k in range(1, n_expert)]
    (act,) = small_call(
        functools.partial(turn_kernel, n_expert),
        [(owned, hid, n_expert * ROOM)],
        [hidden_act[0]],
        "turn",
    )
    beside[0], payload, act, notes[1:] = lax.optimization_barrier(
        (beside[0], payload, act, notes[1:])
    )
    blocks[n_expert - 1] = turned(payload, -1, -1)
    blocks[0] = turned(payload, -1)
    for k in range(2, n_expert - 1):
        blocks[k] = turned(blocks[k - 1], 0, 1)
    (place,) = small_call(
        functools.partial(place_kernel, owned), [(n_expert, 16 * (owned + 1), TOK)], notes, "place"
    )
    def weighed(sources):
        return small_call(
            functools.partial(early_kernel, range(len(sources))),
            [(place.shape[1], feat_dev)] * len(sources),
            [place, *sources],
            "early",
        )

    middle = n_expert - 2
    own = weighed([blocks[k] for k in range(n_expert - 1)])
    for k in range(1, n_expert):
        if k == middle:
            others = {t: weighed([beside[i][t] for i in range(k)]) for t in range(1, n_tensor)}
            blocks[k], own, others = lax.optimization_barrier((blocks[k], own, others))
        beside[k] = {t: turned(blocks[k], 0, 0, t) for t in range(1, n_tensor)}
    out = grad_into(None, [*own, blocks[n_expert - 1]], 0, n_expert - 1)
    for t in others:
        late = [beside[k][t] for k in range(middle, n_expert)]
        out = grad_into(out, [*others[t], *late], n_tensor - t, middle)
    return out[None]


def local(*arrays):
    owned, slot_count = arrays[4].shape[1:3]
    tokens = lax.axis_size("expert") * TOK
    by_tokens = owned <= 16 and tokens <= owned * slot_count
    return (local_by_tokens if by_tokens else local_by_slots)(*arrays)


def solution(mesh):
    in_specs = (
        P("pipe", "expert", "tensor"),
        P("expert", "tensor"),
        P("pipe", "expert", None),
        P("pipe", "expert", None),
        P("pipe", "expert", None, "tensor"),
    )
    out_specs = P("pipe", "expert", "tensor", None)
    return jax.shard_map(local, mesh=mesh, in_specs=in_specs, out_specs=out_specs, check_vma=False)
```

```python
import functools
import itertools

import jax
import jax.numpy as jnp
from jax import lax
from jax.experimental import pallas as pl
from jax.experimental.pallas import tpu as pltpu
from jax.sharding import PartitionSpec as P

EXPERTS = 64
TOPK = 8
TOK = 128
MOST = 17
ROOM = 32
BUFFERS = 4


def passed_along(array, axis, by):
    peers = lax.axis_size(axis)
    pairs = [(i, i + by) for i in range(peers) if 0 <= i + by < peers]
    return lax.ppermute(array, axis, pairs)


def slot_ranks(pair_ids):
    onehot = (pair_ids[:, :, None] == jnp.arange(EXPERTS, dtype=jnp.int32)[None, None, :]).astype(
        jnp.int32
    )
    before = jnp.cumsum(onehot, axis=1) - onehot
    return jnp.sum(before * onehot, axis=2)


def place_rows(targets, capacity, source_rows, gate_values):
    pair_count = targets.shape[0]
    owner_pair = (
        jnp.full((capacity,), pair_count, jnp.int32)
        .at[targets]
        .set(jnp.arange(pair_count, dtype=jnp.int32), mode="drop")
    )
    filled = owner_pair < pair_count
    safe_pair = jnp.minimum(owner_pair, pair_count - 1)
    placed = jnp.where(
        filled[:, None], source_rows[safe_pair // TOPK], jnp.zeros((), source_rows.dtype)
    )
    placed_gate = jnp.where(
        filled, gate_values.reshape(-1)[safe_pair], jnp.zeros((), gate_values.dtype)
    )
    return (placed, placed_gate)


def arriving(sent_grad, head_grad):
    shifted = passed_along(sent_grad, "pipe", -1)
    is_last = lax.axis_index("pipe") == lax.axis_size("pipe") - 1
    return jnp.where(is_last, head_grad, shifted[0])


def local_by_slots(sent_grad, head_grad, probs, expert_ids, hidden_act):
    incoming = arriving(sent_grad, head_grad)
    feat_dev = incoming.shape[1]
    local_ids = expert_ids[0].reshape(1, TOK * TOPK)
    local_targets = (local_ids * MOST + slot_ranks(local_ids)).reshape(-1)
    send_rows, send_gate = place_rows(local_targets, EXPERTS * MOST, incoming, probs[0])
    recv_rows, recv_gate = (
        lax.all_to_all(
            send_rows.reshape(EXPERTS, MOST, feat_dev),
            "expert",
            split_axis=0,
            concat_axis=1,
            tiled=True,
        ),
        lax.all_to_all(
            send_gate.reshape(EXPERTS, MOST), "expert", split_axis=0, concat_axis=1, tiled=True
        ),
    )
    gate_wide = recv_gate.astype(jnp.float32)[:, :, None]
    full_rows = lax.all_gather(recv_rows, "tensor", axis=2, tiled=True)
    weighted = (full_rows.astype(jnp.float32) * gate_wide).astype(jnp.bfloat16)
    weight_grad = jnp.einsum(
        "esh,esd->ehd", hidden_act[0], weighted, preferred_element_type=jnp.float32
    ).astype(jnp.bfloat16)
    return weight_grad[None]


def notes_kernel(ids_ref, probs_ref, notes_ref):
    notes_ref[...] = jnp.concatenate(
        [ids_ref[...].astype(jnp.float32), probs_ref[...].astype(jnp.float32)], axis=0
    ).astype(jnp.bfloat16)


def turn_kernel(n_expert, act_ref, turned_ref):
    owned, slot_count, _ = act_ref.shape
    me = lax.axis_index("expert")
    slot = lax.broadcasted_iota(jnp.int32, (slot_count, n_expert * ROOM), 0)
    spot = lax.broadcasted_iota(jnp.int32, (slot_count, n_expert * ROOM), 1)
    block = jnp.zeros_like(slot)
    for b in range(1, n_expert):
        block += (slot >= b * MOST).astype(jnp.int32)
    back = me - block
    back = jnp.where(back < 0, back + n_expert, back)
    target = back * ROOM + slot - block * MOST
    for e in range(owned):
        turned_ref[e] = lax.dot_general(
            act_ref[e],
            (spot == target + e).astype(jnp.bfloat16),
            (((0,), (0,)), ((), ())),
            preferred_element_type=jnp.float32,
        ).astype(jnp.bfloat16)


def place_kernel(owned, *refs):
    *notes, place_ref = refs
    first = lax.axis_index("expert") * owned
    rows = place_ref.shape[1]
    experts = (first + lax.broadcasted_iota(jnp.int32, (owned, TOK), 0)).astype(jnp.float32)
    earlier = (
        lax.broadcasted_iota(jnp.int32, (TOK, TOK), 0)
        < lax.broadcasted_iota(jnp.int32, (TOK, TOK), 1)
    ).astype(jnp.float32)
    row = lax.broadcasted_iota(jnp.int32, (rows, owned), 0)
    start = lax.broadcasted_iota(jnp.int32, (rows, owned), 1) * MOST
    spread = ((row >= start) & (row < start + MOST)).astype(jnp.float32)
    wanted = lax.broadcasted_iota(jnp.int32, (rows, TOK), 0)
    for e in range(1, owned):
        wanted -= MOST * (
            lax.broadcasted_iota(jnp.int32, (rows, TOK), 0) >= e * MOST
        ).astype(jnp.int32)
    wanted = wanted.astype(jnp.float32)
    for k, note in enumerate(notes):
        meta = note[...].astype(jnp.float32)
        named = jnp.zeros((owned, TOK), jnp.float32)
        gate = jnp.zeros((owned, TOK), jnp.float32)
        for c in range(TOPK):
            hit = experts == meta[c : c + 1, :]
            named = jnp.where(hit, 1.0, named)
            gate = jnp.where(hit, meta[TOPK + c : TOPK + c + 1, :], gate)
        rank = jnp.dot(named, earlier, preferred_element_type=jnp.float32)
        rank = jnp.where(named > 0.0, rank, -1.0)
        rank = jnp.dot(spread, rank, preferred_element_type=jnp.float32)
        gate = jnp.dot(spread, gate, preferred_element_type=jnp.float32)
        place_ref[k] = jnp.where(rank == wanted, gate, 0.0).astype(jnp.bfloat16)


def early_kernel(ks, place_ref, *refs):
    blocks, outs = refs[: len(ks)], refs[len(ks) :]
    weigh_tiles([place_ref.at[k] for k in ks], blocks, outs)


def weigh_tiles(places, blocks, outs):
    half = blocks[0].shape[1] // 2

    @pl.loop(0, 2)
    def _(t):
        wide = pl.ds(pl.multiple_of(t * half, half), half)
        for place, block, out in zip(places, blocks, outs):
            out[:, wide] = jnp.dot(
                place[...], block[:, wide], preferred_element_type=jnp.float32
            ).astype(jnp.bfloat16)


def grad_kernel(n_expert, other, early, place_ref, act_ref, *refs):
    blocks = refs[:n_expert]
    out_ref, weighted_ref, done_ref, out_sem = refs[-4:]
    owned, hid, _ = act_ref.shape
    features = done_ref.shape[2]
    side = lax.rem(lax.axis_index("tensor") + other, lax.axis_size("tensor"))
    column = pl.multiple_of(side * features, 128)

    def leave(e):
        slot = lax.rem(e, BUFFERS)
        return pltpu.make_async_copy(
            done_ref.at[slot], out_ref.at[e, :, pl.ds(column, features)], out_sem.at[slot]
        )

    late = [k for k in range(n_expert) if k not in early]
    weighted = list(blocks)
    for i, k in enumerate(late):
        weighted[k] = weighted_ref.at[i]
    weigh_tiles([place_ref.at[k] for k in late], [blocks[k] for k in late], [weighted[k] for k in late])

    @pl.loop(0, owned)
    def _(e):
        @pl.when(e >= BUFFERS)
        def _():
            leave(e - BUFFERS).wait()

        window = pl.ds(pl.multiple_of(e * 16, 16), ROOM)
        for n in range(0, features, 256):
            wide = slice(n, min(n + 256, features))
            right = jnp.concatenate([rows[window, wide] for rows in weighted], axis=0)
            done_ref[lax.rem(e, BUFFERS), :, wide] = jnp.dot(
                act_ref[e], right, preferred_element_type=jnp.float32
            ).astype(jnp.bfloat16)
        leave(e).start()

    @pl.loop(owned - BUFFERS, owned)
    def _(e):
        leave(e).wait()


def local_by_tokens(sent_grad, head_grad, probs, expert_ids, hidden_act):
    n_expert = lax.axis_size("expert")
    n_tensor = lax.axis_size("tensor")
    owned, _, hid = hidden_act.shape[1:]
    feat_dev = sent_grad.shape[2]
    vmem = pl.BlockSpec(memory_space=pltpu.VMEM)
    anywhere = pl.BlockSpec(memory_space=pl.ANY)

    def small_call(kernel, shapes, operands, name):
        return pl.pallas_call(
            kernel,
            out_shape=[jax.ShapeDtypeStruct(shape, jnp.bfloat16) for shape in shapes],
            in_specs=[vmem] * len(operands),
            out_specs=[vmem] * len(shapes),
            compiler_params=pltpu.CompilerParams(vmem_limit_bytes=16 * 2**20),
            name=name,
        )(*operands)

    def turned(array, pipe=0, expert=0, tensor=0):
        axes = ("pipe", "expert", "tensor")
        sizes = [lax.axis_size(axis) for axis in axes]
        steps = (pipe, expert, tensor)

        def rank(place):
            return (place[0] * sizes[1] + place[1]) * sizes[2] + place[2]

        pairs = []
        for place in itertools.product(*map(range, sizes)):
            target = [(i + by) % size for i, by, size in zip(place, steps, sizes)]
            pairs.append((rank(place), rank(target)))
        return lax.ppermute(array, axes, pairs)

    def grad_into(out, blocks, other, early):
        operands = [place, act, *blocks]
        in_specs = [vmem] * len(operands)
        aliases = {}
        if out is not None:
            aliases = {len(operands): 0}
            in_specs.append(anywhere)
            operands.append(out)
        return pl.pallas_call(
            functools.partial(grad_kernel, n_expert, other, early),
            out_shape=jax.ShapeDtypeStruct((owned, hid, n_tensor * feat_dev), jnp.bfloat16),
            in_specs=in_specs,
            out_specs=anywhere,
            scratch_shapes=[
                pltpu.VMEM((n_expert - len(early), place.shape[1], feat_dev), jnp.bfloat16),
                pltpu.VMEM((BUFFERS, hid, feat_dev), jnp.bfloat16),
                pltpu.SemaphoreType.DMA((BUFFERS,)),
            ],
            input_output_aliases=aliases,
            compiler_params=pltpu.CompilerParams(vmem_limit_bytes=28 * 2**20),
            cost_estimate=pl.CostEstimate(
                flops=2 * owned * hid * 256 * feat_dev,
                bytes_accessed=2 * owned * hid * feat_dev,
                transcendentals=0,
            ),
            name="weight_grad",
        )(*operands)

    payload = jnp.where(lax.axis_index("pipe") == 0, head_grad, sent_grad[0])
    blocks = {1: turned(payload, -1, 1)}
    beside = {0: {t: turned(payload, -1, 0, t) for t in range(1, n_tensor)}}
    (notes,) = small_call(
        notes_kernel, [(2 * TOPK, TOK)], [expert_ids[0].T, probs[0].T], "notes"
    )
    notes = [notes] + [turned(notes, 0, k) for k in range(1, n_expert)]
    (act,) = small_call(
        functools.partial(turn_kernel, n_expert),
        [(owned, hid, n_expert * ROOM)],
        [hidden_act[0]],
        "turn",
    )
    beside[0], payload, act, notes[1:] = lax.optimization_barrier(
        (beside[0], payload, act, notes[1:])
    )
    blocks[n_expert - 1] = turned(payload, -1, -1)
    for k in range(2, n_expert - 1):
        blocks[k] = turned(blocks[k - 1], 0, 1)
    (place,) = small_call(
        functools.partial(place_kernel, owned), [(n_expert, 16 * (owned + 1), TOK)], notes, "place"
    )
    blocks[0] = turned(payload, -1)

    def weighed(sources, ks):
        done = small_call(
            functools.partial(early_kernel, ks),
            [(place.shape[1], feat_dev)] * len(ks),
            [place, *(sources[k] for k in ks)],
            "early",
        )
        return dict(zip(ks, done))

    last = n_expert - 1
    early = tuple(range(1, last))
    own = weighed(blocks, early)
    blocks[last - 1], own = lax.optimization_barrier((blocks[last - 1], own))
    for k in range(1, n_expert):
        beside[k] = {t: turned(blocks[k], 0, 0, t) for t in range(1, n_tensor)}
    out = grad_into(None, [own.get(k, blocks[k]) for k in range(n_expert)], 0, early)
    for t in range(1, n_tensor):
        out = grad_into(out, [beside[k][t] for k in range(n_expert)], n_tensor - t, ())
    return out[None]


def local(*arrays):
    owned, slot_count = arrays[4].shape[1:3]
    tokens = lax.axis_size("expert") * TOK
    by_tokens = owned <= 16 and tokens <= owned * slot_count
    return (local_by_tokens if by_tokens else local_by_slots)(*arrays)


def solution(mesh):
    in_specs = (
        P("pipe", "expert", "tensor"),
        P("expert", "tensor"),
        P("pipe", "expert", None),
        P("pipe", "expert", None),
        P("pipe", "expert", None, "tensor"),
    )
    out_specs = P("pipe", "expert", "tensor", None)
    return jax.shard_map(local, mesh=mesh, in_specs=in_specs, out_specs=out_specs, check_vma=False)
```

```python
import functools
import itertools

import jax
import jax.numpy as jnp
from jax import lax
from jax.experimental import pallas as pl
from jax.experimental.pallas import tpu as pltpu
from jax.sharding import PartitionSpec as P

EXPERTS = 64
TOPK = 8
TOK = 128
MOST = 17
ROOM = 32
BUFFERS = 4


def passed_along(array, axis, by):
    peers = lax.axis_size(axis)
    pairs = [(i, i + by) for i in range(peers) if 0 <= i + by < peers]
    return lax.ppermute(array, axis, pairs)


def slot_ranks(pair_ids):
    onehot = (pair_ids[:, :, None] == jnp.arange(EXPERTS, dtype=jnp.int32)[None, None, :]).astype(
        jnp.int32
    )
    before = jnp.cumsum(onehot, axis=1) - onehot
    return jnp.sum(before * onehot, axis=2)


def place_rows(targets, capacity, source_rows, gate_values):
    pair_count = targets.shape[0]
    owner_pair = (
        jnp.full((capacity,), pair_count, jnp.int32)
        .at[targets]
        .set(jnp.arange(pair_count, dtype=jnp.int32), mode="drop")
    )
    filled = owner_pair < pair_count
    safe_pair = jnp.minimum(owner_pair, pair_count - 1)
    placed = jnp.where(
        filled[:, None], source_rows[safe_pair // TOPK], jnp.zeros((), source_rows.dtype)
    )
    placed_gate = jnp.where(
        filled, gate_values.reshape(-1)[safe_pair], jnp.zeros((), gate_values.dtype)
    )
    return (placed, placed_gate)


def arriving(sent_grad, head_grad):
    shifted = passed_along(sent_grad, "pipe", -1)
    is_last = lax.axis_index("pipe") == lax.axis_size("pipe") - 1
    return jnp.where(is_last, head_grad, shifted[0])


def local_by_slots(sent_grad, head_grad, probs, expert_ids, hidden_act):
    incoming = arriving(sent_grad, head_grad)
    feat_dev = incoming.shape[1]
    local_ids = expert_ids[0].reshape(1, TOK * TOPK)
    local_targets = (local_ids * MOST + slot_ranks(local_ids)).reshape(-1)
    send_rows, send_gate = place_rows(local_targets, EXPERTS * MOST, incoming, probs[0])
    recv_rows, recv_gate = (
        lax.all_to_all(
            send_rows.reshape(EXPERTS, MOST, feat_dev),
            "expert",
            split_axis=0,
            concat_axis=1,
            tiled=True,
        ),
        lax.all_to_all(
            send_gate.reshape(EXPERTS, MOST), "expert", split_axis=0, concat_axis=1, tiled=True
        ),
    )
    gate_wide = recv_gate.astype(jnp.float32)[:, :, None]
    full_rows = lax.all_gather(recv_rows, "tensor", axis=2, tiled=True)
    weighted = (full_rows.astype(jnp.float32) * gate_wide).astype(jnp.bfloat16)
    weight_grad = jnp.einsum(
        "esh,esd->ehd", hidden_act[0], weighted, preferred_element_type=jnp.float32
    ).astype(jnp.bfloat16)
    return weight_grad[None]


def notes_kernel(ids_ref, probs_ref, notes_ref):
    notes_ref[...] = jnp.concatenate(
        [ids_ref[...].astype(jnp.float32), probs_ref[...].astype(jnp.float32)], axis=0
    ).astype(jnp.bfloat16)


def turn_kernel(n_expert, act_ref, turned_ref):
    owned, slot_count, _ = act_ref.shape
    me = lax.axis_index("expert")
    slot = lax.broadcasted_iota(jnp.int32, (slot_count, n_expert * ROOM), 0)
    spot = lax.broadcasted_iota(jnp.int32, (slot_count, n_expert * ROOM), 1)
    block = jnp.zeros_like(slot)
    for b in range(1, n_expert):
        block += (slot >= b * MOST).astype(jnp.int32)
    back = me - block
    back = jnp.where(back < 0, back + n_expert, back)
    target = back * ROOM + slot - block * MOST
    for e in range(owned):
        turned_ref[e] = lax.dot_general(
            act_ref[e],
            (spot == target + e).astype(jnp.bfloat16),
            (((0,), (0,)), ((), ())),
            preferred_element_type=jnp.float32,
        ).astype(jnp.bfloat16)


def place_kernel(owned, *refs):
    *notes, place_ref = refs
    first = lax.axis_index("expert") * owned
    rows = place_ref.shape[1]
    experts = (first + lax.broadcasted_iota(jnp.int32, (owned, TOK), 0)).astype(jnp.float32)
    earlier = (
        lax.broadcasted_iota(jnp.int32, (TOK, TOK), 0)
        < lax.broadcasted_iota(jnp.int32, (TOK, TOK), 1)
    ).astype(jnp.float32)
    row = lax.broadcasted_iota(jnp.int32, (rows, owned), 0)
    start = lax.broadcasted_iota(jnp.int32, (rows, owned), 1) * MOST
    spread = ((row >= start) & (row < start + MOST)).astype(jnp.float32)
    wanted = lax.broadcasted_iota(jnp.int32, (rows, TOK), 0)
    for e in range(1, owned):
        wanted -= MOST * (
            lax.broadcasted_iota(jnp.int32, (rows, TOK), 0) >= e * MOST
        ).astype(jnp.int32)
    wanted = wanted.astype(jnp.float32)
    for k, note in enumerate(notes):
        meta = note[...].astype(jnp.float32)
        named = jnp.zeros((owned, TOK), jnp.float32)
        gate = jnp.zeros((owned, TOK), jnp.float32)
        for c in range(TOPK):
            hit = experts == meta[c : c + 1, :]
            named = jnp.where(hit, 1.0, named)
            gate = jnp.where(hit, meta[TOPK + c : TOPK + c + 1, :], gate)
        rank = jnp.dot(named, earlier, preferred_element_type=jnp.float32)
        rank = jnp.where(named > 0.0, rank, -1.0)
        rank = jnp.dot(spread, rank, preferred_element_type=jnp.float32)
        gate = jnp.dot(spread, gate, preferred_element_type=jnp.float32)
        place_ref[k] = jnp.where(rank == wanted, gate, 0.0).astype(jnp.bfloat16)


def early_kernel(ks, place_ref, *refs):
    blocks, outs = refs[: len(ks)], refs[len(ks) :]
    weigh_tiles([place_ref.at[k] for k in ks], blocks, outs)


def weigh_tiles(places, blocks, outs):
    half = blocks[0].shape[1] // 2

    @pl.loop(0, 2)
    def _(t):
        wide = pl.ds(pl.multiple_of(t * half, half), half)
        for place, block, out in zip(places, blocks, outs):
            out[:, wide] = jnp.dot(
                place[...], block[:, wide], preferred_element_type=jnp.float32
            ).astype(jnp.bfloat16)


def grad_kernel(n_expert, other, early, place_ref, act_ref, *refs):
    blocks = refs[:n_expert]
    out_ref, weighted_ref, done_ref, out_sem = refs[-4:]
    owned, hid, _ = act_ref.shape
    features = done_ref.shape[2]
    side = lax.rem(lax.axis_index("tensor") + other, lax.axis_size("tensor"))
    column = pl.multiple_of(side * features, 128)

    def leave(e):
        slot = lax.rem(e, BUFFERS)
        return pltpu.make_async_copy(
            done_ref.at[slot], out_ref.at[e, :, pl.ds(column, features)], out_sem.at[slot]
        )

    late = [k for k in range(n_expert) if k not in early]
    weighted = list(blocks)
    for i, k in enumerate(late):
        weighted[k] = weighted_ref.at[i]
    weigh_tiles([place_ref.at[k] for k in late], [blocks[k] for k in late], [weighted[k] for k in late])

    @pl.loop(0, owned)
    def _(e):
        @pl.when(e >= BUFFERS)
        def _():
            leave(e - BUFFERS).wait()

        window = pl.ds(pl.multiple_of(e * 16, 16), ROOM)
        for n in range(0, features, 256):
            wide = slice(n, min(n + 256, features))
            right = jnp.concatenate([rows[window, wide] for rows in weighted], axis=0)
            done_ref[lax.rem(e, BUFFERS), :, wide] = jnp.dot(
                act_ref[e], right, preferred_element_type=jnp.float32
            ).astype(jnp.bfloat16)
        leave(e).start()

    @pl.loop(owned - BUFFERS, owned)
    def _(e):
        leave(e).wait()


def local_by_tokens(sent_grad, head_grad, probs, expert_ids, hidden_act):
    n_expert = lax.axis_size("expert")
    n_tensor = lax.axis_size("tensor")
    owned, _, hid = hidden_act.shape[1:]
    feat_dev = sent_grad.shape[2]
    vmem = pl.BlockSpec(memory_space=pltpu.VMEM)
    anywhere = pl.BlockSpec(memory_space=pl.ANY)

    def small_call(kernel, shapes, operands, name):
        return pl.pallas_call(
            kernel,
            out_shape=[jax.ShapeDtypeStruct(shape, jnp.bfloat16) for shape in shapes],
            in_specs=[vmem] * len(operands),
            out_specs=[vmem] * len(shapes),
            compiler_params=pltpu.CompilerParams(vmem_limit_bytes=16 * 2**20),
            name=name,
        )(*operands)

    def turned(array, pipe=0, expert=0, tensor=0):
        axes = ("pipe", "expert", "tensor")
        sizes = [lax.axis_size(axis) for axis in axes]
        steps = (pipe, expert, tensor)

        def rank(place):
            return (place[0] * sizes[1] + place[1]) * sizes[2] + place[2]

        pairs = []
        for place in itertools.product(*map(range, sizes)):
            target = [(i + by) % size for i, by, size in zip(place, steps, sizes)]
            pairs.append((rank(place), rank(target)))
        return lax.ppermute(array, axes, pairs)

    def grad_into(out, blocks, other, early):
        operands = [place, act, *blocks]
        in_specs = [vmem] * len(operands)
        aliases = {}
        if out is not None:
            aliases = {len(operands): 0}
            in_specs.append(anywhere)
            operands.append(out)
        return pl.pallas_call(
            functools.partial(grad_kernel, n_expert, other, early),
            out_shape=jax.ShapeDtypeStruct((owned, hid, n_tensor * feat_dev), jnp.bfloat16),
            in_specs=in_specs,
            out_specs=anywhere,
            scratch_shapes=[
                pltpu.VMEM((n_expert - len(early), place.shape[1], feat_dev), jnp.bfloat16),
                pltpu.VMEM((BUFFERS, hid, feat_dev), jnp.bfloat16),
                pltpu.SemaphoreType.DMA((BUFFERS,)),
            ],
            input_output_aliases=aliases,
            compiler_params=pltpu.CompilerParams(vmem_limit_bytes=28 * 2**20),
            cost_estimate=pl.CostEstimate(
                flops=2 * owned * hid * 256 * feat_dev,
                bytes_accessed=2 * owned * hid * feat_dev,
                transcendentals=0,
            ),
            name="weight_grad",
        )(*operands)

    payload = jnp.where(lax.axis_index("pipe") == 0, head_grad, sent_grad[0])
    blocks = {1: turned(payload, -1, 1)}
    beside = {0: {t: turned(payload, -1, 0, t) for t in range(1, n_tensor)}}
    (notes,) = small_call(
        notes_kernel, [(2 * TOPK, TOK)], [expert_ids[0].T, probs[0].T], "notes"
    )
    notes = [notes] + [turned(notes, 0, k) for k in range(1, n_expert)]
    (act,) = small_call(
        functools.partial(turn_kernel, n_expert),
        [(owned, hid, n_expert * ROOM)],
        [hidden_act[0]],
        "turn",
    )
    beside[0], payload, act, notes[1:] = lax.optimization_barrier(
        (beside[0], payload, act, notes[1:])
    )
    blocks[n_expert - 1] = turned(payload, -1, -1)
    for k in range(2, n_expert - 1):
        blocks[k] = turned(blocks[k - 1], 0, 1)
    (place,) = small_call(
        functools.partial(place_kernel, owned), [(n_expert, 16 * (owned + 1), TOK)], notes, "place"
    )
    blocks[0] = turned(payload, -1)

    def weighed(sources, ks):
        done = small_call(
            functools.partial(early_kernel, ks),
            [(place.shape[1], feat_dev)] * len(ks),
            [place, *(sources[k] for k in ks)],
            "early",
        )
        return dict(zip(ks, done))

    last = n_expert - 1
    early = tuple(range(1, last))
    own = weighed(blocks, early)
    for k in range(1, n_expert):
        if k == last - 1:
            blocks[k], own, beside[k - 1] = lax.optimization_barrier((blocks[k], own, beside[k - 1]))
        beside[k] = {t: turned(blocks[k], 0, 0, t) for t in range(1, n_tensor)}
    out = grad_into(None, [own.get(k, blocks[k]) for k in range(n_expert)], 0, early)
    for t in range(1, n_tensor):
        out = grad_into(out, [beside[k][t] for k in range(n_expert)], n_tensor - t, ())
    return out[None]


def local(*arrays):
    owned, slot_count = arrays[4].shape[1:3]
    tokens = lax.axis_size("expert") * TOK
    by_tokens = owned <= 16 and tokens <= owned * slot_count
    return (local_by_tokens if by_tokens else local_by_slots)(*arrays)


def solution(mesh):
    in_specs = (
        P("pipe", "expert", "tensor"),
        P("expert", "tensor"),
        P("pipe", "expert", None),
        P("pipe", "expert", None),
        P("pipe", "expert", None, "tensor"),
    )
    out_specs = P("pipe", "expert", "tensor", None)
    return jax.shard_map(local, mesh=mesh, in_specs=in_specs, out_specs=out_specs, check_vma=False)
```

```python
import functools
import itertools

import jax
import jax.numpy as jnp
from jax import lax
from jax.experimental import pallas as pl
from jax.experimental.pallas import tpu as pltpu
from jax.sharding import PartitionSpec as P

EXPERTS = 64
TOPK = 8
TOK = 128
MOST = 17
ROOM = 32
BUFFERS = 4


def passed_along(array, axis, by):
    peers = lax.axis_size(axis)
    pairs = [(i, i + by) for i in range(peers) if 0 <= i + by < peers]
    return lax.ppermute(array, axis, pairs)


def slot_ranks(pair_ids):
    onehot = (pair_ids[:, :, None] == jnp.arange(EXPERTS, dtype=jnp.int32)[None, None, :]).astype(
        jnp.int32
    )
    before = jnp.cumsum(onehot, axis=1) - onehot
    return jnp.sum(before * onehot, axis=2)


def place_rows(targets, capacity, source_rows, gate_values):
    pair_count = targets.shape[0]
    owner_pair = (
        jnp.full((capacity,), pair_count, jnp.int32)
        .at[targets]
        .set(jnp.arange(pair_count, dtype=jnp.int32), mode="drop")
    )
    filled = owner_pair < pair_count
    safe_pair = jnp.minimum(owner_pair, pair_count - 1)
    placed = jnp.where(
        filled[:, None], source_rows[safe_pair // TOPK], jnp.zeros((), source_rows.dtype)
    )
    placed_gate = jnp.where(
        filled, gate_values.reshape(-1)[safe_pair], jnp.zeros((), gate_values.dtype)
    )
    return (placed, placed_gate)


def arriving(sent_grad, head_grad):
    shifted = passed_along(sent_grad, "pipe", -1)
    is_last = lax.axis_index("pipe") == lax.axis_size("pipe") - 1
    return jnp.where(is_last, head_grad, shifted[0])


def local_by_slots(sent_grad, head_grad, probs, expert_ids, hidden_act):
    incoming = arriving(sent_grad, head_grad)
    feat_dev = incoming.shape[1]
    local_ids = expert_ids[0].reshape(1, TOK * TOPK)
    local_targets = (local_ids * MOST + slot_ranks(local_ids)).reshape(-1)
    send_rows, send_gate = place_rows(local_targets, EXPERTS * MOST, incoming, probs[0])
    recv_rows, recv_gate = (
        lax.all_to_all(
            send_rows.reshape(EXPERTS, MOST, feat_dev),
            "expert",
            split_axis=0,
            concat_axis=1,
            tiled=True,
        ),
        lax.all_to_all(
            send_gate.reshape(EXPERTS, MOST), "expert", split_axis=0, concat_axis=1, tiled=True
        ),
    )
    gate_wide = recv_gate.astype(jnp.float32)[:, :, None]
    full_rows = lax.all_gather(recv_rows, "tensor", axis=2, tiled=True)
    weighted = (full_rows.astype(jnp.float32) * gate_wide).astype(jnp.bfloat16)
    weight_grad = jnp.einsum(
        "esh,esd->ehd", hidden_act[0], weighted, preferred_element_type=jnp.float32
    ).astype(jnp.bfloat16)
    return weight_grad[None]


def notes_kernel(ids_ref, probs_ref, notes_ref):
    notes_ref[...] = jnp.concatenate(
        [ids_ref[...].astype(jnp.float32), probs_ref[...].astype(jnp.float32)], axis=0
    ).astype(jnp.bfloat16)


def turn_kernel(n_expert, act_ref, turned_ref):
    owned, slot_count, _ = act_ref.shape
    me = lax.axis_index("expert")
    slot = lax.broadcasted_iota(jnp.int32, (slot_count, n_expert * ROOM), 0)
    spot = lax.broadcasted_iota(jnp.int32, (slot_count, n_expert * ROOM), 1)
    block = jnp.zeros_like(slot)
    for b in range(1, n_expert):
        block += (slot >= b * MOST).astype(jnp.int32)
    back = me - block
    back = jnp.where(back < 0, back + n_expert, back)
    target = back * ROOM + slot - block * MOST
    for e in range(owned):
        turned_ref[e] = lax.dot_general(
            act_ref[e],
            (spot == target + e).astype(jnp.bfloat16),
            (((0,), (0,)), ((), ())),
            preferred_element_type=jnp.float32,
        ).astype(jnp.bfloat16)


def place_kernel(owned, *refs):
    *notes, place_ref = refs
    first = lax.axis_index("expert") * owned
    rows = place_ref.shape[1]
    experts = (first + lax.broadcasted_iota(jnp.int32, (owned, TOK), 0)).astype(jnp.float32)
    earlier = (
        lax.broadcasted_iota(jnp.int32, (TOK, TOK), 0)
        < lax.broadcasted_iota(jnp.int32, (TOK, TOK), 1)
    ).astype(jnp.float32)
    row = lax.broadcasted_iota(jnp.int32, (rows, owned), 0)
    start = lax.broadcasted_iota(jnp.int32, (rows, owned), 1) * MOST
    spread = ((row >= start) & (row < start + MOST)).astype(jnp.float32)
    wanted = lax.broadcasted_iota(jnp.int32, (rows, TOK), 0)
    for e in range(1, owned):
        wanted -= MOST * (
            lax.broadcasted_iota(jnp.int32, (rows, TOK), 0) >= e * MOST
        ).astype(jnp.int32)
    wanted = wanted.astype(jnp.float32)
    for k, note in enumerate(notes):
        meta = note[...].astype(jnp.float32)
        named = jnp.zeros((owned, TOK), jnp.float32)
        gate = jnp.zeros((owned, TOK), jnp.float32)
        for c in range(TOPK):
            hit = experts == meta[c : c + 1, :]
            named = jnp.where(hit, 1.0, named)
            gate = jnp.where(hit, meta[TOPK + c : TOPK + c + 1, :], gate)
        rank = jnp.dot(named, earlier, preferred_element_type=jnp.float32)
        rank = jnp.where(named > 0.0, rank, -1.0)
        rank = jnp.dot(spread, rank, preferred_element_type=jnp.float32)
        gate = jnp.dot(spread, gate, preferred_element_type=jnp.float32)
        place_ref[k] = jnp.where(rank == wanted, gate, 0.0).astype(jnp.bfloat16)


def early_kernel(ks, place_ref, *refs):
    blocks, outs = refs[: len(ks)], refs[len(ks) :]
    weigh_tiles([place_ref.at[k] for k in ks], blocks, outs)


def weigh_tiles(places, blocks, outs):
    half = blocks[0].shape[1] // 2

    @pl.loop(0, 2)
    def _(t):
        wide = pl.ds(pl.multiple_of(t * half, half), half)
        for place, block, out in zip(places, blocks, outs):
            out[:, wide] = jnp.dot(
                place[...], block[:, wide], preferred_element_type=jnp.float32
            ).astype(jnp.bfloat16)


def grad_kernel(n_expert, other, early, place_ref, act_ref, *refs):
    blocks = refs[:n_expert]
    out_ref, weighted_ref, done_ref, out_sem = refs[-4:]
    owned, hid, _ = act_ref.shape
    features = done_ref.shape[2]
    side = lax.rem(lax.axis_index("tensor") + other, lax.axis_size("tensor"))
    column = pl.multiple_of(side * features, 128)

    def leave(e):
        slot = lax.rem(e, BUFFERS)
        return pltpu.make_async_copy(
            done_ref.at[slot], out_ref.at[e, :, pl.ds(column, features)], out_sem.at[slot]
        )

    late = [k for k in range(n_expert) if k not in early]
    weighted = list(blocks)
    for i, k in enumerate(late):
        weighted[k] = weighted_ref.at[i]
    weigh_tiles([place_ref.at[k] for k in late], [blocks[k] for k in late], [weighted[k] for k in late])

    @pl.loop(0, owned)
    def _(e):
        @pl.when(e >= BUFFERS)
        def _():
            leave(e - BUFFERS).wait()

        window = pl.ds(pl.multiple_of(e * 16, 16), ROOM)
        for n in range(0, features, 256):
            wide = slice(n, min(n + 256, features))
            right = jnp.concatenate([rows[window, wide] for rows in weighted], axis=0)
            done_ref[lax.rem(e, BUFFERS), :, wide] = jnp.dot(
                act_ref[e], right, preferred_element_type=jnp.float32
            ).astype(jnp.bfloat16)
        leave(e).start()

    @pl.loop(owned - BUFFERS, owned)
    def _(e):
        leave(e).wait()


def local_by_tokens(sent_grad, head_grad, probs, expert_ids, hidden_act):
    n_expert = lax.axis_size("expert")
    n_tensor = lax.axis_size("tensor")
    owned, _, hid = hidden_act.shape[1:]
    feat_dev = sent_grad.shape[2]
    vmem = pl.BlockSpec(memory_space=pltpu.VMEM)
    anywhere = pl.BlockSpec(memory_space=pl.ANY)

    def small_call(kernel, shapes, operands, name):
        return pl.pallas_call(
            kernel,
            out_shape=[jax.ShapeDtypeStruct(shape, jnp.bfloat16) for shape in shapes],
            in_specs=[vmem] * len(operands),
            out_specs=[vmem] * len(shapes),
            compiler_params=pltpu.CompilerParams(vmem_limit_bytes=16 * 2**20),
            name=name,
        )(*operands)

    def turned(array, pipe=0, expert=0, tensor=0):
        axes = ("pipe", "expert", "tensor")
        sizes = [lax.axis_size(axis) for axis in axes]
        steps = (pipe, expert, tensor)

        def rank(place):
            return (place[0] * sizes[1] + place[1]) * sizes[2] + place[2]

        pairs = []
        for place in itertools.product(*map(range, sizes)):
            target = [(i + by) % size for i, by, size in zip(place, steps, sizes)]
            pairs.append((rank(place), rank(target)))
        return lax.ppermute(array, axes, pairs)

    def grad_into(out, blocks, other, early):
        operands = [place, act, *blocks]
        in_specs = [vmem] * len(operands)
        aliases = {}
        if out is not None:
            aliases = {len(operands): 0}
            in_specs.append(anywhere)
            operands.append(out)
        return pl.pallas_call(
            functools.partial(grad_kernel, n_expert, other, early),
            out_shape=jax.ShapeDtypeStruct((owned, hid, n_tensor * feat_dev), jnp.bfloat16),
            in_specs=in_specs,
            out_specs=anywhere,
            scratch_shapes=[
                pltpu.VMEM((n_expert - len(early), place.shape[1], feat_dev), jnp.bfloat16),
                pltpu.VMEM((BUFFERS, hid, feat_dev), jnp.bfloat16),
                pltpu.SemaphoreType.DMA((BUFFERS,)),
            ],
            input_output_aliases=aliases,
            compiler_params=pltpu.CompilerParams(vmem_limit_bytes=28 * 2**20),
            cost_estimate=pl.CostEstimate(
                flops=2 * owned * hid * 256 * feat_dev,
                bytes_accessed=2 * owned * hid * feat_dev,
                transcendentals=0,
            ),
            name="weight_grad",
        )(*operands)

    payload = jnp.where(lax.axis_index("pipe") == 0, head_grad, sent_grad[0])
    blocks = {1: turned(payload, -1, 1)}
    beside = {0: {t: turned(payload, -1, 0, t) for t in range(1, n_tensor)}}
    (notes,) = small_call(
        notes_kernel, [(2 * TOPK, TOK)], [expert_ids[0].T, probs[0].T], "notes"
    )
    notes = [notes] + [turned(notes, 0, k) for k in range(1, n_expert)]
    (act,) = small_call(
        functools.partial(turn_kernel, n_expert),
        [(owned, hid, n_expert * ROOM)],
        [hidden_act[0]],
        "turn",
    )
    beside[0], payload, act, notes[1:] = lax.optimization_barrier(
        (beside[0], payload, act, notes[1:])
    )
    blocks[n_expert - 1] = turned(payload, -1, -1)
    for k in range(2, n_expert - 1):
        blocks[k] = turned(blocks[k - 1], 0, 1)
    (place,) = small_call(
        functools.partial(place_kernel, owned), [(n_expert, 16 * (owned + 1), TOK)], notes, "place"
    )
    blocks[0] = turned(payload, -1)

    def weighed(sources, ks):
        done = small_call(
            functools.partial(early_kernel, ks),
            [(place.shape[1], feat_dev)] * len(ks),
            [place, *(sources[k] for k in ks)],
            "early",
        )
        return dict(zip(ks, done))

    last = n_expert - 1
    early = tuple(range(1, last))
    own = weighed(blocks, early)
    others = {t: weighed({0: beside[0][t]}, (0,)) for t in range(1, n_tensor)}
    for k in range(1, n_expert):
        if k == last - 1:
            blocks[k], own, others, beside[k - 1] = lax.optimization_barrier(
                (blocks[k], own, others, beside[k - 1])
            )
        beside[k] = {t: turned(blocks[k], 0, 0, t) for t in range(1, n_tensor)}
    out = grad_into(None, [own.get(k, blocks[k]) for k in range(n_expert)], 0, early)
    for t in range(1, n_tensor):
        sources = [others[t].get(k, beside[k][t]) for k in range(n_expert)]
        out = grad_into(out, sources, n_tensor - t, (0,))
    return out[None]


def local(*arrays):
    owned, slot_count = arrays[4].shape[1:3]
    tokens = lax.axis_size("expert") * TOK
    by_tokens = owned <= 16 and tokens <= owned * slot_count
    return (local_by_tokens if by_tokens else local_by_slots)(*arrays)


def solution(mesh):
    in_specs = (
        P("pipe", "expert", "tensor"),
        P("expert", "tensor"),
        P("pipe", "expert", None),
        P("pipe", "expert", None),
        P("pipe", "expert", None, "tensor"),
    )
    out_specs = P("pipe", "expert", "tensor", None)
    return jax.shard_map(local, mesh=mesh, in_specs=in_specs, out_specs=out_specs, check_vma=False)
```

```python
import functools
import itertools

import jax
import jax.numpy as jnp
from jax import lax
from jax.experimental import pallas as pl
from jax.experimental.pallas import tpu as pltpu
from jax.sharding import PartitionSpec as P

EXPERTS = 64
TOPK = 8
TOK = 128
MOST = 17
ROOM = 32
BUFFERS = 4


def passed_along(array, axis, by):
    peers = lax.axis_size(axis)
    pairs = [(i, i + by) for i in range(peers) if 0 <= i + by < peers]
    return lax.ppermute(array, axis, pairs)


def slot_ranks(pair_ids):
    onehot = (pair_ids[:, :, None] == jnp.arange(EXPERTS, dtype=jnp.int32)[None, None, :]).astype(
        jnp.int32
    )
    before = jnp.cumsum(onehot, axis=1) - onehot
    return jnp.sum(before * onehot, axis=2)


def place_rows(targets, capacity, source_rows, gate_values):
    pair_count = targets.shape[0]
    owner_pair = (
        jnp.full((capacity,), pair_count, jnp.int32)
        .at[targets]
        .set(jnp.arange(pair_count, dtype=jnp.int32), mode="drop")
    )
    filled = owner_pair < pair_count
    safe_pair = jnp.minimum(owner_pair, pair_count - 1)
    placed = jnp.where(
        filled[:, None], source_rows[safe_pair // TOPK], jnp.zeros((), source_rows.dtype)
    )
    placed_gate = jnp.where(
        filled, gate_values.reshape(-1)[safe_pair], jnp.zeros((), gate_values.dtype)
    )
    return (placed, placed_gate)


def arriving(sent_grad, head_grad):
    shifted = passed_along(sent_grad, "pipe", -1)
    is_last = lax.axis_index("pipe") == lax.axis_size("pipe") - 1
    return jnp.where(is_last, head_grad, shifted[0])


def local_by_slots(sent_grad, head_grad, probs, expert_ids, hidden_act):
    incoming = arriving(sent_grad, head_grad)
    feat_dev = incoming.shape[1]
    local_ids = expert_ids[0].reshape(1, TOK * TOPK)
    local_targets = (local_ids * MOST + slot_ranks(local_ids)).reshape(-1)
    send_rows, send_gate = place_rows(local_targets, EXPERTS * MOST, incoming, probs[0])
    recv_rows, recv_gate = (
        lax.all_to_all(
            send_rows.reshape(EXPERTS, MOST, feat_dev),
            "expert",
            split_axis=0,
            concat_axis=1,
            tiled=True,
        ),
        lax.all_to_all(
            send_gate.reshape(EXPERTS, MOST), "expert", split_axis=0, concat_axis=1, tiled=True
        ),
    )
    gate_wide = recv_gate.astype(jnp.float32)[:, :, None]
    full_rows = lax.all_gather(recv_rows, "tensor", axis=2, tiled=True)
    weighted = (full_rows.astype(jnp.float32) * gate_wide).astype(jnp.bfloat16)
    weight_grad = jnp.einsum(
        "esh,esd->ehd", hidden_act[0], weighted, preferred_element_type=jnp.float32
    ).astype(jnp.bfloat16)
    return weight_grad[None]


def notes_kernel(ids_ref, probs_ref, notes_ref):
    notes_ref[...] = jnp.concatenate(
        [ids_ref[...].astype(jnp.float32), probs_ref[...].astype(jnp.float32)], axis=0
    ).astype(jnp.bfloat16)


def turn_kernel(n_expert, act_ref, turned_ref):
    owned, slot_count, _ = act_ref.shape
    me = lax.axis_index("expert")
    slot = lax.broadcasted_iota(jnp.int32, (slot_count, n_expert * ROOM), 0)
    spot = lax.broadcasted_iota(jnp.int32, (slot_count, n_expert * ROOM), 1)
    block = jnp.zeros_like(slot)
    for b in range(1, n_expert):
        block += (slot >= b * MOST).astype(jnp.int32)
    back = me - block
    back = jnp.where(back < 0, back + n_expert, back)
    target = back * ROOM + slot - block * MOST
    for e in range(owned):
        turned_ref[e] = lax.dot_general(
            act_ref[e],
            (spot == target + e).astype(jnp.bfloat16),
            (((0,), (0,)), ((), ())),
            preferred_element_type=jnp.float32,
        ).astype(jnp.bfloat16)


def place_kernel(owned, *refs):
    *notes, place_ref = refs
    first = lax.axis_index("expert") * owned
    rows = place_ref.shape[1]
    experts = (first + lax.broadcasted_iota(jnp.int32, (owned, TOK), 0)).astype(jnp.float32)
    earlier = (
        lax.broadcasted_iota(jnp.int32, (TOK, TOK), 0)
        < lax.broadcasted_iota(jnp.int32, (TOK, TOK), 1)
    ).astype(jnp.float32)
    row = lax.broadcasted_iota(jnp.int32, (rows, owned), 0)
    start = lax.broadcasted_iota(jnp.int32, (rows, owned), 1) * MOST
    spread = ((row >= start) & (row < start + MOST)).astype(jnp.float32)
    wanted = lax.broadcasted_iota(jnp.int32, (rows, TOK), 0)
    for e in range(1, owned):
        wanted -= MOST * (
            lax.broadcasted_iota(jnp.int32, (rows, TOK), 0) >= e * MOST
        ).astype(jnp.int32)
    wanted = wanted.astype(jnp.float32)
    for k, note in enumerate(notes):
        meta = note[...].astype(jnp.float32)
        named = jnp.zeros((owned, TOK), jnp.float32)
        gate = jnp.zeros((owned, TOK), jnp.float32)
        for c in range(TOPK):
            hit = experts == meta[c : c + 1, :]
            named = jnp.where(hit, 1.0, named)
            gate = jnp.where(hit, meta[TOPK + c : TOPK + c + 1, :], gate)
        rank = jnp.dot(named, earlier, preferred_element_type=jnp.float32)
        rank = jnp.where(named > 0.0, rank, -1.0)
        rank = jnp.dot(spread, rank, preferred_element_type=jnp.float32)
        gate = jnp.dot(spread, gate, preferred_element_type=jnp.float32)
        place_ref[k] = jnp.where(rank == wanted, gate, 0.0).astype(jnp.bfloat16)


def early_kernel(ks, place_ref, *refs):
    blocks, outs = refs[: len(ks)], refs[len(ks) :]
    weigh_tiles([place_ref.at[k] for k in ks], blocks, outs)


def weigh_tiles(places, blocks, outs):
    half = blocks[0].shape[1] // 2

    @pl.loop(0, 2)
    def _(t):
        wide = pl.ds(pl.multiple_of(t * half, half), half)
        for place, block, out in zip(places, blocks, outs):
            out[:, wide] = jnp.dot(
                place[...], block[:, wide], preferred_element_type=jnp.float32
            ).astype(jnp.bfloat16)


def grad_kernel(n_expert, other, early, place_ref, act_ref, *refs):
    blocks = refs[:n_expert]
    out_ref, weighted_ref, done_ref, out_sem = refs[-4:]
    owned, hid, _ = act_ref.shape
    features = done_ref.shape[2]
    side = lax.rem(lax.axis_index("tensor") + other, lax.axis_size("tensor"))
    column = pl.multiple_of(side * features, 128)

    def leave(e):
        slot = lax.rem(e, BUFFERS)
        return pltpu.make_async_copy(
            done_ref.at[slot], out_ref.at[e, :, pl.ds(column, features)], out_sem.at[slot]
        )

    late = [k for k in range(n_expert) if k not in early]
    weighted = list(blocks)
    for i, k in enumerate(late):
        weighted[k] = weighted_ref.at[i]
    weigh_tiles([place_ref.at[k] for k in late], [blocks[k] for k in late], [weighted[k] for k in late])

    @pl.loop(0, owned)
    def _(e):
        @pl.when(e >= BUFFERS)
        def _():
            leave(e - BUFFERS).wait()

        window = pl.ds(pl.multiple_of(e * 16, 16), ROOM)
        for n in range(0, features, 256):
            wide = slice(n, min(n + 256, features))
            right = jnp.concatenate([rows[window, wide] for rows in weighted], axis=0)
            done_ref[lax.rem(e, BUFFERS), :, wide] = jnp.dot(
                act_ref[e], right, preferred_element_type=jnp.float32
            ).astype(jnp.bfloat16)
        leave(e).start()

    @pl.loop(owned - BUFFERS, owned)
    def _(e):
        leave(e).wait()


def local_by_tokens(sent_grad, head_grad, probs, expert_ids, hidden_act):
    n_expert = lax.axis_size("expert")
    n_tensor = lax.axis_size("tensor")
    owned, _, hid = hidden_act.shape[1:]
    feat_dev = sent_grad.shape[2]
    vmem = pl.BlockSpec(memory_space=pltpu.VMEM)
    anywhere = pl.BlockSpec(memory_space=pl.ANY)

    def small_call(kernel, shapes, operands, name):
        return pl.pallas_call(
            kernel,
            out_shape=[jax.ShapeDtypeStruct(shape, jnp.bfloat16) for shape in shapes],
            in_specs=[vmem] * len(operands),
            out_specs=[vmem] * len(shapes),
            compiler_params=pltpu.CompilerParams(vmem_limit_bytes=16 * 2**20),
            name=name,
        )(*operands)

    def turned(array, pipe=0, expert=0, tensor=0):
        axes = ("pipe", "expert", "tensor")
        sizes = [lax.axis_size(axis) for axis in axes]
        steps = (pipe, expert, tensor)

        def rank(place):
            return (place[0] * sizes[1] + place[1]) * sizes[2] + place[2]

        pairs = []
        for place in itertools.product(*map(range, sizes)):
            target = [(i + by) % size for i, by, size in zip(place, steps, sizes)]
            pairs.append((rank(place), rank(target)))
        return lax.ppermute(array, axes, pairs)

    def grad_into(out, blocks, other, early):
        operands = [place, act, *blocks]
        in_specs = [vmem] * len(operands)
        aliases = {}
        if out is not None:
            aliases = {len(operands): 0}
            in_specs.append(anywhere)
            operands.append(out)
        return pl.pallas_call(
            functools.partial(grad_kernel, n_expert, other, early),
            out_shape=jax.ShapeDtypeStruct((owned, hid, n_tensor * feat_dev), jnp.bfloat16),
            in_specs=in_specs,
            out_specs=anywhere,
            scratch_shapes=[
                pltpu.VMEM((n_expert - len(early), place.shape[1], feat_dev), jnp.bfloat16),
                pltpu.VMEM((BUFFERS, hid, feat_dev), jnp.bfloat16),
                pltpu.SemaphoreType.DMA((BUFFERS,)),
            ],
            input_output_aliases=aliases,
            compiler_params=pltpu.CompilerParams(vmem_limit_bytes=28 * 2**20),
            cost_estimate=pl.CostEstimate(
                flops=2 * owned * hid * 256 * feat_dev,
                bytes_accessed=2 * owned * hid * feat_dev,
                transcendentals=0,
            ),
            name="weight_grad",
        )(*operands)

    payload = jnp.where(lax.axis_index("pipe") == 0, head_grad, sent_grad[0])
    blocks = {1: turned(payload, -1, 1)}
    beside = {0: {t: turned(payload, -1, 0, t) for t in range(1, n_tensor)}}
    (notes,) = small_call(
        notes_kernel, [(2 * TOPK, TOK)], [expert_ids[0].T, probs[0].T], "notes"
    )
    notes = [notes] + [turned(notes, 0, k) for k in range(1, n_expert)]
    (act,) = small_call(
        functools.partial(turn_kernel, n_expert),
        [(owned, hid, n_expert * ROOM)],
        [hidden_act[0]],
        "turn",
    )
    beside[0], payload, act, notes[1:] = lax.optimization_barrier(
        (beside[0], payload, act, notes[1:])
    )
    blocks[n_expert - 1] = turned(payload, -1, -1)
    for k in range(2, n_expert - 1):
        blocks[k] = turned(blocks[k - 1], 0, 1)
    (place,) = small_call(
        functools.partial(place_kernel, owned), [(n_expert, 16 * (owned + 1), TOK)], notes, "place"
    )
    blocks[0] = turned(payload, -1)

    def weighed(sources, ks):
        done = small_call(
            functools.partial(early_kernel, ks),
            [(place.shape[1], feat_dev)] * len(ks),
            [place, *(sources[k] for k in ks)],
            "early",
        )
        return dict(zip(ks, done))

    last = n_expert - 1
    early = tuple(range(1, last))
    own = weighed(blocks, early)
    others = {t: weighed({0: beside[0][t]}, (0,)) for t in range(1, n_tensor)}
    for k in range(1, n_expert):
        if k == last - 1:
            blocks[k], others = lax.optimization_barrier((blocks[k], others))
        if k == last:
            blocks[k], own, beside[1] = lax.optimization_barrier((blocks[k], own, beside[1]))
        beside[k] = {t: turned(blocks[k], 0, 0, t) for t in range(1, n_tensor)}
    out = grad_into(None, [own.get(k, blocks[k]) for k in range(n_expert)], 0, early)
    for t in range(1, n_tensor):
        sources = [others[t].get(k, beside[k][t]) for k in range(n_expert)]
        out = grad_into(out, sources, n_tensor - t, (0,))
    return out[None]


def local(*arrays):
    owned, slot_count = arrays[4].shape[1:3]
    tokens = lax.axis_size("expert") * TOK
    by_tokens = owned <= 16 and tokens <= owned * slot_count
    return (local_by_tokens if by_tokens else local_by_slots)(*arrays)


def solution(mesh):
    in_specs = (
        P("pipe", "expert", "tensor"),
        P("expert", "tensor"),
        P("pipe", "expert", None),
        P("pipe", "expert", None),
        P("pipe", "expert", None, "tensor"),
    )
    out_specs = P("pipe", "expert", "tensor", None)
    return jax.shard_map(local, mesh=mesh, in_specs=in_specs, out_specs=out_specs, check_vma=False)
```
